128 devices in a mesh: face: 4 (over x), tile: 32 (over y, z, core).
Axes of the slice: x: 4, y: 4, z: 4, core: 2. Of those that a mesh axis runs over, the one named last changes fastest.
Arguments:
- atmos_state: float32 [4, 8, 768, 3072], P(None, None, 'tile', 'face'), may hold values from -6 to 6
- courant: float32 [3, 768, 3072], P(None, 'tile', 'face'), may hold values from 0.04 to 0.15
- level_weights: float32 [4, 8], replicated, may hold values from 0.2 to 1
- remap_tiles: bfloat16 [36864, 128, 128], P(('face', 'tile')), may hold values from -0.25 to 0.25
- src_block: int32 [128, 288], P(('face', 'tile')), may hold values from 0 to 143
- owner: int32 [128, 288, 1], P(('face', 'tile')), may hold values from 0 to 127; in each aligned block of 288 rows (0 to 287, 288 to 575, ..., all dimensions but the last counted through in order) at most 5 rows name the same one
- offset: int32 [128, 288], P(('face', 'tile')), may hold values from 0 to 63
- tile_index: int32 [128, 288], P(('face', 'tile')), may hold values from 0 to 287, each once within a row
- ocean_state: float32 [4, 8, 256, 4096], P(None, None, 'face', 'tile'), may hold values from -6 to 6
- mixing: float32 [256, 4096], P('face', 'tile'), may hold values from 0.05 to 0.4
- land_mask: int32 [256, 4096], P('face', 'tile'), may hold values 0 or 1
Outputs:
- air_state: float32 [4, 8, 768, 3072], P(None, None, 'tile', 'face')
- ocean_out: float32 [4, 8, 256, 4096], P(None, None, 'face', 'tile')
- atmos_surface: float32 [4, 768, 3072], P(None, 'tile', 'face')
The draws below stay inside these ranges and needn't reach their ends.
Inputs may be any that keep to these rules, and one draw needn't show every extreme that they name: Among the 288 entries of one device, no owner is named more than 5 times, a bound that some block reaches. `tile_index`: each device's entries use each of its 288 stored tiles exactly once.
All inputs are finite; a program needn't handle non-finite values. No bound on the sum of `land_mask` on one device may be relied on, other than what follows from the above.
Results may differ from the reference program's by a relative error of at most 0.0033.
Values may be sent and summed in bfloat16 or wider, within the bound.
No kernel may reach another device: no remote copies, remote signals or barrier semaphores. Data moves between devices by JAX's collectives and lax.ppermute only.
A program may use at most 64 MiB of HBM per device.

```python
import math
import jax
import jax.numpy as jnp
import numpy as np
from jax import lax

NF = 4
FC = 768
BLK = 128
STEPS = 3
LEV = 8
OLEV = 8
OR = 64
CT = 24
SBLK = 144
ENT = 288
CAP = 5
ROWS = 768
COLS = 3072
OROWS = 256
OCOLS = 4096
N_FACE = 4
N_TILE = 32
DEVICES = 128


def with_ends(array, key, least, largest):
    longest = array.shape.index(max(array.shape))
    spots = []
    for shift in (0, 1):
        where = [jax.random.randint(jax.random.fold_in(key, axis), (), 0, length) for axis, length in enumerate(array.shape)]
        where[longest] = (where[longest] + shift) % array.shape[longest]
        spots.append(tuple(where))
    return array.at[spots[0]].set(least).at[spots[1]].set(largest)


def level_of(rng, extent, pieces, least, largest):
    def one(dim, parts):
        heights = jax.random.uniform(jax.random.fold_in(jax.random.fold_in(rng, 6), dim), (parts,), jnp.float32, least / len(pieces), largest / len(pieces))
        return jnp.repeat(jnp.exp(heights), extent[dim] // parts).reshape((-1,) + (1,) * (len(extent) - dim - 1))

    loudness = one(*pieces[0])
    for cut in pieces[1:]:
        loudness = loudness * one(*cut)
    return loudness


def deal_out(stream_key, own, number, rows, count, top, most, lean):
    ranking = jax.random.permutation(stream_key, count)
    heavy_load, usual = shares(count, rows * top, most, lean, True), shares(count, rows * top, most, lean, False)
    places = jnp.arange(count)

    def named(lengths, rotation):
        used = int((lengths > 0).sum())
        fixed = max(1, used // 4)
        passed = fixed + (places - fixed + rotation * (used - fixed)) % max(1, count - fixed)
        return jnp.zeros((count,), jnp.int32).at[ranking[jnp.where(places < fixed, places, passed)]].set(jnp.asarray(lengths, jnp.int32))

    lengths = jnp.where(number % 4 == 0, named(heavy_load, number // 4), named(usual, number - number // 4 - 1))
    mixed = jax.random.permutation(jax.random.fold_in(own, 3), count)
    giver, sink = mixed[0:count // 2 * 2:2], mixed[1:count // 2 * 2:2]
    margin = jnp.minimum(lengths[giver] - 1, most - lengths[sink]) // 2
    margin = jnp.where((giver == ranking[0]) | (sink == ranking[0]) | (lengths[sink] == 0), 0, jnp.maximum(margin, 0))
    passed = jax.random.randint(jax.random.fold_in(own, 4), (count // 2,), 0, 1 << 20) % (margin + 1)
    lengths = lengths.at[giver].add(-passed).at[sink].add(passed)
    members = jnp.searchsorted(jnp.cumsum(lengths), jnp.arange(rows * top), side="right").astype(jnp.int32)
    listing = members.reshape(top, rows).T
    listing = listing[jax.random.permutation(jax.random.fold_in(own, 1), rows)]
    rotation = jax.random.randint(jax.random.fold_in(own, 2), (rows, 1), 0, top)
    return jnp.take_along_axis(listing, (jnp.arange(top)[None, :] + rotation) % top, axis=1)


def shares(count, total, most, lean, full):
    loads = [(1 << 20) // math.isqrt(grade ** lean) + 1 for grade in range(1, count + 1)]
    largest = most if full else min(most, max(-(-total // count), total * loads[0] // sum(loads)))
    least = 1 if total - largest >= count - 1 else 0
    given, spare = [largest] + [least] * (count - 1), total - largest - least * (count - 1)
    while spare > 0:
        free = [i for i in range(1, count) if given[i] < largest] or [i for i in range(1, count) if given[i] < most]
        mass, left = sum([loads[i] for i in free]), spare
        for i in free:
            addition = min(most - given[i], max(1, left * loads[i] // mass), spare)
            given[i] = given[i] + addition
            spare = spare - addition
    return np.array(given)


def noise(rng, shape, scale, most, split=(), kind=jnp.bfloat16):
    level = level_of(rng, shape, split, -0.22, 0.18) if split else 1.0
    values = jax.random.normal(rng, shape, jnp.float32) * scale * level
    return jnp.minimum(jnp.maximum(values, -most), most).astype(kind)


def setup_inputs(seed: int = 0) -> dict:
    keys = jax.random.split(jax.random.key(seed), 12)
    atmos_state = noise(keys[0], (NF, LEV, ROWS, COLS), 1.0, 6.0, ((2, 32), (3, 4)), jnp.float32)
    courant = jnp.clip(0.04 + 0.11000001 * jax.random.uniform(keys[1], (3, ROWS, COLS), jnp.float32) ** level_of(keys[1], (3, ROWS, COLS), ((1, 32), (2, 4)), -0.2, 0.2), 0.04, 0.15)
    level_weights = jnp.clip(jax.random.uniform(keys[2], (NF, LEV), jnp.float32, 0.2, 1.0), 0.2, 1.0)
    remap_tiles = noise(keys[3], (DEVICES * ENT, BLK, BLK), (4 * BLK) ** -0.5, 0.25, ((0, 128),))
    src_block = with_ends(jax.random.randint(keys[4], (DEVICES, ENT), 0, SBLK), jax.random.fold_in(keys[4], 1), 0, SBLK - 1).astype(jnp.int32)
    owner_keys = jax.random.split(jax.random.fold_in(keys[5], 1), DEVICES * ENT // ENT)
    owner_turns = jax.random.permutation(jax.random.fold_in(keys[5], 3), DEVICES * ENT // ENT)
    owner = jax.vmap(lambda own, number: deal_out(jax.random.fold_in(keys[5], 2), own, number, ENT, DEVICES, 1, CAP, 2))(owner_keys, owner_turns).reshape((DEVICES, ENT, 1))
    offset = with_ends(jax.random.randint(keys[6], (DEVICES, ENT), 0, OR), jax.random.fold_in(keys[6], 1), 0, OR - 1).astype(jnp.int32)
    tile_index = jax.vmap(lambda own: jax.random.permutation(own, ENT))(jax.random.split(keys[7], DEVICES)).reshape((DEVICES, ENT)).astype(jnp.int32)
    ocean_state = noise(keys[8], (NF, OLEV, OROWS, OCOLS), 1.0, 6.0, ((2, 4), (3, 32)), jnp.float32)
    mixing = jnp.clip(0.05 + 0.35 * jax.random.uniform(keys[9], (OROWS, OCOLS), jnp.float32) ** level_of(keys[9], (OROWS, OCOLS), ((0, 4), (1, 32)), -0.2, 0.2), 0.05, 0.4)
    land_mask = with_ends((jax.random.randint(keys[10], (OROWS, OCOLS), 0, 10) < 7).astype(jnp.int32), jax.random.fold_in(keys[10], 1), 0, 1)
    return dict(atmos_state=atmos_state, courant=courant, level_weights=level_weights, remap_tiles=remap_tiles, src_block=src_block, owner=owner, offset=offset, tile_index=tile_index, ocean_state=ocean_state, mixing=mixing, land_mask=land_mask)


def advect(air_state, courant):
    along_x, along_y, spread = courant[0], courant[1], courant[2]
    west_cells = jnp.roll(air_state, 1, axis=3)
    east_cells = jnp.roll(air_state, -1, axis=3)
    padded = jnp.pad(air_state, ((0, 0), (0, 0), (1, 1), (0, 0)))
    south_cells = padded[:, :, :-2]
    north_cells = padded[:, :, 2:]
    return air_state - along_x * (air_state - west_cells) - along_y * (air_state - south_cells) + spread * (east_cells + west_cells + north_cells + south_cells - 4.0 * air_state)


def reference(atmos_state, courant, level_weights, remap_tiles, src_block, owner, offset, tile_index, ocean_state, mixing, land_mask):
    air_state = atmos_state
    for step_index in range(STEPS):
        air_state = advect(air_state, courant)
    air_flux = jnp.einsum("fl,flrc->frc", level_weights, air_state, precision=lax.Precision.HIGHEST).astype(jnp.bfloat16)
    devices = N_FACE * N_TILE
    blocks = air_flux.reshape(NF, N_TILE, CT, N_FACE, FC // BLK, BLK).transpose(3, 1, 2, 4, 0, 5).reshape(devices, SBLK, NF, BLK)
    tile_store = remap_tiles.reshape(devices, ENT, BLK, BLK)
    device_ids = jnp.arange(devices, dtype=jnp.int32)

    def forward(device_index):
        block_rows = blocks[device_index][src_block[device_index]].astype(jnp.float32)
        chosen = tile_store[device_index][tile_index[device_index]].astype(jnp.float32)
        return jnp.einsum("efk,ekm->efm", block_rows, chosen, precision=lax.Precision.HIGHEST)

    contribution = lax.map(forward, device_ids)
    target = owner[:, :, 0] * OR + offset
    summed = jax.ops.segment_sum(contribution.reshape(devices * ENT, NF, BLK), target.reshape(-1), num_segments=devices * OR)
    ocean_flux = summed.reshape(N_FACE, N_TILE, OR, NF, BLK).transpose(3, 0, 2, 1, 4).reshape(NF, OROWS, OCOLS)
    wet_cells = land_mask.astype(jnp.float32)
    forced = ocean_state.at[:, 0].add(wet_cells * ocean_flux)
    level_above = jnp.concatenate([forced[:, :1], forced[:, :-1]], axis=1)
    level_below = jnp.concatenate([forced[:, 1:], forced[:, -1:]], axis=1)
    ocean_out = forced + wet_cells * mixing * (level_above + level_below - 2.0 * forced)
    sea_surface = (wet_cells * ocean_out[:, 0]).astype(jnp.bfloat16)
    surface_blocks = sea_surface.reshape(NF, N_FACE, OR, N_TILE, BLK).transpose(1, 3, 2, 0, 4).reshape(devices * OR, NF, BLK)

    def backward(device_index):
        block_rows = surface_blocks[target[device_index]].astype(jnp.float32)
        chosen = tile_store[device_index][tile_index[device_index]].astype(jnp.float32)
        return jnp.einsum("efm,ekm->efk", block_rows, chosen, precision=lax.Precision.HIGHEST)

    returned = lax.map(backward, device_ids)
    source = device_ids[:, None] * SBLK + src_block
    gathered = jax.ops.segment_sum(returned.reshape(devices * ENT, NF, BLK), source.reshape(-1), num_segments=devices * SBLK)
    atmos_surface = gathered.reshape(N_FACE, N_TILE, CT, FC // BLK, NF, BLK).transpose(4, 1, 2, 0, 3, 5).reshape(NF, ROWS, COLS)
    return air_state, ocean_out, atmos_surface
```

```python
import functools

import jax
import jax.numpy as jnp
from jax import lax
from jax.experimental import pallas as pl
from jax.experimental.pallas import tpu as pltpu
from jax.sharding import PartitionSpec as P

STEPS = 3
FIELDS, LEVELS, ROWS, COLS, BLK = 4, 8, 24, 768, 128
PLANES = 36
ENTRIES, DEVICES, CAP, OCEAN_ROWS = 288, 128, 5, 64
CHUNK = 22
BACK = CAP * FIELDS
GROUP = 36
f32, bf16 = jnp.float32, jnp.bfloat16


def iota(shape, dim):
    return lax.broadcasted_iota(jnp.int32, shape, dim)


def roll(x, shift, axis):
    shift = shift % x.shape[axis]
    return pltpu.roll(x, shift, axis) if shift else x


def params(mib=48):
    return pltpu.CompilerParams(vmem_limit_bytes=mib << 20)


def pack_rows(air_ref, cour_ref, out_ref, at_top):
    sub = iota((8, COLS), 0)
    first = 0 if at_top else 3

    def rows(p):
        if p < 32:
            return air_ref[p // LEVELS, p % LEVELS]
        if p < 35:
            return cour_ref[p - 32]
        return jnp.zeros((8, COLS), f32)

    def pair(p):
        return jnp.where(sub < 4, roll(rows(p), first, 0), roll(rows(p + 1), first + 4, 0))

    for p in range(0, PLANES, 4):
        out_ref[p * 4 : p * 4 + 16, :] = jnp.concatenate([pair(p), pair(p + 2)], 0).astype(bf16)


def row_kernel(top_air, bot_air, top_cour, bot_cour, sib_ref, nxt_ref):
    odd = lax.axis_index("tile") % 2

    @pl.when(odd == 1)
    def _():
        pack_rows(top_air, top_cour, sib_ref, True)
        pack_rows(bot_air, bot_cour, nxt_ref, False)

    @pl.when(odd == 0)
    def _():
        pack_rows(bot_air, bot_cour, sib_ref, False)
        pack_rows(top_air, top_cour, nxt_ref, True)


def row_messages(air, courant):
    shape = jax.ShapeDtypeStruct((PLANES * 4, COLS), bf16)
    return pl.pallas_call(
        row_kernel,
        out_shape=(shape, shape),
        grid=(1,),
        in_specs=[
            pl.BlockSpec((FIELDS, LEVELS, 8, COLS), lambda i: (0, 0, 0, 0)),
            pl.BlockSpec((FIELDS, LEVELS, 8, COLS), lambda i: (0, 0, 2, 0)),
            pl.BlockSpec((3, 8, COLS), lambda i: (0, 0, 0)),
            pl.BlockSpec((3, 8, COLS), lambda i: (0, 2, 0)),
        ],
        out_specs=(pl.BlockSpec((PLANES * 4, COLS), lambda i: (0, 0)),) * 2,
        compiler_params=params(),
        cost_estimate=pl.CostEstimate(flops=400000, bytes_accessed=2000000, transcendentals=0),
        name="row_messages",
    )(air, air, courant, courant)


def halo_rows(north, south, plane):
    base = plane // 2 * 8
    n, s = north[base : base + 8], south[base : base + 8]
    sub = iota(n.shape, 0)
    if plane % 2:
        return jnp.where(sub < 3, roll(n, 4, 0), roll(s, 1, 0))
    return jnp.where(sub < 3, n, roll(s, 5, 0))


def north_south(sib, nxt):
    odd = lax.axis_index("tile") % 2 == 1
    a, b = sib[...].astype(f32), nxt[...].astype(f32)
    return jnp.where(odd, b, a), jnp.where(odd, a, b)


def strip_kernel(w_air, e_air, w_cour, e_cour, w_sib, w_nxt, e_sib, e_nxt, strip, coef, send_w, send_e):
    lane = iota((32, 128), 1)
    place = lane % 16
    for side, (air, cour, sib, nxt, send) in enumerate(
        ((w_air, w_cour, w_sib, w_nxt, send_w), (e_air, e_cour, e_sib, e_nxt, send_e))
    ):
        north, south = north_south(sib, nxt)
        own = lane < 6 if side == 0 else lane >= 122
        shift = 3 if side == 0 else 6

        def plane(p):
            rows = air[p // LEVELS, p % LEVELS] if p < 32 else cour[p - 32]
            whole = jnp.concatenate([rows, halo_rows(north, south, p)], 0)
            return jnp.where(own, whole, 0.0)

        middle = (place >= 3) & (place < 6)
        message = jnp.zeros((32, 128), f32)
        for f in range(FIELDS):
            total = roll(plane(f * LEVELS), shift, 1)
            for l in range(1, LEVELS):
                total = total + roll(plane(f * LEVELS + l), l * 16 + shift, 1)
            strip[side, f] = total
            message = message + roll(jnp.where(middle, total, 0.0), 3 * f - 3, 1)
        for k in range(3):
            total = roll(plane(32 + k), shift, 1)
            for s in (16, 32, 64):
                total = total + roll(total, s, 1)
            coef[side, k] = total
            message = message + roll(jnp.where(middle & (lane // 16 == k), total, 0.0), 9, 1)
        send[...] = message


def column_messages(air, courant, sib, nxt):
    message = jax.ShapeDtypeStruct((32, 128), f32)
    row_spec = lambda c: pl.BlockSpec((PLANES * 4, 128), lambda i: (0, c))
    return pl.pallas_call(
        strip_kernel,
        out_shape=(
            jax.ShapeDtypeStruct((2, FIELDS, 32, 128), f32),
            jax.ShapeDtypeStruct((2, 3, 32, 128), f32),
            message,
            message,
        ),
        grid=(1,),
        in_specs=[
            pl.BlockSpec((FIELDS, LEVELS, ROWS, 128), lambda i: (0, 0, 0, 0)),
            pl.BlockSpec((FIELDS, LEVELS, ROWS, 128), lambda i: (0, 0, 0, 5)),
            pl.BlockSpec((3, ROWS, 128), lambda i: (0, 0, 0)),
            pl.BlockSpec((3, ROWS, 128), lambda i: (0, 0, 5)),
            row_spec(0),
            row_spec(0),
            row_spec(5),
            row_spec(5),
        ],
        out_specs=(
            pl.BlockSpec((2, FIELDS, 32, 128), lambda i: (0, 0, 0, 0)),
            pl.BlockSpec((2, 3, 32, 128), lambda i: (0, 0, 0, 0)),
            pl.BlockSpec((32, 128), lambda i: (0, 0)),
            pl.BlockSpec((32, 128), lambda i: (0, 0)),
        ),
        compiler_params=params(),
        cost_estimate=pl.CostEstimate(flops=400000, bytes_accessed=1200000, transcendentals=0),
        name="column_messages",
    )(air, air, courant, courant, sib, nxt, sib, nxt)


def coefficients(cx, cy, kd):
    return 1.0 - cx - cy - 4.0 * kd, cx + kd, cy + kd, kd


def step(q, c):
    return (
        q * c[0]
        + roll(q, 1, 1) * c[1]
        + roll(q, 1, 0) * c[2]
        + (roll(q, -1, 1) + roll(q, -1, 0)) * c[3]
    )


def main_kernel(weights, air, cour, sib, nxt, cour_sib, cour_nxt, out, flux, coef):
    f = pl.program_id(0)

    @pl.when(f == 0)
    def _():
        north, south = north_south(cour_sib, cour_nxt)
        three = [jnp.concatenate([cour[k], halo_rows(north, south, k)], 0) for k in range(3)]
        for k, c in enumerate(coefficients(*three)):
            coef[k] = c

    north, south = north_south(sib, nxt)
    total = None
    for l in range(LEVELS):
        q = jnp.concatenate([air[0, l], halo_rows(north, south, l)], 0)
        for _ in range(STEPS):
            q = step(q, coef)
        out[0, l] = q[:ROWS]
        term = weights[f, l] * q[:ROWS]
        total = term if l == 0 else total + term
    total = total.astype(bf16).astype(f32)
    for c in range(COLS // BLK):
        flux[pl.ds(c * FIELDS + f, ROWS, stride=24), :] = total[:, c * BLK : (c + 1) * BLK]


def main_stencil(weights, air, courant, sib, nxt):
    rows = pl.BlockSpec((32, COLS), lambda f: (f, 0))
    tail = pl.BlockSpec((16, COLS), lambda f: (8, 0))
    return pl.pallas_call(
        main_kernel,
        out_shape=(
            jax.ShapeDtypeStruct((FIELDS, LEVELS, ROWS, COLS), f32),
            jax.ShapeDtypeStruct((ROWS * 24, BLK), f32),
        ),
        grid=(FIELDS,),
        in_specs=[
            pl.BlockSpec(memory_space=pltpu.SMEM),
            pl.BlockSpec((1, LEVELS, ROWS, COLS), lambda f: (f, 0, 0, 0)),
            pl.BlockSpec((3, ROWS, COLS), lambda f: (0, 0, 0)),
            rows,
            rows,
            tail,
            tail,
        ],
        out_specs=(
            pl.BlockSpec((1, LEVELS, ROWS, COLS), lambda f: (f, 0, 0, 0)),
            pl.BlockSpec((ROWS * 24, BLK), lambda f: (0, 0)),
        ),
        scratch_shapes=[pltpu.VMEM((4, 32, COLS), f32)],
        compiler_params=params(),
        cost_estimate=pl.CostEstimate(flops=30000000, bytes_accessed=6000000, transcendentals=0),
        name="main_stencil",
    )(weights, air, courant, sib, nxt, sib, nxt)


def fix_edges(weights, strip, coef, from_w, from_e, fixed, flux):
    lane = iota((32, 128), 1)
    place = lane % 16
    for side, received in enumerate((from_w, from_e)):
        got = received[...]
        first = 0 if side == 0 else 6
        here = (place >= first) & (place < first + 3)
        three = []
        for k in range(3):
            c = jnp.where((lane // 16 == k) & (place >= 12) & (place < 15), got, 0.0)
            c = roll(c, first - 12, 1)
            for s in (16, 32, 64):
                c = c + roll(c, s, 1)
            three.append(jnp.where(here, c, coef[side, k]))
        coefs = coefficients(*three)
        for f in range(FIELDS):
            q = jnp.where(here, roll(got, first - 3 * f, 1), strip[side, f])
            for _ in range(STEPS):
                q = step(q, coefs)
            q = q[:ROWS]
            fixed[side, f] = q
            scale = jnp.zeros((1, 128), f32)
            for l in range(LEVELS):
                scale = jnp.where(iota((1, 128), 1) // 16 == l, weights[f, l], scale)
            total = q * scale
            for s in (64, 32, 16):
                total = total + roll(total, s, 1)
            total = total.astype(bf16).astype(f32)
            column = iota((ROWS, 128), 1)
            at = pl.ds(8 + f + (0 if side == 0 else 20), ROWS, stride=24)
            if side == 0:
                flux[at, :] = jnp.where(column < 3, roll(total, -3, 1), flux[at, :])
            else:
                flux[at, :] = jnp.where(column >= 125, roll(total, 122, 1), flux[at, :])


def block_rows(ref, at, low):
    half = iota((8, BLK), 0) < 4
    if low:
        return jnp.where(half, ref[pl.ds(at + 8, 8), :], 0.0)
    return jnp.where(half, 0.0, ref[pl.ds(at + 4, 8), :])


def four_rows(ref, at):
    left = jnp.concatenate([block_rows(ref, at[0], True), block_rows(ref, at[2], True)], 0)
    right = jnp.concatenate([block_rows(ref, at[1], False), block_rows(ref, at[3], False)], 0)
    return jnp.concatenate([left, right], 1).astype(bf16)


def four_results(r):
    return r[0:4, :BLK], r[4:8, :BLK], r[8:12, BLK:], r[12:16, BLK:]


def send_kernel(
    src, row, weights, flux_in, strip, coef, from_w, from_e, offsets, tiles, out, fixed, flux, total
):
    g = pl.program_id(0)

    @pl.when(g == 0)
    def _():
        flux[0:8, :] = jnp.zeros((8, BLK), f32)
        flux[8 : 8 + ROWS * 24, :] = flux_in[...]
        flux[8 + ROWS * 24 :, :] = jnp.zeros((8, BLK), f32)
        fix_edges(weights, strip, coef, from_w, from_e, fixed, flux)
        total[...] = jnp.zeros(total.shape, f32)
        total[pl.ds(BACK, DEVICES, stride=CHUNK), :] = offsets[...]

    for t in range(0, GROUP, 4):
        at = [src[g * GROUP + t + i] for i in range(4)]
        w = jnp.concatenate(
            [
                jnp.concatenate([tiles[t], tiles[t + 1]], 0),
                jnp.concatenate([tiles[t + 2], tiles[t + 3]], 0),
            ],
            1,
        )
        r = jnp.dot(four_rows(flux, at), w, preferred_element_type=f32)
        for i, piece in enumerate(four_results(r)):
            total[pl.ds(row[g * GROUP + t + i], 4), :] = piece

    @pl.when(g == ENTRIES // GROUP - 1)
    def _():
        out[...] = total[...].astype(bf16)


def send_blocks(src, row, weights, flux, strip, coef, from_w, from_e, offsets, tiles):
    whole = lambda *shape: pl.BlockSpec(shape, lambda g: (0,) * len(shape))
    smem = pl.BlockSpec(memory_space=pltpu.SMEM)
    return pl.pallas_call(
        send_kernel,
        out_shape=(
            jax.ShapeDtypeStruct((DEVICES * CHUNK, BLK), bf16),
            jax.ShapeDtypeStruct((2, FIELDS, ROWS, 128), f32),
        ),
        grid=(ENTRIES // GROUP,),
        in_specs=[
            smem,
            smem,
            smem,
            whole(ROWS * 24, BLK),
            whole(2, FIELDS, 32, 128),
            whole(2, 3, 32, 128),
            whole(32, 128),
            whole(32, 128),
            whole(DEVICES, 128),
            pl.BlockSpec((GROUP, BLK, BLK), lambda g: (g, 0, 0)),
        ],
        out_specs=(whole(DEVICES * CHUNK, BLK), whole(2, FIELDS, ROWS, 128)),
        scratch_shapes=[
            pltpu.VMEM((ROWS * 24 + 16, BLK), f32),
            pltpu.VMEM((DEVICES * CHUNK, BLK), f32),
        ],
        compiler_params=params(),
        cost_estimate=pl.CostEstimate(flops=40000000, bytes_accessed=11000000, transcendentals=0),
        name="send_blocks",
    )(src, row, weights, flux, strip, coef, from_w, from_e, offsets, tiles)


def patch_kernel(fixed, air, out):
    column = iota((ROWS, 128), 1)

    def patch(west):
        for f in range(FIELDS):
            q = fixed[0, f]
            for l in range(LEVELS):
                first = 0 if west else 125
                new = roll(q, first - (l * 16 + 3), 1)
                keep = column >= 3 if west else column < 125
                out[f, l] = jnp.where(keep, air[f, l], new)

    @pl.when(pl.program_id(0) == 0)
    def _():
        patch(True)

    @pl.when(pl.program_id(0) == 1)
    def _():
        patch(False)


def patch_columns(fixed, air):
    lanes = pl.BlockSpec((FIELDS, LEVELS, ROWS, 128), lambda i: (0, 0, 0, 5 * i))
    return pl.pallas_call(
        patch_kernel,
        out_shape=jax.ShapeDtypeStruct(air.shape, f32),
        grid=(2,),
        in_specs=[pl.BlockSpec((1, FIELDS, ROWS, 128), lambda i: (i, 0, 0, 0)), lanes],
        out_specs=lanes,
        input_output_aliases={1: 0},
        compiler_params=params(),
        cost_estimate=pl.CostEstimate(flops=400000, bytes_accessed=1600000, transcendentals=0),
        name="patch_columns",
    )(fixed, air)


def ocean_kernel(payload, ocean, mixing, mask, out, back, got, ret):
    got[...] = payload[...].astype(f32)
    offsets = got[pl.ds(BACK, DEVICES, stride=CHUNK), :]
    by_slot = offsets.T
    blocks = iota((OCEAN_ROWS, DEVICES), 0).astype(f32)
    flux = None
    for j in range(CAP):
        place = (by_slot[j : j + 1, :] == blocks).astype(f32).astype(bf16)
        data = jnp.concatenate(
            [got[pl.ds(j * FIELDS + f, DEVICES, stride=CHUNK), :] for f in range(FIELDS)], 1
        ).astype(bf16)
        part = jnp.dot(place, data, preferred_element_type=f32)
        flux = part if j == 0 else flux + part
    wet = mask[...].astype(f32)
    mix = wet * mixing[...]
    surface = []
    for f in range(FIELDS):
        q = [ocean[f, l] for l in range(8)]
        q[0] = q[0] + wet * flux[:, f * BLK : (f + 1) * BLK]
        for l in range(8):
            new = q[l] + mix * (q[max(l - 1, 0)] + q[min(l + 1, 7)] - 2.0 * q[l])
            out[f, l] = new
            if l == 0:
                surface.append((wet * new).astype(bf16))
    surface = jnp.concatenate(surface, 1)
    lanes = iota((DEVICES, OCEAN_ROWS), 1).astype(f32)
    for j in range(CAP):
        pick = (offsets[:, j : j + 1] == lanes).astype(f32).astype(bf16)
        rows = jnp.dot(pick, surface, preferred_element_type=f32)
        for f in range(FIELDS):
            ret[pl.ds(j * FIELDS + f, DEVICES, stride=BACK), :] = rows[:, f * BLK : (f + 1) * BLK]
    back[...] = ret[...].astype(bf16)


def ocean_step(payload, ocean, mixing, mask):
    return pl.pallas_call(
        ocean_kernel,
        out_shape=(
            jax.ShapeDtypeStruct(ocean.shape, f32),
            jax.ShapeDtypeStruct((DEVICES * BACK, BLK), bf16),
        ),
        scratch_shapes=[
            pltpu.VMEM((DEVICES * CHUNK, BLK), f32),
            pltpu.VMEM((DEVICES * BACK, BLK), f32),
        ],
        compiler_params=params(),
        cost_estimate=pl.CostEstimate(flops=100000000, bytes_accessed=4000000, transcendentals=0),
        name="ocean_step",
    )(payload, ocean, mixing, mask)


def return_kernel(src, row, payload, tiles, out, got, total):
    g = pl.program_id(0)

    @pl.when(g == 0)
    def _():
        got[0:8, :] = jnp.zeros((8, BLK), f32)
        got[8 : 8 + DEVICES * BACK, :] = payload[...].astype(f32)
        got[8 + DEVICES * BACK :, :] = jnp.zeros((8, BLK), f32)
        total[...] = jnp.zeros(total.shape, f32)

    for t in range(0, GROUP, 4):
        at = [row[g * GROUP + t + i] for i in range(4)]
        w = jnp.concatenate(
            [
                jnp.concatenate([tiles[t], tiles[t + 1]], 1),
                jnp.concatenate([tiles[t + 2], tiles[t + 3]], 1),
            ],
            0,
        )
        r = lax.dot_general(
            four_rows(got, at), w, (((1,), (1,)), ((), ())), preferred_element_type=f32
        )
        for i, piece in enumerate(four_results(r)):
            here = pl.ds(src[g * GROUP + t + i], 4)
            total[here, :] = total[here, :] + piece

    @pl.when(g == ENTRIES // GROUP - 1)
    def _():
        for f in range(FIELDS):
            for c in range(COLS // BLK):
                out[f, :, c * BLK : (c + 1) * BLK] = total[pl.ds(c * FIELDS + f, ROWS, stride=24), :]


def return_blocks(src, row, payload, tiles):
    smem = pl.BlockSpec(memory_space=pltpu.SMEM)
    return pl.pallas_call(
        return_kernel,
        out_shape=jax.ShapeDtypeStruct((FIELDS, ROWS, COLS), f32),
        grid=(ENTRIES // GROUP,),
        in_specs=[
            smem,
            smem,
            pl.BlockSpec((DEVICES * BACK, BLK), lambda g: (0, 0)),
            pl.BlockSpec((GROUP, BLK, BLK), lambda g: (g, 0, 0)),
        ],
        out_specs=pl.BlockSpec((FIELDS, ROWS, COLS), lambda g: (0, 0, 0)),
        scratch_shapes=[
            pltpu.VMEM((DEVICES * BACK + 16, BLK), f32),
            pltpu.VMEM((ROWS * 24, BLK), f32),
        ],
        compiler_params=params(),
        cost_estimate=pl.CostEstimate(flops=40000000, bytes_accessed=11000000, transcendentals=0),
        name="return_blocks",
    )(src, row, payload, tiles)


def routes(src_block, owner, offset, tile_index):
    ids = jnp.arange(ENTRIES, dtype=jnp.int32)
    pick = tile_index[0][:, None] == ids[None, :]
    by_tile = lambda v: jnp.sum(jnp.where(pick, v[:, None], 0), axis=0)
    src, dest, place = by_tile(src_block[0]), by_tile(owner[0, :, 0]), by_tile(offset[0])
    earlier = (ids[None, :] < ids[:, None]) & (dest[:, None] == dest[None, :])
    rank = jnp.sum(earlier.astype(jnp.int32), axis=1)
    devices = jnp.arange(DEVICES, dtype=jnp.int32)
    to_dest = (devices[:, None] == dest[None, :]).astype(bf16)
    at_rank = jnp.where(rank[:, None] == devices[None, :], (place + 1)[:, None], 0).astype(bf16)
    offsets = jnp.dot(to_dest, at_rank, preferred_element_type=f32) - 1.0
    return src * FIELDS, dest * CHUNK + rank * FIELDS, dest * BACK + rank * FIELDS, offsets


def exchange(x, rows):
    x = x.reshape(DEVICES * CAP, rows // CAP, BLK) if rows == BACK else x.reshape(-1, 2, BLK)
    x = lax.all_to_all(x, ("face", "tile"), split_axis=0, concat_axis=0, tiled=True)
    return x.reshape(DEVICES * rows, BLK)


def shards(
    atmos_state,
    courant,
    level_weights,
    remap_tiles,
    src_block,
    owner,
    offset,
    tile_index,
    ocean_state,
    mixing,
    land_mask,
):
    faces, tile_count = lax.axis_size("face"), lax.axis_size("tile")
    sib, nxt = row_messages(atmos_state, courant)
    sib = lax.ppermute(sib, "tile", [(i, i ^ 1) for i in range(tile_count)])
    inner = [(i, i + 1) for i in range(1, tile_count - 1, 2)]
    nxt = lax.ppermute(nxt, "tile", inner + [(b, a) for a, b in inner])
    src, out_row, back_row, offsets = routes(src_block, owner, offset, tile_index)
    strip, coef, send_w, send_e = column_messages(atmos_state, courant, sib, nxt)
    from_e = lax.ppermute(send_w, "face", [((i + 1) % faces, i) for i in range(faces)])
    from_w = lax.ppermute(send_e, "face", [(i, (i + 1) % faces) for i in range(faces)])
    air, flux = main_stencil(level_weights, atmos_state, courant, sib, nxt)
    message, fixed = send_blocks(
        src, out_row, level_weights, flux, strip, coef, from_w, from_e, offsets, remap_tiles
    )
    message = exchange(message, CHUNK)
    air_state = patch_columns(fixed, air)
    ocean_out, back = ocean_step(message, ocean_state, mixing, land_mask)
    back = exchange(back, BACK)
    atmos_surface = return_blocks(src, back_row, back, remap_tiles)
    return air_state, ocean_out, atmos_surface


def solution(mesh):
    return jax.shard_map(
        shards,
        mesh=mesh,
        in_specs=(
            P(None, None, "tile", "face"),
            P(None, "tile", "face"),
            P(),
            P(("face", "tile"), None, None),
            P(("face", "tile"), None),
            P(("face", "tile"), None, None),
            P(("face", "tile"), None),
            P(("face", "tile"), None),
            P(None, None, "face", "tile"),
            P("face", "tile"),
            P("face", "tile"),
        ),
        out_specs=(
            P(None, None, "tile", "face"),
            P(None, None, "face", "tile"),
            P(None, "tile", "face"),
        ),
        check_vma=False,
    )
```

```python
import jax
import jax.numpy as jnp
from jax import lax
from jax.experimental import pallas as pl
from jax.experimental.pallas import tpu as pltpu
from jax.sharding import PartitionSpec as P

STEPS = 3
FIELDS, LEVELS, ROWS, COLS, BLK = 4, 8, 24, 768, 128
MESSAGE = 112
ENTRIES, DEVICES, CAP, OCEAN_ROWS = 288, 128, 5, 64
CHUNK = 22
BACK = CAP * FIELDS
f32, bf16 = jnp.float32, jnp.bfloat16


def iota(shape, dim):
    return lax.broadcasted_iota(jnp.int32, shape, dim)


def roll(x, shift, axis):
    shift = shift % x.shape[axis]
    return pltpu.roll(x, shift, axis) if shift else x


def params(mib=16):
    return pltpu.CompilerParams(vmem_limit_bytes=mib << 20)


in_vmem = pl.BlockSpec(memory_space=pltpu.VMEM)
in_smem = pl.BlockSpec(memory_space=pltpu.SMEM)
in_hbm = pl.BlockSpec(memory_space=pltpu.HBM)


def hbm(*arrays):
    return [pltpu.with_memory_space_constraint(x, pltpu.HBM) for x in arrays]


def start_all(pairs, sems):
    copies = [pltpu.make_async_copy(a, b, sems.at[i]) for i, (a, b) in enumerate(pairs)]
    for copy in copies:
        copy.start()
    return copies


def wait_all(copies):
    for copy in copies:
        copy.wait()


def start_tiles(stored, tiles, sems, bounds):
    parts = [pl.ds(a, b - a) for a, b in zip(bounds, bounds[1:])]
    pairs = [(stored.at[part], tiles.at[part]) for part in parts]
    return dict(zip(bounds, start_all(pairs, sems)))


def row_kernel(air, cour, sib_ref, nxt_ref, top, bot, top_cour, bot_cour, sems):
    copies = []
    for c in range(COLS // BLK):
        lanes = pl.ds(c * BLK, BLK)
        copies.append((air.at[:, :, pl.ds(0, 8), lanes], top.at[c]))
        copies.append((air.at[:, :, pl.ds(16, 8), lanes], bot.at[c]))
    copies.append((cour.at[:, pl.ds(0, 8), :], top_cour))
    copies.append((cour.at[:, pl.ds(16, 8), :], bot_cour))
    copies = [pltpu.make_async_copy(a, b, sems.at[i]) for i, (a, b) in enumerate(copies)]
    for copy in copies:
        copy.start()
    for copy in copies:
        copy.wait()

    def pack(out, at_top):
        first = 0 if at_top else 5
        rows, numbers = (top, top_cour) if at_top else (bot, bot_cour)
        for c in range(COLS // BLK):
            flat = rows.at[c].reshape(FIELDS * LEVELS * 8, BLK)

            def tile(i):
                return flat[pl.ds(i // 3 * 64 + first + i % 3, LEVELS, stride=8), :]

            for i in range(0, FIELDS * 3, 2):
                both = jnp.concatenate([tile(i), tile(i + 1)], 0)
                out[i * 8 : i * 8 + 16, c * BLK : (c + 1) * BLK] = both.astype(bf16)
        sub = iota((8, COLS), 0)
        pair = jnp.where(sub < 4, roll(numbers[0], -first, 0), roll(numbers[1], 4 - first, 0))
        last = jnp.where(sub < 4, roll(numbers[2], -first, 0), 0.0)
        out[96:112, :] = jnp.concatenate([pair, last], 0).astype(bf16)

    odd = lax.axis_index("tile") % 2

    @pl.when(odd == 1)
    def _():
        pack(sib_ref, True)
        pack(nxt_ref, False)

    @pl.when(odd == 0)
    def _():
        pack(sib_ref, False)
        pack(nxt_ref, True)


def row_messages(air, courant):
    shape = jax.ShapeDtypeStruct((MESSAGE, COLS), bf16)
    return pl.pallas_call(
        row_kernel,
        out_shape=(shape, shape),
        in_specs=[in_hbm] * 2,
        out_specs=(in_vmem,) * 2,
        scratch_shapes=[pltpu.VMEM((COLS // BLK, FIELDS, LEVELS, 8, BLK), f32)] * 2
        + [pltpu.VMEM((3, 8, COLS), f32)] * 2
        + [pltpu.SemaphoreType.DMA((14,))],
        compiler_params=params(),
        cost_estimate=pl.CostEstimate(flops=400000, bytes_accessed=2000000, transcendentals=0),
        name="row_messages",
    )(*hbm(air, courant))


def courant_rows(north, south, k):
    base = k // 2 * 8
    n, s = north[base : base + 8], south[base : base + 8]
    sub = iota(n.shape, 0)
    if k % 2:
        return jnp.where(sub < 3, roll(n, 4, 0), roll(s, 1, 0))
    return jnp.where(sub < 3, n, roll(s, 5, 0))


def halo_sum(weights, f, north, south):
    sub = iota((8, north.shape[1]), 0)
    scale = jnp.zeros(sub.shape, f32)
    for l in range(LEVELS):
        scale = jnp.where(sub == l, weights[f, l], scale)
    rows = jnp.zeros(sub.shape, f32)
    for j in range(3):
        at = slice((f * 3 + j) * 8, (f * 3 + j + 1) * 8)
        rows = jnp.where(sub == j, jnp.sum(north[at] * scale, axis=0, keepdims=True), rows)
        rows = jnp.where(sub == 5 + j, jnp.sum(south[at] * scale, axis=0, keepdims=True), rows)
    return rows


def north_south(sib, nxt):
    odd = lax.axis_index("tile") % 2 == 1
    a, b = sib.astype(f32), nxt.astype(f32)
    return jnp.where(odd, b, a), jnp.where(odd, a, b)


SHIFTS = (3, 6)


def edge_lanes(side):
    return slice(0, BLK) if side == 0 else slice(COLS - BLK, COLS)


def own_columns(side, rows):
    lane = iota((rows, 128), 1)
    return lane < 6 if side == 0 else lane >= 122


def gather_levels(level, shift):
    total = roll(level(0), shift, 1)
    for l in range(1, LEVELS):
        total = total + roll(level(l), l * 16 + shift, 1)
    return total


def spread(x):
    for s in (16, 32, 64):
        x = x + roll(x, s, 1)
    return x


def message_rows(strips, coefs, sums):
    lane = iota(strips[0].shape, 1)
    place = lane % 16
    middle = (place >= 3) & (place < 6)
    message = jnp.zeros(strips[0].shape, f32)
    for f in range(FIELDS):
        message = message + roll(jnp.where(middle, strips[f], 0.0), 3 * f - 3, 1)
    for k in range(3):
        mine = middle & (lane // 16 == k)
        message = message + roll(jnp.where(mine, coefs[k], 0.0), 9, 1)
    return message + roll(jnp.where(middle & (lane < 64), sums, 0.0), 57, 1)


def level_lanes(weights, f, rows):
    lane = iota((rows, 128), 1) // 16
    scale = jnp.zeros((rows, 128), f32)
    for l in range(LEVELS):
        scale = jnp.where(lane == l, weights[f, l], scale)
    return scale


def sum_strip(weights, strips):
    rows = strips[0].shape[0]
    group = iota((rows, 128), 1) // 16
    total = jnp.zeros((rows, 128), f32)
    for f in range(FIELDS):
        whole = spread(strips[f] * level_lanes(weights, f, rows))
        total = jnp.where(group == f, whole, total)
    return total


def route(src, owner, offset, tile_index, routes, offsets):
    row = lambda ref: ref[...].astype(f32)
    sub = iota((8, ENTRIES), 0)
    known = jnp.where(sub == 0, row(src), jnp.where(sub == 1, row(owner), row(offset))).astype(bf16)
    pick = (iota((ENTRIES, ENTRIES), 0) == tile_index[...]).astype(f32).astype(bf16)
    along = (((1,), (1,)), ((), ()))
    by_tile = lax.dot_general(known, pick, along, preferred_element_type=f32)
    down = lax.dot_general(pick, known, along, preferred_element_type=f32)
    source, dest, place = by_tile[0:1], by_tile[1:2], by_tile[2:3]
    earlier = iota((ENTRIES, ENTRIES), 0) < iota((ENTRIES, ENTRIES), 1)
    same = jnp.where(earlier & (down[:, 1:2] == dest), 1.0, 0.0)
    rank = jnp.sum(same, axis=0, keepdims=True)
    numbers = jnp.where(
        sub == 0,
        source * FIELDS,
        jnp.where(sub == 1, dest * CHUNK + rank * FIELDS, dest * BACK + rank * FIELDS),
    )
    routes[...] = numbers.astype(jnp.int32)
    device = iota((DEVICES, ENTRIES), 0).astype(f32)
    to_dest = (device == dest).astype(f32).astype(bf16)
    at_rank = jnp.where(device == rank, place + 1.0, 0.0).astype(bf16)
    offsets[...] = lax.dot_general(to_dest, at_rank, along, preferred_element_type=f32) - 1.0


def own_kernel(weights, *refs):
    given, (strip_out, coef, message, sums, level_sum, routes, offsets, tiles), refs = (
        refs[:7],
        refs[7:15],
        refs[15:],
    )
    here, (strip, sems) = refs[:6], refs[6:]
    copies = start_all(zip(given, (*here, tiles)), sems)
    wait_all(copies[:4])
    route(*here[:4], routes, offsets)
    wait_all(copies[4:6])
    air, cour = here[4:6]
    for side in range(2):
        lanes, own, shift = edge_lanes(side), own_columns(side, ROWS), SHIFTS[side]
        strips, coefs = [], []
        for f in range(FIELDS):
            level = lambda l: jnp.where(own, air[f, l, :, lanes], 0.0)
            strips.append(gather_levels(level, shift))
            strip[side, f] = strips[f]
        for k in range(3):
            coefs.append(spread(roll(jnp.where(own, cour[k, :, lanes], 0.0), shift, 1)))
            coef[side, k] = coefs[k]
        sums[side] = sum_strip(weights, strips)
        message[side] = message_rows(strips, coefs, sums[side])
    copy = pltpu.make_async_copy(strip, strip_out, sems.at[7])
    copy.start()
    for f in range(FIELDS):
        total = weights[f, 0] * air[f, 0]
        for l in range(1, LEVELS):
            total = total + weights[f, l] * air[f, l]
        level_sum[f] = total
    copy.wait()
    copies[6].wait()


def own_parts(weights, *given):
    return pl.pallas_call(
        own_kernel,
        out_shape=(
            pltpu.HBM((2, FIELDS, ROWS, 128), f32),
            jax.ShapeDtypeStruct((2, 3, ROWS, 128), f32),
            jax.ShapeDtypeStruct((2, ROWS, 128), f32),
            jax.ShapeDtypeStruct((2, ROWS, 128), f32),
            jax.ShapeDtypeStruct((FIELDS, ROWS, COLS), f32),
            jax.ShapeDtypeStruct((8, ENTRIES), jnp.int32),
            jax.ShapeDtypeStruct((DEVICES, 128), f32),
            pltpu.VMEM(given[6].shape, bf16),
        ),
        in_specs=[in_smem] + [in_hbm] * 7,
        out_specs=(in_hbm,) + (in_vmem,) * 7,
        scratch_shapes=[pltpu.VMEM(x.shape, x.dtype) for x in given[:6]]
        + [pltpu.VMEM((2, FIELDS, ROWS, 128), f32), pltpu.SemaphoreType.DMA((8,))],
        compiler_params=params(),
        cost_estimate=pl.CostEstimate(flops=1600000, bytes_accessed=1200000, transcendentals=0),
        name="own_parts",
    )(*hbm(weights, *given))


def halo_kernel(weights, sib, nxt, own_message, strip, coef, sums, send_w, send_e, halo):
    for side, send in enumerate((send_w, send_e)):
        lanes, own, shift = edge_lanes(side), own_columns(side, 8), SHIFTS[side]
        north, south = north_south(sib[:, lanes], nxt[:, lanes])
        for f in range(FIELDS):
            for j in range(3):
                at = f * 64 + j * 8
                halo[side, at : at + 8, :] = north[(f * 3 + j) * 8 : (f * 3 + j + 1) * 8]
                halo[side, at + 40 : at + 48, :] = south[(f * 3 + j) * 8 : (f * 3 + j + 1) * 8]
            halo[side, f * 64 + 24 : f * 64 + 40, :] = jnp.zeros((16, BLK), f32)
        strips, coefs = [], []
        for f in range(FIELDS):
            level = lambda l: jnp.where(own, halo[side, pl.ds(f * 64 + l, 8, stride=8), :], 0.0)
            strips.append(gather_levels(level, shift))
            strip[side, f] = strips[f]
        for k in range(3):
            rows = courant_rows(north[96:112], south[96:112], k)
            coefs.append(spread(roll(jnp.where(own, rows, 0.0), shift, 1)))
            coef[side, k] = coefs[k]
        total = jnp.zeros((8, BLK), f32)
        for f in range(FIELDS):
            rows = jnp.where(own, halo_sum(weights, f, north, south), 0.0)
            total = total + roll(rows, f * 16 + shift, 1)
        sums[side] = total
        send[:ROWS] = own_message[side]
        send[ROWS:] = message_rows(strips, coefs, sums[side])


def column_messages(weights, sib, nxt, own_message):
    message = jax.ShapeDtypeStruct((32, 128), f32)
    return pl.pallas_call(
        halo_kernel,
        out_shape=(
            jax.ShapeDtypeStruct((2, FIELDS, 8, 128), f32),
            jax.ShapeDtypeStruct((2, 3, 8, 128), f32),
            jax.ShapeDtypeStruct((2, 8, 128), f32),
            message,
            message,
        ),
        in_specs=[in_smem] + [in_vmem] * 3,
        out_specs=(in_vmem,) * 5,
        scratch_shapes=[pltpu.VMEM((2, FIELDS * 64, BLK), f32)],
        compiler_params=params(),
        cost_estimate=pl.CostEstimate(flops=100000, bytes_accessed=400000, transcendentals=0),
        name="column_messages",
    )(*hbm(weights), sib, nxt, own_message)


def received(side, got):
    lane = iota((32, 128), 1)
    place, group = lane % 16, lane // 16
    first = 0 if side == 0 else 6
    here = (place >= first) & (place < first + 3)
    spare = (place >= 12) & (place < 15)
    numbers = [
        spread(roll(jnp.where((group == k) & spare, got, 0.0), first - 12, 1)) for k in range(3)
    ]
    return here, numbers, roll(got, first - 60, 1)


def coefficients(cx, cy, kd):
    return 1.0 - cx - cy - 4.0 * kd, cx + kd, cy + kd, kd


def step(q, c):
    return (
        q * c[0]
        + roll(q, 1, 1) * c[1]
        + roll(q, 1, 0) * c[2]
        + (roll(q, -1, 1) + roll(q, -1, 0)) * c[3]
    )


def level_weight(weights, f, shape):
    scale = jnp.zeros(shape, f32)
    for l in range(LEVELS):
        scale = jnp.where(iota(shape, 0) == l, weights[f, l], scale)
    return scale


def flux_kernel(weights, level_sum, given, sib, nxt, flux, sib_out, nxt_out, cour, sems):
    copies = start_all([(given, cour), (sib, sib_out), (nxt, nxt_out)], sems)
    copies[0].wait()
    north, south = north_south(sib[...], nxt[...])
    three = [
        jnp.concatenate([cour[k], courant_rows(north[96:], south[96:], k)], 0) for k in range(3)
    ]
    coefs = coefficients(*three)
    for f in range(FIELDS):
        rows = halo_sum(weights, f, north, south)
        q = jnp.concatenate([level_sum[f], rows], 0)
        for _ in range(STEPS):
            q = step(q, coefs)
        q = q[:ROWS].astype(bf16).astype(f32)
        for c in range(COLS // BLK):
            flux[pl.ds(c * FIELDS + f, ROWS, stride=24), :] = q[:, c * BLK : (c + 1) * BLK]
    wait_all(copies[1:])


def flux_stencil(weights, level_sum, courant, sib, nxt):
    return pl.pallas_call(
        flux_kernel,
        out_shape=(
            jax.ShapeDtypeStruct((ROWS * 24, BLK), f32),
            pltpu.HBM(sib.shape, bf16),
            pltpu.HBM(nxt.shape, bf16),
        ),
        in_specs=[in_smem, in_vmem, in_hbm, in_vmem, in_vmem],
        out_specs=(in_vmem, in_hbm, in_hbm),
        scratch_shapes=[pltpu.VMEM(courant.shape, f32), pltpu.SemaphoreType.DMA((3,))],
        compiler_params=params(),
        cost_estimate=pl.CostEstimate(flops=3000000, bytes_accessed=1000000, transcendentals=0),
        name="flux_stencil",
    )(*hbm(weights), level_sum, *hbm(courant), sib, nxt)


def advance(c, q, below, above):
    return q * c[0] + roll(q, 1, 1) * c[1] + below * c[2] + (roll(q, -1, 1) + above) * c[3]


def sweep(coef, starts, done, emits):
    for r in range(-3, ROWS + 3):
        for start, d in zip(starts, done):
            d[0][r] = start(r)
        for s in range(3):
            at = r - 1 - s
            if s - 2 <= at < ROWS + 2 - s:
                c = [coef[k, at % 32 : at % 32 + 1, :] for k in range(4)]
                for d in done:
                    d[s + 1][at] = advance(c, d[s][at], d[s][at - 1], d[s][at + 1])
                if s == 2:
                    for emit, d in zip(emits, done):
                        emit(at, d[3][at])


def air_kernel(air, *refs):
    given, (out, ocean_out, *here), refs = refs[:12], refs[12:26], refs[26:]
    into, done, halo, coef, levels, in_sems, out_sems, sems = refs
    flux, ocean, mixing, mask, cour, sib, nxt, own_strip, halo_strip, strip_coef, from_w, from_e = here
    parts = COLS // BLK

    def copy_in(f, c):
        source = air.at[f, :, :, pl.ds(c * BLK, BLK)]
        return pltpu.make_async_copy(source, into.at[f, c], in_sems.at[f, c])

    def copy_out(f, c):
        target = out.at[f, :, :, pl.ds(c * BLK, BLK)]
        return pltpu.make_async_copy(done.at[f, c], target, out_sems.at[f, c])

    small = start_all(zip(given, here), sems)
    for f in range(FIELDS):
        for c in range(parts):
            copy_in(f, c).start()
    wait_all(small)
    ocean_copy = pltpu.make_async_copy(levels, ocean_out, sems.at[12])
    ocean_levels(flux, ocean, mixing, mask, levels)
    ocean_copy.start()
    north, south = north_south(sib[...], nxt[...])
    halo[0] = south[:96]
    halo[1] = north[:96]
    three = [
        jnp.concatenate([cour[k], courant_rows(north[96:], south[96:], k)], 0) for k in range(3)
    ]
    for k, c in enumerate(coefficients(*three)):
        coef[k] = c
    edges = []
    for side, got in enumerate((from_w, from_e)):
        here, _, _ = received(side, got[...])
        numbers = coefficients(*(strip_coef[side, k] for k in range(3)))
        first = 0 if side == 0 else 6
        for f in range(FIELDS):
            mine = jnp.concatenate([own_strip[side, f], halo_strip[side, f]], 0)
            q = jnp.where(here, roll(got[...], first - 3 * f, 1), mine)
            for _ in range(STEPS):
                q = step(q, numbers)
            edges.append(q[:ROWS])

    def starter(f):
        flat = [into.at[f, c].reshape(LEVELS * ROWS, BLK) for c in range(parts)]

        def start(r):
            if r < 0:
                return halo[0, f * 24 + (r + 3) * 8 : f * 24 + (r + 4) * 8, :]
            if r >= ROWS:
                return halo[1, f * 24 + (r - ROWS) * 8 : f * 24 + (r - ROWS + 1) * 8, :]
            return jnp.concatenate([x[pl.ds(r, LEVELS, stride=ROWS), :] for x in flat], 1)

        return start

    def emitter(f):
        flat = [done.at[f, c].reshape(LEVELS * ROWS, BLK) for c in range(parts)]

        def emit(r, q):
            for c in range(parts):
                flat[c][pl.ds(r, LEVELS, stride=ROWS), :] = q[:, c * BLK : (c + 1) * BLK]

        return emit

    column = iota((ROWS, 128), 1)
    for fields in ((0, 1), (2, 3)):
        for f in fields:
            for c in range(parts):
                copy_in(f, c).wait()
        sweep(
            coef,
            [starter(f) for f in fields],
            [[{}, {}, {}, {}] for f in fields],
            [emitter(f) for f in fields],
        )
        for f in fields:
            for c in range(1, parts - 1):
                copy_out(f, c).start()
            for l in range(LEVELS):
                west, east = roll(edges[f], -l * 16 - 3, 1), roll(edges[FIELDS + f], 122 - l * 16, 1)
                done[f, 0, l] = jnp.where(column < 3, west, done[f, 0, l])
                done[f, parts - 1, l] = jnp.where(column >= 125, east, done[f, parts - 1, l])
            copy_out(f, 0).start()
            copy_out(f, parts - 1).start()
    for f in range(FIELDS):
        for c in range(parts):
            copy_out(f, c).wait()
    ocean_copy.wait()


def ocean_levels(flux, ocean, mixing, mask, out):
    wet = mask[...].astype(f32)
    mix = wet * mixing[...]
    for f in range(FIELDS):
        q = [ocean[f, l] for l in range(8)]
        q[0] = q[0] + wet * flux[f]
        for l in range(8):
            out[f, l] = q[l] + mix * (q[max(l - 1, 0)] + q[min(l + 1, 7)] - 2.0 * q[l])


def air_steps(air, *given):
    parts = COLS // BLK
    return pl.pallas_call(
        air_kernel,
        out_shape=(pltpu.HBM(air.shape, f32), pltpu.HBM(given[1].shape, f32)),
        in_specs=[in_hbm] * 13,
        out_specs=(in_hbm, in_hbm),
        scratch_shapes=[pltpu.VMEM(x.shape, x.dtype) for x in given]
        + [
            pltpu.VMEM((FIELDS, parts, LEVELS, ROWS, BLK), f32),
            pltpu.VMEM((FIELDS, parts, LEVELS, ROWS, BLK), f32),
            pltpu.VMEM((2, 96, COLS), f32),
            pltpu.VMEM((4, 32, COLS), f32),
            pltpu.VMEM(given[1].shape, f32),
            pltpu.SemaphoreType.DMA((FIELDS, parts)),
            pltpu.SemaphoreType.DMA((FIELDS, parts)),
            pltpu.SemaphoreType.DMA((13,)),
        ],
        compiler_params=params(),
        cost_estimate=pl.CostEstimate(flops=30000000, bytes_accessed=6000000, transcendentals=0),
        name="air_steps",
    )(*hbm(air, *given))


def fix_edges(own_sums, halo_sums, own_coef, halo_coef, from_w, from_e, coef_out, flux):
    lane = iota((32, 128), 1)
    column = iota((ROWS, 128), 1)
    for side, got in enumerate((from_w, from_e)):
        here, numbers, sums = received(side, got[...])
        three = []
        for k in range(3):
            mine = jnp.concatenate([own_coef[side, k], halo_coef[side, k]], 0)
            three.append(jnp.where(here, numbers[k], mine))
            coef_out[side, k] = three[k]
        coefs = coefficients(*three)
        mine = jnp.concatenate([own_sums[side], halo_sums[side]], 0)
        q = jnp.where(here & (lane < 64), sums, mine)
        for _ in range(STEPS):
            q = step(q, coefs)
        q = q[:ROWS].astype(bf16).astype(f32)
        for f in range(FIELDS):
            at = pl.ds(8 + f + (0 if side == 0 else 20), ROWS, stride=24)
            if side == 0:
                flux[at, :] = jnp.where(column < 3, roll(q, -f * 16 - 3, 1), flux[at, :])
            else:
                flux[at, :] = jnp.where(column >= 125, roll(q, 122 - f * 16, 1), flux[at, :])


def block_rows(ref, at, low):
    half = iota((8, BLK), 0) < 4
    if low:
        return jnp.where(half, ref[pl.ds(at + 8, 8), :], 0.0)
    return jnp.where(half, 0.0, ref[pl.ds(at + 4, 8), :])


def four_rows(ref, at):
    left = jnp.concatenate([block_rows(ref, at[0], True), block_rows(ref, at[2], True)], 0)
    right = jnp.concatenate([block_rows(ref, at[1], False), block_rows(ref, at[3], False)], 0)
    return jnp.concatenate([left, right], 1).astype(bf16)


def four_results(r):
    return r[0:4, :BLK], r[4:8, :BLK], r[8:12, BLK:], r[12:16, BLK:]


def send_kernel(routes, flux_in, halo_strip, *refs):
    edges, (offsets, tiles, out, *kept, flux, total, coef, sems) = refs[:6], refs[6:]
    copies = start_all(zip((halo_strip, *edges[4:6]), kept), sems)
    flux[0:8, :] = jnp.zeros((8, BLK), f32)
    flux[8 : 8 + ROWS * 24, :] = flux_in[...]
    flux[8 + ROWS * 24 :, :] = jnp.zeros((8, BLK), f32)
    fix_edges(*edges, coef, flux)
    copies.append(pltpu.make_async_copy(coef, kept[3], sems.at[3]))
    copies[3].start()
    total[...] = jnp.zeros(total.shape, f32)
    total[pl.ds(BACK, DEVICES, stride=CHUNK), :] = offsets[...]
    for t in range(0, ENTRIES, 4):
        at = [routes[0, t + i] for i in range(4)]
        w = jnp.concatenate(
            [
                jnp.concatenate([tiles[t], tiles[t + 1]], 0),
                jnp.concatenate([tiles[t + 2], tiles[t + 3]], 0),
            ],
            1,
        )
        r = jnp.dot(four_rows(flux, at), w, preferred_element_type=f32)
        for i, piece in enumerate(four_results(r)):
            total[pl.ds(routes[1, t + i], 4), :] = piece
    out[...] = total[...].astype(bf16)
    wait_all(copies)


def send_blocks(routes, flux, halo_strip, edges, offsets, tiles):
    return pl.pallas_call(
        send_kernel,
        out_shape=(
            jax.ShapeDtypeStruct((DEVICES * CHUNK, BLK), bf16),
            pltpu.HBM(halo_strip.shape, f32),
            pltpu.HBM((32, 128), f32),
            pltpu.HBM((32, 128), f32),
            pltpu.HBM((2, 3, 32, 128), f32),
        ),
        in_specs=[in_smem] + [in_vmem] * 10,
        out_specs=(in_vmem,) + (in_hbm,) * 4,
        scratch_shapes=[
            pltpu.VMEM((ROWS * 24 + 16, BLK), f32),
            pltpu.VMEM((DEVICES * CHUNK, BLK), f32),
            pltpu.VMEM((2, 3, 32, 128), f32),
            pltpu.SemaphoreType.DMA((4,)),
        ],
        compiler_params=params(),
        cost_estimate=pl.CostEstimate(flops=40000000, bytes_accessed=11000000, transcendentals=0),
        name="send_blocks",
    )(routes, flux, halo_strip, *edges, offsets, tiles)


def ocean_kernel(payload, ocean, mixing, mask, flux_out, back, got, ret, packed, kept, sems):
    got[...] = payload[...].astype(f32)
    offsets = got[pl.ds(BACK, DEVICES, stride=CHUNK), :]
    by_slot = offsets.T
    blocks = iota((OCEAN_ROWS, DEVICES), 0).astype(f32)
    flux = None
    for j in range(CAP):
        place = (by_slot[j : j + 1, :] == blocks).astype(f32).astype(bf16)
        data = jnp.concatenate(
            [got[pl.ds(j * FIELDS + f, DEVICES, stride=CHUNK), :] for f in range(FIELDS)], 1
        ).astype(bf16)
        part = jnp.dot(place, data, preferred_element_type=f32)
        flux = part if j == 0 else flux + part
    wet = mask[...].astype(f32)
    mix = wet * mixing[...]
    surface = []
    for f in range(FIELDS):
        piece = flux[:, f * BLK : (f + 1) * BLK]
        kept[f] = piece
        top, below = ocean[f, 0] + wet * piece, ocean[f, 1]
        new = top + mix * (top + below - 2.0 * top)
        surface.append((wet * new).astype(bf16))
    copies = [pltpu.make_async_copy(kept, flux_out, sems.at[0])]
    copies[0].start()
    surface = jnp.concatenate(surface, 1)
    lanes = iota((DEVICES, OCEAN_ROWS), 1).astype(f32)
    for j in range(CAP):
        pick = (offsets[:, j : j + 1] == lanes).astype(f32).astype(bf16)
        rows = jnp.dot(pick, surface, preferred_element_type=f32)
        for f in range(FIELDS):
            ret[pl.ds(j * FIELDS + f, DEVICES, stride=BACK), :] = rows[:, f * BLK : (f + 1) * BLK]
    packed[...] = ret[...].astype(bf16)
    copies.append(pltpu.make_async_copy(packed, back, sems.at[1]))
    copies[1].start()
    for copy in copies:
        copy.wait()


def ocean_surface(payload, ocean, mixing, mask):
    return pl.pallas_call(
        ocean_kernel,
        out_shape=(
            pltpu.HBM((FIELDS, OCEAN_ROWS, BLK), f32),
            pltpu.HBM((DEVICES * BACK, BLK), bf16),
        ),
        in_specs=[in_vmem] * 4,
        out_specs=(in_hbm, in_hbm),
        scratch_shapes=[
            pltpu.VMEM((DEVICES * CHUNK, BLK), f32),
            pltpu.VMEM((DEVICES * BACK, BLK), f32),
            pltpu.VMEM((DEVICES * BACK, BLK), bf16),
            pltpu.VMEM((FIELDS, OCEAN_ROWS, BLK), f32),
            pltpu.SemaphoreType.DMA((2,)),
        ],
        compiler_params=params(),
        cost_estimate=pl.CostEstimate(flops=100000000, bytes_accessed=4000000, transcendentals=0),
        name="ocean_surface",
    )(payload, ocean, mixing, mask)


def return_kernel(routes, payload, stored, out, got, total, arrived, tiles, sems):
    first = start_all([(payload, arrived)], sems)[0]
    waits = start_tiles(stored, tiles, sems.at[pl.ds(1, 6)], (0, 48, 96, 144, 192, 240, ENTRIES))
    got[0:8, :] = jnp.zeros((8, BLK), f32)
    got[8 + DEVICES * BACK :, :] = jnp.zeros((8, BLK), f32)
    total[...] = jnp.zeros(total.shape, f32)
    first.wait()
    got[8 : 8 + DEVICES * BACK, :] = arrived[...].astype(f32)
    for t in range(0, ENTRIES, 4):
        if t in waits:
            waits[t].wait()
        at = [routes[2, t + i] for i in range(4)]
        w = jnp.concatenate(
            [
                jnp.concatenate([tiles[t], tiles[t + 1]], 1),
                jnp.concatenate([tiles[t + 2], tiles[t + 3]], 1),
            ],
            0,
        )
        r = lax.dot_general(
            four_rows(got, at), w, (((1,), (1,)), ((), ())), preferred_element_type=f32
        )
        for i, piece in enumerate(four_results(r)):
            here = pl.ds(routes[0, t + i], 4)
            total[here, :] = total[here, :] + piece
    for f in range(FIELDS):
        for c in range(COLS // BLK):
            out[f, :, c * BLK : (c + 1) * BLK] = total[pl.ds(c * FIELDS + f, ROWS, stride=24), :]


def return_blocks(routes, payload, tiles):
    return pl.pallas_call(
        return_kernel,
        out_shape=jax.ShapeDtypeStruct((FIELDS, ROWS, COLS), f32),
        in_specs=[in_smem, pl.BlockSpec(memory_space=pl.ANY), in_hbm],
        scratch_shapes=[
            pltpu.VMEM((DEVICES * BACK + 16, BLK), f32),
            pltpu.VMEM((ROWS * 24, BLK), f32),
            pltpu.VMEM((DEVICES * BACK, BLK), bf16),
            pltpu.VMEM((ENTRIES, BLK, BLK), bf16),
            pltpu.SemaphoreType.DMA((7,)),
        ],
        compiler_params=params(24),
        cost_estimate=pl.CostEstimate(flops=40000000, bytes_accessed=11000000, transcendentals=0),
        name="return_blocks",
    )(routes, payload, *hbm(tiles))


def exchange(x, rows):
    x = x.reshape(DEVICES * CAP, rows // CAP, BLK) if rows == BACK else x.reshape(-1, 2, BLK)
    x = lax.all_to_all(x, ("face", "tile"), split_axis=0, concat_axis=0, tiled=True)
    return x.reshape(DEVICES * rows, BLK)


def shards(
    atmos_state,
    courant,
    level_weights,
    remap_tiles,
    src_block,
    owner,
    offset,
    tile_index,
    ocean_state,
    mixing,
    land_mask,
):
    faces, tile_count = lax.axis_size("face"), lax.axis_size("tile")
    sib, nxt = row_messages(atmos_state, courant)
    inner = [(i, i + 1) for i in range(1, tile_count - 1, 2)]
    nxt = lax.ppermute(nxt, "tile", inner + [(b, a) for a, b in inner])
    sib = lax.ppermute(sib, "tile", [(i, i ^ 1) for i in range(tile_count)])
    own_strip, own_coef, own_message, own_sums, level_sum, routes, offsets, tiles = own_parts(
        *(level_weights, src_block, owner.reshape(1, -1), offset, tile_index),
        *(atmos_state, courant, remap_tiles),
    )
    halo_strip, halo_coef, halo_sums, send_w, send_e = column_messages(
        level_weights, sib, nxt, own_message
    )
    from_e = lax.ppermute(send_w, "face", [((i + 1) % faces, i) for i in range(faces)])
    from_w = lax.ppermute(send_e, "face", [(i, (i + 1) % faces) for i in range(faces)])
    flux, sib, nxt = flux_stencil(level_weights, level_sum, courant, sib, nxt)
    edges = (own_sums, halo_sums, own_coef, halo_coef, from_w, from_e)
    message, *edges = send_blocks(routes, flux, halo_strip, edges, offsets, tiles)
    halo_strip, from_w, from_e, strip_coef = edges
    message = exchange(message, CHUNK)
    ocean_flux, back = ocean_surface(message, ocean_state, mixing, land_mask)
    back = exchange(back, BACK)
    ocean_inputs = (ocean_flux, ocean_state, mixing, land_mask)
    edges = (own_strip, halo_strip, strip_coef, from_w, from_e)
    air_state, ocean_out = air_steps(atmos_state, *ocean_inputs, courant, sib, nxt, *edges)
    atmos_surface = return_blocks(routes, back, remap_tiles)
    return air_state, ocean_out, atmos_surface


def solution(mesh):
    return jax.shard_map(
        shards,
        mesh=mesh,
        in_specs=(
            P(None, None, "tile", "face"),
            P(None, "tile", "face"),
            P(),
            P(("face", "tile"), None, None),
            P(("face", "tile"), None),
            P(("face", "tile"), None, None),
            P(("face", "tile"), None),
            P(("face", "tile"), None),
            P(None, None, "face", "tile"),
            P("face", "tile"),
            P("face", "tile"),
        ),
        out_specs=(
            P(None, None, "tile", "face"),
            P(None, None, "face", "tile"),
            P(None, "tile", "face"),
        ),
        check_vma=False,
    )
```

```python
import jax
import jax.numpy as jnp
from jax import lax
from jax.experimental import pallas as pl
from jax.experimental.pallas import tpu as pltpu
from jax.sharding import PartitionSpec as P

STEPS = 3
FIELDS, LEVELS, ROWS, COLS, BLK = 4, 8, 24, 768, 128
MESSAGE = 112
ENTRIES, DEVICES, CAP, OCEAN_ROWS = 288, 128, 5, 64
CHUNK = 22
BACK = CAP * FIELDS
HALF = 208
f32, bf16 = jnp.float32, jnp.bfloat16


def iota(shape, dim):
    return lax.broadcasted_iota(jnp.int32, shape, dim)


def roll(x, shift, axis):
    shift = shift % x.shape[axis]
    return pltpu.roll(x, shift, axis) if shift else x


def params(mib=16):
    return pltpu.CompilerParams(vmem_limit_bytes=mib << 20)


in_vmem = pl.BlockSpec(memory_space=pltpu.VMEM)
in_hbm = pl.BlockSpec(memory_space=pltpu.HBM)


def hbm(*arrays):
    return [pltpu.with_memory_space_constraint(x, pltpu.HBM) for x in arrays]


def start_all(pairs, sems):
    copies = [pltpu.make_async_copy(a, b, sems.at[i]) for i, (a, b) in enumerate(pairs)]
    for copy in copies:
        copy.start()
    return copies


def wait_all(copies):
    for copy in copies:
        copy.wait()


def start_tiles(stored, tiles, sems, bounds):
    parts = [pl.ds(a, b - a) for a, b in zip(bounds, bounds[1:])]
    pairs = [(stored.at[part], tiles.at[part]) for part in parts]
    return dict(zip(bounds, start_all(pairs, sems)))


def row_kernel(air, cour, sib_ref, nxt_ref, top, bot, top_cour, bot_cour, sems):
    pairs = [(cour.at[:, pl.ds(0, 8), :], top_cour), (cour.at[:, pl.ds(16, 8), :], bot_cour)]
    for c in range(COLS // BLK):
        lanes = pl.ds(c * BLK, BLK)
        pairs.append((air.at[:, :, pl.ds(0, 8), lanes], top.at[c]))
        pairs.append((air.at[:, :, pl.ds(16, 8), lanes], bot.at[c]))
    copies = start_all(pairs, sems)

    def pack_numbers(out, at_top):
        first, numbers = (0, top_cour) if at_top else (5, bot_cour)
        sub = iota((8, COLS), 0)
        pair = jnp.where(sub < 4, roll(numbers[0], -first, 0), roll(numbers[1], 4 - first, 0))
        last = jnp.where(sub < 4, roll(numbers[2], -first, 0), 0.0)
        out[96:112, :] = jnp.concatenate([pair, last], 0).astype(bf16)

    def pack(out, at_top, c):
        first, rows = (0, top) if at_top else (5, bot)
        flat = rows.at[c].reshape(FIELDS * LEVELS * 8, BLK)

        def tile(i):
            return flat[pl.ds(i // 3 * 64 + first + i % 3, LEVELS, stride=8), :]

        for i in range(0, FIELDS * 3, 2):
            both = jnp.concatenate([tile(i), tile(i + 1)], 0)
            out[i * 8 : i * 8 + 16, c * BLK : (c + 1) * BLK] = both.astype(bf16)

    def send(to_top, to_bot):
        wait_all(copies[:2])
        pack_numbers(to_top, True)
        pack_numbers(to_bot, False)
        for c in range(COLS // BLK):
            wait_all(copies[2 * c + 2 : 2 * c + 4])
            pack(to_top, True, c)
            pack(to_bot, False, c)

    odd = lax.axis_index("tile") % 2

    @pl.when(odd == 1)
    def _():
        send(sib_ref, nxt_ref)

    @pl.when(odd == 0)
    def _():
        send(nxt_ref, sib_ref)


def row_messages(air, courant):
    shape = jax.ShapeDtypeStruct((MESSAGE, COLS), bf16)
    return pl.pallas_call(
        row_kernel,
        out_shape=(shape, shape),
        in_specs=[in_hbm] * 2,
        out_specs=(in_vmem,) * 2,
        scratch_shapes=[pltpu.VMEM((COLS // BLK, FIELDS, LEVELS, 8, BLK), f32)] * 2
        + [pltpu.VMEM((3, 8, COLS), f32)] * 2
        + [pltpu.SemaphoreType.DMA((14,))],
        compiler_params=params(),
        cost_estimate=pl.CostEstimate(flops=400000, bytes_accessed=2000000, transcendentals=0),
        name="row_messages",
    )(*hbm(air, courant))


def courant_rows(north, south, k):
    base = k // 2 * 8
    n, s = north[base : base + 8], south[base : base + 8]
    sub = iota(n.shape, 0)
    if k % 2:
        return jnp.where(sub < 3, roll(n, 4, 0), roll(s, 1, 0))
    return jnp.where(sub < 3, n, roll(s, 5, 0))


def halo_sum(scale, f, north, south):
    sub = iota((8, north.shape[1]), 0)
    weight = jnp.concatenate([scale[f]] * (north.shape[1] // BLK), 1)
    rows = jnp.zeros(sub.shape, f32)
    for j in range(3):
        at = slice((f * 3 + j) * 8, (f * 3 + j + 1) * 8)
        rows = jnp.where(sub == j, jnp.sum(north[at] * weight, axis=0, keepdims=True), rows)
        rows = jnp.where(sub == 5 + j, jnp.sum(south[at] * weight, axis=0, keepdims=True), rows)
    return rows


def north_south(sib, nxt):
    odd = lax.axis_index("tile") % 2 == 1
    a, b = sib.astype(f32), nxt.astype(f32)
    return jnp.where(odd, b, a), jnp.where(odd, a, b)


SHIFTS = (3, 6)


def edge_lanes(side):
    return slice(0, BLK) if side == 0 else slice(COLS - BLK, COLS)


def own_columns(side, rows):
    lane = iota((rows, 128), 1)
    return lane < 6 if side == 0 else lane >= 122


def gather_levels(level, shift):
    total = roll(level(0), shift, 1)
    for l in range(1, LEVELS):
        total = total + roll(level(l), l * 16 + shift, 1)
    return total


def spread(x):
    for s in (16, 32, 64):
        x = x + roll(x, s, 1)
    return x


def message_rows(strips, coefs, sums):
    lane = iota(strips[0].shape, 1)
    place = lane % 16
    middle = (place >= 3) & (place < 6)
    message = jnp.zeros(strips[0].shape, f32)
    for f in range(FIELDS):
        message = message + roll(jnp.where(middle, strips[f], 0.0), 3 * f - 3, 1)
    for k in range(3):
        mine = middle & (lane // 16 == k)
        message = message + roll(jnp.where(mine, coefs[k], 0.0), 9, 1)
    return message + roll(jnp.where(middle & (lane < 64), sums, 0.0), 57, 1)


def level_lanes(weights, f, rows):
    lane = iota((rows, 128), 1) // 16
    scale = jnp.zeros((rows, 128), f32)
    for l in range(LEVELS):
        scale = jnp.where(lane == l, weights[f, l], scale)
    return scale


def sum_strip(weights, strips):
    rows = strips[0].shape[0]
    group = iota((rows, 128), 1) // 16
    total = jnp.zeros((rows, 128), f32)
    for f in range(FIELDS):
        whole = spread(strips[f] * level_lanes(weights, f, rows))
        total = jnp.where(group == f, whole, total)
    return total


def route(src, owner, offset, tile_index, routes, offsets):
    row = lambda ref: ref[...].astype(f32)
    sub = iota((8, ENTRIES), 0)
    known = jnp.where(sub == 0, row(src), jnp.where(sub == 1, row(owner), row(offset))).astype(bf16)
    pick = (iota((ENTRIES, ENTRIES), 0) == tile_index[...]).astype(f32).astype(bf16)
    along = (((1,), (1,)), ((), ()))
    by_tile = lax.dot_general(known, pick, along, preferred_element_type=f32)
    down = lax.dot_general(pick, known, along, preferred_element_type=f32)
    source, dest, place = by_tile[0:1], by_tile[1:2], by_tile[2:3]
    earlier = iota((ENTRIES, ENTRIES), 0) < iota((ENTRIES, ENTRIES), 1)
    same = jnp.where(earlier & (down[:, 1:2] == dest), 1.0, 0.0)
    rank = jnp.sum(same, axis=0, keepdims=True)
    numbers = jnp.where(
        sub == 0,
        source * FIELDS,
        jnp.where(sub == 1, dest * CHUNK + rank * FIELDS, dest * BACK + rank * FIELDS),
    )
    routes[...] = numbers.astype(jnp.int32)
    device = iota((DEVICES, ENTRIES), 0).astype(f32)
    to_dest = (device == dest).astype(f32).astype(bf16)
    at_rank = jnp.where(device == rank, place + 1.0, 0.0).astype(bf16)
    offsets[...] = lax.dot_general(to_dest, at_rank, along, preferred_element_type=f32) - 1.0


def own_kernel(*refs):
    given, made, refs = refs[:8], refs[8:18], refs[18:]
    strip_out, coef, message, sums, level_sum, scale, numbers, routes, offsets, tiles = made
    here, (strip, sems) = refs[:7], refs[7:]
    half = given[7].at[pl.ds(0, HALF)]
    copies = start_all(zip((*given[:7], half), (*here, tiles)), sems)
    wait_all(copies[:5])
    route(*here[1:5], routes, offsets)
    weights, (air, cour) = here[0], here[5:7]
    for f in range(FIELDS):
        total = jnp.zeros((8, BLK), f32)
        for l in range(LEVELS):
            total = jnp.where(iota((8, BLK), 0) == l, weights[f, l], total)
        scale[f] = total
    wait_all(copies[5:7])
    for k in range(3):
        numbers[k] = cour[k]
    for side in range(2):
        lanes, own, shift = edge_lanes(side), own_columns(side, ROWS), SHIFTS[side]
        strips, coefs = [], []
        for f in range(FIELDS):
            level = lambda l: jnp.where(own, air[f, l, :, lanes], 0.0)
            strips.append(gather_levels(level, shift))
            strip[side, f] = strips[f]
        for k in range(3):
            coefs.append(spread(roll(jnp.where(own, cour[k, :, lanes], 0.0), shift, 1)))
            coef[side, k] = coefs[k]
        sums[side] = sum_strip(weights, strips)
        message[side] = message_rows(strips, coefs, sums[side])
    copy = pltpu.make_async_copy(strip, strip_out, sems.at[8])
    copy.start()
    for f in range(FIELDS):
        total = weights[f, 0] * air[f, 0]
        for l in range(1, LEVELS):
            total = total + weights[f, l] * air[f, l]
        level_sum[f] = total
    copy.wait()
    copies[7].wait()


def own_parts(*given):
    return pl.pallas_call(
        own_kernel,
        out_shape=(
            pltpu.HBM((2, FIELDS, ROWS, 128), f32),
            jax.ShapeDtypeStruct((2, 3, ROWS, 128), f32),
            jax.ShapeDtypeStruct((2, ROWS, 128), f32),
            jax.ShapeDtypeStruct((2, ROWS, 128), f32),
            jax.ShapeDtypeStruct((FIELDS, ROWS, COLS), f32),
            jax.ShapeDtypeStruct((FIELDS, 8, BLK), f32),
            jax.ShapeDtypeStruct((3, ROWS, COLS), f32),
            jax.ShapeDtypeStruct((8, ENTRIES), jnp.int32),
            jax.ShapeDtypeStruct((DEVICES, 128), f32),
            pltpu.VMEM((HALF, BLK, BLK), bf16),
        ),
        in_specs=[in_hbm] * 8,
        out_specs=(in_hbm,) + (in_vmem,) * 9,
        scratch_shapes=[pltpu.SMEM(given[0].shape, f32)]
        + [pltpu.VMEM(x.shape, x.dtype) for x in given[1:7]]
        + [pltpu.VMEM((2, FIELDS, ROWS, 128), f32), pltpu.SemaphoreType.DMA((9,))],
        compiler_params=params(),
        cost_estimate=pl.CostEstimate(flops=1600000, bytes_accessed=1200000, transcendentals=0),
        name="own_parts",
    )(*hbm(*given))


def halo_kernel(scale, sib, nxt, own_message, strip, coef, sums, send_w, send_e, halo):
    for side, send in enumerate((send_w, send_e)):
        lanes, own, shift = edge_lanes(side), own_columns(side, 8), SHIFTS[side]
        north, south = north_south(sib[:, lanes], nxt[:, lanes])
        for f in range(FIELDS):
            for j in range(3):
                at = f * 64 + j * 8
                halo[side, at : at + 8, :] = north[(f * 3 + j) * 8 : (f * 3 + j + 1) * 8]
                halo[side, at + 40 : at + 48, :] = south[(f * 3 + j) * 8 : (f * 3 + j + 1) * 8]
            halo[side, f * 64 + 24 : f * 64 + 40, :] = jnp.zeros((16, BLK), f32)
        strips, coefs = [], []
        for f in range(FIELDS):
            level = lambda l: jnp.where(own, halo[side, pl.ds(f * 64 + l, 8, stride=8), :], 0.0)
            strips.append(gather_levels(level, shift))
            strip[side, f] = strips[f]
        for k in range(3):
            rows = courant_rows(north[96:112], south[96:112], k)
            coefs.append(spread(roll(jnp.where(own, rows, 0.0), shift, 1)))
            coef[side, k] = coefs[k]
        total = jnp.zeros((8, BLK), f32)
        for f in range(FIELDS):
            rows = jnp.where(own, halo_sum(scale, f, north, south), 0.0)
            total = total + roll(rows, f * 16 + shift, 1)
        sums[side] = total
        send[:ROWS] = own_message[side]
        send[ROWS:] = message_rows(strips, coefs, sums[side])


def column_messages(scale, sib, nxt, own_message):
    message = jax.ShapeDtypeStruct((32, 128), f32)
    return pl.pallas_call(
        halo_kernel,
        out_shape=(
            jax.ShapeDtypeStruct((2, FIELDS, 8, 128), f32),
            jax.ShapeDtypeStruct((2, 3, 8, 128), f32),
            jax.ShapeDtypeStruct((2, 8, 128), f32),
            message,
            message,
        ),
        in_specs=[in_vmem] * 4,
        out_specs=(in_vmem,) * 5,
        scratch_shapes=[pltpu.VMEM((2, FIELDS * 64, BLK), f32)],
        compiler_params=params(),
        cost_estimate=pl.CostEstimate(flops=100000, bytes_accessed=400000, transcendentals=0),
        name="column_messages",
    )(scale, sib, nxt, own_message)


def received(side, got):
    lane = iota((32, 128), 1)
    place, group = lane % 16, lane // 16
    first = 0 if side == 0 else 6
    here = (place >= first) & (place < first + 3)
    spare = (place >= 12) & (place < 15)
    numbers = [
        spread(roll(jnp.where((group == k) & spare, got, 0.0), first - 12, 1)) for k in range(3)
    ]
    return here, numbers, roll(got, first - 60, 1)


def coefficients(cx, cy, kd):
    return 1.0 - cx - cy - 4.0 * kd, cx + kd, cy + kd, kd


def step(q, c):
    return (
        q * c[0]
        + roll(q, 1, 1) * c[1]
        + roll(q, 1, 0) * c[2]
        + (roll(q, -1, 1) + roll(q, -1, 0)) * c[3]
    )


def level_weight(weights, f, shape):
    scale = jnp.zeros(shape, f32)
    for l in range(LEVELS):
        scale = jnp.where(iota(shape, 0) == l, weights[f, l], scale)
    return scale


def flux_kernel(scale, level_sum, cour, sib, nxt, stored, flux, sib_out, nxt_out, tiles, sems):
    half = stored.at[pl.ds(HALF, ENTRIES - HALF)]
    copies = start_all([(half, tiles), (sib, sib_out), (nxt, nxt_out)], sems)
    north, south = north_south(sib[...], nxt[...])
    three = [
        jnp.concatenate([cour[k], courant_rows(north[96:], south[96:], k)], 0) for k in range(3)
    ]
    coefs = coefficients(*three)
    for f in range(FIELDS):
        rows = halo_sum(scale, f, north, south)
        q = jnp.concatenate([level_sum[f], rows], 0)
        for _ in range(STEPS):
            q = step(q, coefs)
        q = q[:ROWS].astype(bf16).astype(f32)
        for c in range(COLS // BLK):
            flux[pl.ds(c * FIELDS + f, ROWS, stride=24), :] = q[:, c * BLK : (c + 1) * BLK]
    wait_all(copies)


def flux_stencil(scale, level_sum, courant, sib, nxt, tiles):
    return pl.pallas_call(
        flux_kernel,
        out_shape=(
            jax.ShapeDtypeStruct((ROWS * 24, BLK), f32),
            pltpu.HBM(sib.shape, bf16),
            pltpu.HBM(nxt.shape, bf16),
            pltpu.VMEM((ENTRIES - HALF, BLK, BLK), bf16),
        ),
        in_specs=[in_vmem] * 5 + [in_hbm],
        out_specs=(in_vmem, in_hbm, in_hbm, in_vmem),
        scratch_shapes=[pltpu.SemaphoreType.DMA((3,))],
        compiler_params=params(),
        cost_estimate=pl.CostEstimate(flops=3000000, bytes_accessed=1000000, transcendentals=0),
        name="flux_stencil",
    )(scale, level_sum, courant, sib, nxt, *hbm(tiles))


def advance(c, q, below, above):
    return q * c[0] + roll(q, 1, 1) * c[1] + below * c[2] + (roll(q, -1, 1) + above) * c[3]


def sweep(coef, starts, done, emits):
    for r in range(-3, ROWS + 3):
        for start, d in zip(starts, done):
            d[0][r] = start(r)
        for s in range(3):
            at = r - 1 - s
            if s - 2 <= at < ROWS + 2 - s:
                c = [coef[k, at % 32 : at % 32 + 1, :] for k in range(4)]
                for d in done:
                    d[s + 1][at] = advance(c, d[s][at], d[s][at - 1], d[s][at + 1])
                if s == 2:
                    for emit, d in zip(emits, done):
                        emit(at, d[3][at])


def air_kernel(air, *refs):
    given, (out, ocean_out, *here), refs = refs[:12], refs[12:26], refs[26:]
    into, done, halo, coef, levels, in_sems, out_sems, sems = refs
    flux, ocean, mixing, mask, cour, sib, nxt, own_strip, halo_strip, strip_coef, from_w, from_e = here
    parts = COLS // BLK

    def copy_in(f, c):
        source = air.at[f, :, :, pl.ds(c * BLK, BLK)]
        return pltpu.make_async_copy(source, into.at[f, c], in_sems.at[f, c])

    def copy_out(f, c):
        target = out.at[f, :, :, pl.ds(c * BLK, BLK)]
        return pltpu.make_async_copy(done.at[f, c], target, out_sems.at[f, c])

    small = start_all(zip(given, here), sems)
    for f in range(FIELDS):
        for c in range(parts):
            copy_in(f, c).start()
    wait_all(small)
    ocean_copy = pltpu.make_async_copy(levels, ocean_out, sems.at[12])
    ocean_levels(flux, ocean, mixing, mask, levels)
    ocean_copy.start()
    north, south = north_south(sib[...], nxt[...])
    halo[0] = south[:96]
    halo[1] = north[:96]
    three = [
        jnp.concatenate([cour[k], courant_rows(north[96:], south[96:], k)], 0) for k in range(3)
    ]
    for k, c in enumerate(coefficients(*three)):
        coef[k] = c
    edges = []
    for side, got in enumerate((from_w, from_e)):
        here, _, _ = received(side, got[...])
        numbers = coefficients(*(strip_coef[side, k] for k in range(3)))
        first = 0 if side == 0 else 6
        for f in range(FIELDS):
            mine = jnp.concatenate([own_strip[side, f], halo_strip[side, f]], 0)
            q = jnp.where(here, roll(got[...], first - 3 * f, 1), mine)
            for _ in range(STEPS):
                q = step(q, numbers)
            edges.append(q[:ROWS])

    def starter(f):
        flat = [into.at[f, c].reshape(LEVELS * ROWS, BLK) for c in range(parts)]

        def start(r):
            if r < 0:
                return halo[0, f * 24 + (r + 3) * 8 : f * 24 + (r + 4) * 8, :]
            if r >= ROWS:
                return halo[1, f * 24 + (r - ROWS) * 8 : f * 24 + (r - ROWS + 1) * 8, :]
            return jnp.concatenate([x[pl.ds(r, LEVELS, stride=ROWS), :] for x in flat], 1)

        return start

    def emitter(f):
        flat = [done.at[f, c].reshape(LEVELS * ROWS, BLK) for c in range(parts)]

        def emit(r, q):
            for c in range(parts):
                flat[c][pl.ds(r, LEVELS, stride=ROWS), :] = q[:, c * BLK : (c + 1) * BLK]

        return emit

    column = iota((ROWS, 128), 1)
    for fields in ((0, 1), (2, 3)):
        for f in fields:
            for c in range(parts):
                copy_in(f, c).wait()
        sweep(
            coef,
            [starter(f) for f in fields],
            [[{}, {}, {}, {}] for f in fields],
            [emitter(f) for f in fields],
        )
        for f in fields:
            for c in range(1, parts - 1):
                copy_out(f, c).start()
            for l in range(LEVELS):
                west, east = roll(edges[f], -l * 16 - 3, 1), roll(edges[FIELDS + f], 122 - l * 16, 1)
                done[f, 0, l] = jnp.where(column < 3, west, done[f, 0, l])
                done[f, parts - 1, l] = jnp.where(column >= 125, east, done[f, parts - 1, l])
            copy_out(f, 0).start()
            copy_out(f, parts - 1).start()
    for f in range(FIELDS):
        for c in range(parts):
            copy_out(f, c).wait()
    ocean_copy.wait()


def ocean_levels(flux, ocean, mixing, mask, out):
    wet = mask[...].astype(f32)
    mix = wet * mixing[...]
    for f in range(FIELDS):
        q = [ocean[f, l] for l in range(8)]
        q[0] = q[0] + wet * flux[f]
        for l in range(8):
            out[f, l] = q[l] + mix * (q[max(l - 1, 0)] + q[min(l + 1, 7)] - 2.0 * q[l])


def air_steps(air, *given):
    parts = COLS // BLK
    return pl.pallas_call(
        air_kernel,
        out_shape=(pltpu.HBM(air.shape, f32), pltpu.HBM(given[1].shape, f32)),
        in_specs=[in_hbm] * 13,
        out_specs=(in_hbm, in_hbm),
        scratch_shapes=[pltpu.VMEM(x.shape, x.dtype) for x in given]
        + [
            pltpu.VMEM((FIELDS, parts, LEVELS, ROWS, BLK), f32),
            pltpu.VMEM((FIELDS, parts, LEVELS, ROWS, BLK), f32),
            pltpu.VMEM((2, 96, COLS), f32),
            pltpu.VMEM((4, 32, COLS), f32),
            pltpu.VMEM(given[1].shape, f32),
            pltpu.SemaphoreType.DMA((FIELDS, parts)),
            pltpu.SemaphoreType.DMA((FIELDS, parts)),
            pltpu.SemaphoreType.DMA((13,)),
        ],
        compiler_params=params(),
        cost_estimate=pl.CostEstimate(flops=30000000, bytes_accessed=6000000, transcendentals=0),
        name="air_steps",
    )(*hbm(air, *given))


def fix_edges(own_sums, halo_sums, own_coef, halo_coef, from_w, from_e, coef_out, flux):
    lane = iota((32, 128), 1)
    column = iota((ROWS, 128), 1)
    for side, got in enumerate((from_w, from_e)):
        here, numbers, sums = received(side, got[...])
        three = []
        for k in range(3):
            mine = jnp.concatenate([own_coef[side, k], halo_coef[side, k]], 0)
            three.append(jnp.where(here, numbers[k], mine))
            coef_out[side, k] = three[k]
        coefs = coefficients(*three)
        mine = jnp.concatenate([own_sums[side], halo_sums[side]], 0)
        q = jnp.where(here & (lane < 64), sums, mine)
        for _ in range(STEPS):
            q = step(q, coefs)
        q = q[:ROWS].astype(bf16).astype(f32)
        for f in range(FIELDS):
            at = pl.ds(8 + f + (0 if side == 0 else 20), ROWS, stride=24)
            if side == 0:
                flux[at, :] = jnp.where(column < 3, roll(q, -f * 16 - 3, 1), flux[at, :])
            else:
                flux[at, :] = jnp.where(column >= 125, roll(q, 122 - f * 16, 1), flux[at, :])


def block_rows(ref, at, low):
    half = iota((8, BLK), 0) < 4
    if low:
        return jnp.where(half, ref[pl.ds(at + 8, 8), :], 0.0)
    return jnp.where(half, 0.0, ref[pl.ds(at + 4, 8), :])


def four_rows(ref, at):
    left = jnp.concatenate([block_rows(ref, at[0], True), block_rows(ref, at[2], True)], 0)
    right = jnp.concatenate([block_rows(ref, at[1], False), block_rows(ref, at[3], False)], 0)
    return jnp.concatenate([left, right], 1).astype(bf16)


def four_results(r):
    return r[0:4, :BLK], r[4:8, :BLK], r[8:12, BLK:], r[12:16, BLK:]


def send_kernel(routes, flux_in, halo_strip, *refs):
    edges, (offsets, early, late, out, *kept, flux, total, coef, numbers, sems) = refs[:6], refs[6:]
    listed = pltpu.make_async_copy(routes, numbers, sems.at[4])
    listed.start()
    copies = start_all(zip((halo_strip, *edges[4:6]), kept), sems)
    flux[0:8, :] = jnp.zeros((8, BLK), f32)
    flux[8 : 8 + ROWS * 24, :] = flux_in[...]
    flux[8 + ROWS * 24 :, :] = jnp.zeros((8, BLK), f32)
    fix_edges(*edges, coef, flux)
    copies.append(pltpu.make_async_copy(coef, kept[3], sems.at[3]))
    copies[3].start()
    total[...] = jnp.zeros(total.shape, f32)
    total[pl.ds(BACK, DEVICES, stride=CHUNK), :] = offsets[...]
    listed.wait()
    for t in range(0, ENTRIES, 4):
        at = [numbers[0, t + i] for i in range(4)]
        tiles, u = (early, t) if t < HALF else (late, t - HALF)
        w = jnp.concatenate(
            [
                jnp.concatenate([tiles[u], tiles[u + 1]], 0),
                jnp.concatenate([tiles[u + 2], tiles[u + 3]], 0),
            ],
            1,
        )
        r = jnp.dot(four_rows(flux, at), w, preferred_element_type=f32)
        for i, piece in enumerate(four_results(r)):
            total[pl.ds(numbers[1, t + i], 4), :] = piece
    out[...] = total[...].astype(bf16)
    wait_all(copies)


def send_blocks(routes, flux, halo_strip, edges, offsets, early, late):
    return pl.pallas_call(
        send_kernel,
        out_shape=(
            jax.ShapeDtypeStruct((DEVICES * CHUNK, BLK), bf16),
            pltpu.HBM(halo_strip.shape, f32),
            pltpu.HBM((32, 128), f32),
            pltpu.HBM((32, 128), f32),
            pltpu.HBM((2, 3, 32, 128), f32),
        ),
        in_specs=[in_vmem] * 12,
        out_specs=(in_vmem,) + (in_hbm,) * 4,
        scratch_shapes=[
            pltpu.VMEM((ROWS * 24 + 16, BLK), f32),
            pltpu.VMEM((DEVICES * CHUNK, BLK), f32),
            pltpu.VMEM((2, 3, 32, 128), f32),
            pltpu.SMEM((8, ENTRIES), jnp.int32),
            pltpu.SemaphoreType.DMA((5,)),
        ],
        compiler_params=params(),
        cost_estimate=pl.CostEstimate(flops=40000000, bytes_accessed=11000000, transcendentals=0),
        name="send_blocks",
    )(routes, flux, halo_strip, *edges, offsets, early, late)


def ocean_kernel(payload, ocean, mixing, mask, flux_out, back, got, ret, packed, kept, sems):
    got[...] = payload[...].astype(f32)
    offsets = got[pl.ds(BACK, DEVICES, stride=CHUNK), :]
    by_slot = offsets.T
    blocks = iota((OCEAN_ROWS, DEVICES), 0).astype(f32)
    flux = None
    for j in range(CAP):
        place = (by_slot[j : j + 1, :] == blocks).astype(f32).astype(bf16)
        data = jnp.concatenate(
            [got[pl.ds(j * FIELDS + f, DEVICES, stride=CHUNK), :] for f in range(FIELDS)], 1
        ).astype(bf16)
        part = jnp.dot(place, data, preferred_element_type=f32)
        flux = part if j == 0 else flux + part
    wet = mask[...].astype(f32)
    mix = wet * mixing[...]
    surface = []
    for f in range(FIELDS):
        piece = flux[:, f * BLK : (f + 1) * BLK]
        kept[f] = piece
        top, below = ocean[f, 0] + wet * piece, ocean[f, 1]
        new = top + mix * (top + below - 2.0 * top)
        surface.append((wet * new).astype(bf16))
    copies = [pltpu.make_async_copy(kept, flux_out, sems.at[0])]
    copies[0].start()
    surface = jnp.concatenate(surface, 1)
    half = DEVICES // 2
    lanes = iota((half, OCEAN_ROWS), 1).astype(f32)
    for h in range(2):
        mine = offsets[h * half : (h + 1) * half]
        for j in range(CAP):
            pick = (mine[:, j : j + 1] == lanes).astype(f32).astype(bf16)
            rows = jnp.dot(pick, surface, preferred_element_type=f32)
            for f in range(FIELDS):
                at = pl.ds(h * half * BACK + j * FIELDS + f, half, stride=BACK)
                ret[at, :] = rows[:, f * BLK : (f + 1) * BLK]
        at = pl.ds(h * half * BACK, half * BACK)
        packed[at, :] = ret[at, :].astype(bf16)
        copies.append(pltpu.make_async_copy(packed.at[at], back.at[at], sems.at[1 + h]))
        copies[1 + h].start()
    wait_all(copies)


def ocean_surface(payload, ocean, mixing, mask):
    return pl.pallas_call(
        ocean_kernel,
        out_shape=(
            pltpu.HBM((FIELDS, OCEAN_ROWS, BLK), f32),
            pltpu.HBM((DEVICES * BACK, BLK), bf16),
        ),
        in_specs=[in_vmem] * 4,
        out_specs=(in_hbm, in_hbm),
        scratch_shapes=[
            pltpu.VMEM((DEVICES * CHUNK, BLK), f32),
            pltpu.VMEM((DEVICES * BACK, BLK), f32),
            pltpu.VMEM((DEVICES * BACK, BLK), bf16),
            pltpu.VMEM((FIELDS, OCEAN_ROWS, BLK), f32),
            pltpu.SemaphoreType.DMA((3,)),
        ],
        compiler_params=params(),
        cost_estimate=pl.CostEstimate(flops=100000000, bytes_accessed=4000000, transcendentals=0),
        name="ocean_surface",
    )(payload, ocean, mixing, mask)


PARTS = (0, 16, 56, 104, 160, 224, ENTRIES)


def return_kernel(routes, payload, stored, out, got, total, numbers, tiles, done, sems):
    listed = start_all([(routes, numbers)], sems)[0]
    waits = start_tiles(stored, tiles, sems.at[pl.ds(1, 6)], PARTS)
    got[0:8, :] = jnp.zeros((8, BLK), f32)
    got[8 : 8 + DEVICES * BACK, :] = payload[...].astype(f32)
    got[8 + DEVICES * BACK :, :] = jnp.zeros((8, BLK), f32)
    total[...] = jnp.zeros(total.shape, f32)
    listed.wait()
    for t in range(0, ENTRIES, 4):
        if t in waits:
            waits[t].wait()
        at = [numbers[2, t + i] for i in range(4)]
        w = jnp.concatenate(
            [
                jnp.concatenate([tiles[t], tiles[t + 1]], 1),
                jnp.concatenate([tiles[t + 2], tiles[t + 3]], 1),
            ],
            0,
        )
        r = lax.dot_general(
            four_rows(got, at), w, (((1,), (1,)), ((), ())), preferred_element_type=f32
        )
        for i, piece in enumerate(four_results(r)):
            here = pl.ds(numbers[0, t + i], 4)
            total[here, :] = total[here, :] + piece
    copies = []
    for f in range(FIELDS):
        for c in range(COLS // BLK):
            done[f, :, c * BLK : (c + 1) * BLK] = total[pl.ds(c * FIELDS + f, ROWS, stride=24), :]
        copies.append(pltpu.make_async_copy(done.at[f], out.at[f], sems.at[7 + f]))
        copies[f].start()
    wait_all(copies)


def return_blocks(routes, payload, tiles):
    return pl.pallas_call(
        return_kernel,
        out_shape=pltpu.HBM((FIELDS, ROWS, COLS), f32),
        in_specs=[in_vmem, in_vmem, in_hbm],
        out_specs=in_hbm,
        scratch_shapes=[
            pltpu.VMEM((DEVICES * BACK + 16, BLK), f32),
            pltpu.VMEM((ROWS * 24, BLK), f32),
            pltpu.SMEM((8, ENTRIES), jnp.int32),
            pltpu.VMEM((ENTRIES, BLK, BLK), bf16),
            pltpu.VMEM((FIELDS, ROWS, COLS), f32),
            pltpu.SemaphoreType.DMA((11,)),
        ],
        compiler_params=params(24),
        cost_estimate=pl.CostEstimate(flops=40000000, bytes_accessed=11000000, transcendentals=0),
        name="return_blocks",
    )(routes, payload, *hbm(tiles))


def exchange(x, rows):
    x = x.reshape(DEVICES * CAP, rows // CAP, BLK) if rows == BACK else x.reshape(-1, 2, BLK)
    x = lax.all_to_all(x, ("face", "tile"), split_axis=0, concat_axis=0, tiled=True)
    return x.reshape(DEVICES * rows, BLK)


def shards(
    atmos_state,
    courant,
    level_weights,
    remap_tiles,
    src_block,
    owner,
    offset,
    tile_index,
    ocean_state,
    mixing,
    land_mask,
):
    faces, tile_count = lax.axis_size("face"), lax.axis_size("tile")
    sib, nxt = row_messages(atmos_state, courant)
    inner = [(i, i + 1) for i in range(1, tile_count - 1, 2)]
    nxt = lax.ppermute(nxt, "tile", inner + [(b, a) for a, b in inner])
    sib = lax.ppermute(sib, "tile", [(i, i ^ 1) for i in range(tile_count)])
    own_strip, own_coef, own_message, own_sums, level_sum, scale, numbers, *rest = own_parts(
        *(level_weights, src_block, owner.reshape(1, -1), offset, tile_index),
        *(atmos_state, courant, remap_tiles),
    )
    routes, offsets, early = rest
    halo_strip, halo_coef, halo_sums, send_w, send_e = column_messages(
        scale, sib, nxt, own_message
    )
    from_e = lax.ppermute(send_w, "face", [((i + 1) % faces, i) for i in range(faces)])
    from_w = lax.ppermute(send_e, "face", [(i, (i + 1) % faces) for i in range(faces)])
    flux, sib, nxt, late = flux_stencil(scale, level_sum, numbers, sib, nxt, remap_tiles)
    edges = (own_sums, halo_sums, own_coef, halo_coef, from_w, from_e)
    message, *edges = send_blocks(
        routes, flux, halo_strip, edges, offsets, early, late
    )
    halo_strip, from_w, from_e, strip_coef = edges
    message = exchange(message, CHUNK)
    ocean_flux, back = ocean_surface(message, ocean_state, mixing, land_mask)
    back = exchange(back, BACK)
    ocean_inputs = (ocean_flux, ocean_state, mixing, land_mask)
    edges = (own_strip, halo_strip, strip_coef, from_w, from_e)
    air_state, ocean_out = air_steps(atmos_state, *ocean_inputs, courant, sib, nxt, *edges)
    atmos_surface = return_blocks(routes, back, remap_tiles)
    return air_state, ocean_out, atmos_surface


def solution(mesh):
    return jax.shard_map(
        shards,
        mesh=mesh,
        in_specs=(
            P(None, None, "tile", "face"),
            P(None, "tile", "face"),
            P(),
            P(("face", "tile"), None, None),
            P(("face", "tile"), None),
            P(("face", "tile"), None, None),
            P(("face", "tile"), None),
            P(("face", "tile"), None),
            P(None, None, "face", "tile"),
            P("face", "tile"),
            P("face", "tile"),
        ),
        out_specs=(
            P(None, None, "tile", "face"),
            P(None, None, "face", "tile"),
            P(None, "tile", "face"),
        ),
        check_vma=False,
    )
```

```python
import jax
import jax.numpy as jnp
from jax import lax
from jax.experimental import pallas as pl
from jax.experimental.pallas import tpu as pltpu
from jax.sharding import PartitionSpec as P

STEPS = 3
FIELDS, LEVELS, ROWS, COLS, BLK = 4, 8, 24, 768, 128
MESSAGE = 112
ENTRIES, DEVICES, CAP, OCEAN_ROWS = 288, 128, 5, 64
CHUNK = 22
BACK = CAP * FIELDS
HALF = 208
f32, bf16 = jnp.float32, jnp.bfloat16


def iota(shape, dim):
    return lax.broadcasted_iota(jnp.int32, shape, dim)


def roll(x, shift, axis):
    shift = shift % x.shape[axis]
    return pltpu.roll(x, shift, axis) if shift else x


def params(mib=16):
    return pltpu.CompilerParams(vmem_limit_bytes=mib << 20)


in_vmem = pl.BlockSpec(memory_space=pltpu.VMEM)
in_hbm = pl.BlockSpec(memory_space=pltpu.HBM)


def hbm(*arrays):
    return [pltpu.with_memory_space_constraint(x, pltpu.HBM) for x in arrays]


def start_all(pairs, sems):
    copies = [pltpu.make_async_copy(a, b, sems.at[i]) for i, (a, b) in enumerate(pairs)]
    for copy in copies:
        copy.start()
    return copies


def wait_all(copies):
    for copy in copies:
        copy.wait()


def start_tiles(stored, tiles, sems, bounds):
    parts = [pl.ds(a, b - a) for a, b in zip(bounds, bounds[1:])]
    pairs = [(stored.at[part], tiles.at[part]) for part in parts]
    return dict(zip(bounds, start_all(pairs, sems)))


def row_kernel(air, cour, nxt_ref, sib_ref, top, bot, top_cour, bot_cour, sems):
    pairs = [(cour.at[:, pl.ds(0, 8), :], top_cour), (cour.at[:, pl.ds(16, 8), :], bot_cour)]
    for c in range(COLS // BLK):
        lanes = pl.ds(c * BLK, BLK)
        pairs.append((air.at[:, :, pl.ds(0, 4), lanes], top.at[c]))
        pairs.append((air.at[:, :, pl.ds(20, 4), lanes], bot.at[c]))
    copies = start_all(pairs, sems)

    def pack_numbers(out, at_top):
        first, numbers = (0, top_cour) if at_top else (5, bot_cour)
        sub = iota((8, COLS), 0)
        pair = jnp.where(sub < 4, roll(numbers[0], -first, 0), roll(numbers[1], 4 - first, 0))
        last = jnp.where(sub < 4, roll(numbers[2], -first, 0), 0.0)
        out[96:112, :] = jnp.concatenate([pair, last], 0).astype(bf16)

    def pack(out, at_top, c):
        first, rows = (0, top) if at_top else (1, bot)
        flat = rows.at[c].reshape(FIELDS * LEVELS * 4, BLK)

        def tile(i):
            return flat[pl.ds(i // 3 * 32 + first + i % 3, LEVELS, stride=4), :]

        for i in range(0, FIELDS * 3, 2):
            both = jnp.concatenate([tile(i), tile(i + 1)], 0)
            out[i * 8 : i * 8 + 16, c * BLK : (c + 1) * BLK] = both.astype(bf16)

    def send(to_top, to_bot):
        wait_all(copies[:2])
        pack_numbers(to_top, True)
        pack_numbers(to_bot, False)
        for c in range(COLS // BLK):
            wait_all(copies[2 * c + 2 : 2 * c + 4])
            pack(to_top, True, c)
            pack(to_bot, False, c)

    odd = lax.axis_index("tile") % 2

    @pl.when(odd == 1)
    def _():
        send(sib_ref, nxt_ref)

    @pl.when(odd == 0)
    def _():
        send(nxt_ref, sib_ref)


def row_messages(air, courant):
    shape = jax.ShapeDtypeStruct((MESSAGE, COLS), bf16)
    return pl.pallas_call(
        row_kernel,
        out_shape=(shape, shape),
        in_specs=[in_hbm] * 2,
        out_specs=(in_vmem,) * 2,
        scratch_shapes=[pltpu.VMEM((COLS // BLK, FIELDS, LEVELS, 4, BLK), f32)] * 2
        + [pltpu.VMEM((3, 8, COLS), f32)] * 2
        + [pltpu.SemaphoreType.DMA((14,))],
        compiler_params=params(),
        cost_estimate=pl.CostEstimate(flops=400000, bytes_accessed=2000000, transcendentals=0),
        name="row_messages",
    )(*hbm(air, courant))


def courant_rows(north, south, k):
    base = k // 2 * 8
    n, s = north[base : base + 8], south[base : base + 8]
    sub = iota(n.shape, 0)
    if k % 2:
        return jnp.where(sub < 3, roll(n, 4, 0), roll(s, 1, 0))
    return jnp.where(sub < 3, n, roll(s, 5, 0))


def halo_sum(scale, f, north, south):
    sub = iota((8, north.shape[1]), 0)
    weight = jnp.concatenate([scale[f]] * (north.shape[1] // BLK), 1)
    rows = jnp.zeros(sub.shape, f32)
    for j in range(3):
        at = slice((f * 3 + j) * 8, (f * 3 + j + 1) * 8)
        rows = jnp.where(sub == j, jnp.sum(north[at] * weight, axis=0, keepdims=True), rows)
        rows = jnp.where(sub == 5 + j, jnp.sum(south[at] * weight, axis=0, keepdims=True), rows)
    return rows


def north_south(sib, nxt):
    odd = lax.axis_index("tile") % 2 == 1
    a, b = sib.astype(f32), nxt.astype(f32)
    return jnp.where(odd, b, a), jnp.where(odd, a, b)


SHIFTS = (3, 6)


def edge_lanes(side):
    return slice(0, BLK) if side == 0 else slice(COLS - BLK, COLS)


def own_columns(side, rows):
    lane = iota((rows, 128), 1)
    return lane < 6 if side == 0 else lane >= 122


def gather_levels(level, shift):
    total = roll(level(0), shift, 1)
    for l in range(1, LEVELS):
        total = total + roll(level(l), l * 16 + shift, 1)
    return total


def spread(x):
    for s in (16, 32, 64):
        x = x + roll(x, s, 1)
    return x


def message_rows(strips, coefs, sums):
    lane = iota(strips[0].shape, 1)
    place = lane % 16
    middle = (place >= 3) & (place < 6)
    message = jnp.zeros(strips[0].shape, f32)
    for f in range(FIELDS):
        message = message + roll(jnp.where(middle, strips[f], 0.0), 3 * f - 3, 1)
    for k in range(3):
        mine = middle & (lane // 16 == k)
        message = message + roll(jnp.where(mine, coefs[k], 0.0), 9, 1)
    return message + roll(jnp.where(middle & (lane < 64), sums, 0.0), 57, 1)


def level_lanes(weights, f, rows):
    lane = iota((rows, 128), 1) // 16
    scale = jnp.zeros((rows, 128), f32)
    for l in range(LEVELS):
        scale = jnp.where(lane == l, weights[f, l], scale)
    return scale


def sum_strip(weights, strips):
    rows = strips[0].shape[0]
    group = iota((rows, 128), 1) // 16
    total = jnp.zeros((rows, 128), f32)
    for f in range(FIELDS):
        whole = spread(strips[f] * level_lanes(weights, f, rows))
        total = jnp.where(group == f, whole, total)
    return total


def route(src, owner, offset, tile_index, routes, offsets):
    row = lambda ref: ref[...].astype(f32)
    sub = iota((8, ENTRIES), 0)
    known = jnp.where(sub == 0, row(src), jnp.where(sub == 1, row(owner), row(offset))).astype(bf16)
    pick = (iota((ENTRIES, ENTRIES), 0) == tile_index[...]).astype(f32).astype(bf16)
    along = (((1,), (1,)), ((), ()))
    by_tile = lax.dot_general(known, pick, along, preferred_element_type=f32)
    down = lax.dot_general(pick, known, along, preferred_element_type=f32)
    source, dest, place = by_tile[0:1], by_tile[1:2], by_tile[2:3]
    earlier = iota((ENTRIES, ENTRIES), 0) < iota((ENTRIES, ENTRIES), 1)
    same = jnp.where(earlier & (down[:, 1:2] == dest), 1.0, 0.0)
    rank = jnp.sum(same, axis=0, keepdims=True)
    numbers = jnp.where(
        sub == 0,
        source * FIELDS,
        jnp.where(sub == 1, dest * CHUNK + rank * FIELDS, dest * BACK + rank * FIELDS),
    )
    routes[...] = numbers.astype(jnp.int32)
    device = iota((DEVICES, ENTRIES), 0).astype(f32)
    to_dest = (device == dest).astype(f32).astype(bf16)
    at_rank = jnp.where(device == rank, place + 1.0, 0.0).astype(bf16)
    offsets[...] = lax.dot_general(to_dest, at_rank, along, preferred_element_type=f32) - 1.0


def own_kernel(*refs):
    given, made, refs = refs[:8], refs[8:18], refs[18:]
    strip_out, coef, message, sums, level_sum, scale, numbers, routes, offsets, tiles = made
    here, (strip, sems) = refs[:7], refs[7:]
    half = given[7].at[pl.ds(0, HALF)]
    copies = start_all(zip((*given[:7], half), (*here, tiles)), sems)
    wait_all(copies[:5])
    route(*here[1:5], routes, offsets)
    weights, (air, cour) = here[0], here[5:7]
    for f in range(FIELDS):
        total = jnp.zeros((8, BLK), f32)
        for l in range(LEVELS):
            total = jnp.where(iota((8, BLK), 0) == l, weights[f, l], total)
        scale[f] = total
    wait_all(copies[5:7])
    for k in range(3):
        numbers[k] = cour[k]
    for side in range(2):
        lanes, own, shift = edge_lanes(side), own_columns(side, ROWS), SHIFTS[side]
        strips, coefs = [], []
        for f in range(FIELDS):
            level = lambda l: jnp.where(own, air[f, l, :, lanes], 0.0)
            strips.append(gather_levels(level, shift))
            strip[side, f] = strips[f]
        for k in range(3):
            coefs.append(spread(roll(jnp.where(own, cour[k, :, lanes], 0.0), shift, 1)))
            coef[side, k] = coefs[k]
        sums[side] = sum_strip(weights, strips)
        message[side] = message_rows(strips, coefs, sums[side])
    copy = pltpu.make_async_copy(strip, strip_out, sems.at[8])
    copy.start()
    for f in range(FIELDS):
        total = weights[f, 0] * air[f, 0]
        for l in range(1, LEVELS):
            total = total + weights[f, l] * air[f, l]
        level_sum[f] = total
    copy.wait()
    copies[7].wait()


def own_parts(*given):
    return pl.pallas_call(
        own_kernel,
        out_shape=(
            pltpu.HBM((2, FIELDS, ROWS, 128), f32),
            jax.ShapeDtypeStruct((2, 3, ROWS, 128), f32),
            jax.ShapeDtypeStruct((2, ROWS, 128), f32),
            jax.ShapeDtypeStruct((2, ROWS, 128), f32),
            jax.ShapeDtypeStruct((FIELDS, ROWS, COLS), f32),
            jax.ShapeDtypeStruct((FIELDS, 8, BLK), f32),
            jax.ShapeDtypeStruct((3, ROWS, COLS), f32),
            jax.ShapeDtypeStruct((8, ENTRIES), jnp.int32),
            jax.ShapeDtypeStruct((DEVICES, 128), f32),
            pltpu.VMEM((HALF, BLK, BLK), bf16),
        ),
        in_specs=[in_hbm] * 8,
        out_specs=(in_hbm,) + (in_vmem,) * 9,
        scratch_shapes=[pltpu.SMEM(given[0].shape, f32)]
        + [pltpu.VMEM(x.shape, x.dtype) for x in given[1:7]]
        + [pltpu.VMEM((2, FIELDS, ROWS, 128), f32), pltpu.SemaphoreType.DMA((9,))],
        compiler_params=params(),
        cost_estimate=pl.CostEstimate(flops=1600000, bytes_accessed=1200000, transcendentals=0),
        name="own_parts",
    )(*hbm(*given))


def halo_kernel(scale, nxt, sib, own_message, strip, coef, sums, send_w, send_e, halo):
    for side, send in enumerate((send_w, send_e)):
        lanes, own, shift = edge_lanes(side), own_columns(side, 8), SHIFTS[side]
        north, south = north_south(sib[:, lanes], nxt[:, lanes])
        for f in range(FIELDS):
            for j in range(3):
                at = f * 64 + j * 8
                halo[side, at : at + 8, :] = north[(f * 3 + j) * 8 : (f * 3 + j + 1) * 8]
                halo[side, at + 40 : at + 48, :] = south[(f * 3 + j) * 8 : (f * 3 + j + 1) * 8]
            halo[side, f * 64 + 24 : f * 64 + 40, :] = jnp.zeros((16, BLK), f32)
        strips, coefs = [], []
        for f in range(FIELDS):
            level = lambda l: jnp.where(own, halo[side, pl.ds(f * 64 + l, 8, stride=8), :], 0.0)
            strips.append(gather_levels(level, shift))
            strip[side, f] = strips[f]
        for k in range(3):
            rows = courant_rows(north[96:112], south[96:112], k)
            coefs.append(spread(roll(jnp.where(own, rows, 0.0), shift, 1)))
            coef[side, k] = coefs[k]
        total = jnp.zeros((8, BLK), f32)
        for f in range(FIELDS):
            rows = jnp.where(own, halo_sum(scale, f, north, south), 0.0)
            total = total + roll(rows, f * 16 + shift, 1)
        sums[side] = total
        send[:ROWS] = own_message[side]
        send[ROWS:] = message_rows(strips, coefs, sums[side])


def column_messages(scale, nxt, sib, own_message):
    message = jax.ShapeDtypeStruct((32, 128), f32)
    return pl.pallas_call(
        halo_kernel,
        out_shape=(
            jax.ShapeDtypeStruct((2, FIELDS, 8, 128), f32),
            jax.ShapeDtypeStruct((2, 3, 8, 128), f32),
            jax.ShapeDtypeStruct((2, 8, 128), f32),
            message,
            message,
        ),
        in_specs=[in_vmem] * 4,
        out_specs=(in_vmem,) * 5,
        scratch_shapes=[pltpu.VMEM((2, FIELDS * 64, BLK), f32)],
        compiler_params=params(),
        cost_estimate=pl.CostEstimate(flops=100000, bytes_accessed=400000, transcendentals=0),
        name="column_messages",
    )(scale, nxt, sib, own_message)


def received(side, got):
    lane = iota((32, 128), 1)
    place, group = lane % 16, lane // 16
    first = 0 if side == 0 else 6
    here = (place >= first) & (place < first + 3)
    spare = (place >= 12) & (place < 15)
    numbers = [
        spread(roll(jnp.where((group == k) & spare, got, 0.0), first - 12, 1)) for k in range(3)
    ]
    return here, numbers, roll(got, first - 60, 1)


def coefficients(cx, cy, kd):
    return 1.0 - cx - cy - 4.0 * kd, cx + kd, cy + kd, kd


def step(q, c):
    return (
        q * c[0]
        + roll(q, 1, 1) * c[1]
        + roll(q, 1, 0) * c[2]
        + (roll(q, -1, 1) + roll(q, -1, 0)) * c[3]
    )


def level_weight(weights, f, shape):
    scale = jnp.zeros(shape, f32)
    for l in range(LEVELS):
        scale = jnp.where(iota(shape, 0) == l, weights[f, l], scale)
    return scale


def flux_kernel(scale, level_sum, cour, nxt, sib, stored, flux, nxt_out, sib_out, tiles, sems):
    half = stored.at[pl.ds(HALF, ENTRIES - HALF)]
    copies = start_all([(half, tiles), (sib, sib_out), (nxt, nxt_out)], sems)
    north, south = north_south(sib[...], nxt[...])
    three = [
        jnp.concatenate([cour[k], courant_rows(north[96:], south[96:], k)], 0) for k in range(3)
    ]
    coefs = coefficients(*three)
    for f in range(FIELDS):
        rows = halo_sum(scale, f, north, south)
        q = jnp.concatenate([level_sum[f], rows], 0)
        for _ in range(STEPS):
            q = step(q, coefs)
        q = q[:ROWS].astype(bf16).astype(f32)
        for c in range(COLS // BLK):
            flux[pl.ds(c * FIELDS + f, ROWS, stride=24), :] = q[:, c * BLK : (c + 1) * BLK]
    wait_all(copies)


def flux_stencil(scale, level_sum, courant, nxt, sib, tiles):
    return pl.pallas_call(
        flux_kernel,
        out_shape=(
            jax.ShapeDtypeStruct((ROWS * 24, BLK), f32),
            pltpu.HBM(nxt.shape, bf16),
            pltpu.HBM(sib.shape, bf16),
            pltpu.VMEM((ENTRIES - HALF, BLK, BLK), bf16),
        ),
        in_specs=[in_vmem] * 5 + [in_hbm],
        out_specs=(in_vmem, in_hbm, in_hbm, in_vmem),
        scratch_shapes=[pltpu.SemaphoreType.DMA((3,))],
        compiler_params=params(),
        cost_estimate=pl.CostEstimate(flops=3000000, bytes_accessed=1000000, transcendentals=0),
        name="flux_stencil",
    )(scale, level_sum, courant, nxt, sib, *hbm(tiles))


def advance(c, q, below, above):
    return q * c[0] + roll(q, 1, 1) * c[1] + below * c[2] + (roll(q, -1, 1) + above) * c[3]


def sweep(coef, starts, done, emits):
    for r in range(-3, ROWS + 3):
        for start, d in zip(starts, done):
            d[0][r] = start(r)
        for s in range(3):
            at = r - 1 - s
            if s - 2 <= at < ROWS + 2 - s:
                c = [coef[k, at % 32 : at % 32 + 1, :] for k in range(4)]
                for d in done:
                    d[s + 1][at] = advance(c, d[s][at], d[s][at - 1], d[s][at + 1])
                if s == 2:
                    for emit, d in zip(emits, done):
                        emit(at, d[3][at])


def air_kernel(air, *refs):
    given, (out, ocean_out, *here), refs = refs[:12], refs[12:26], refs[26:]
    into, done, halo, coef, levels, in_sems, out_sems, sems = refs
    flux, ocean, mixing, mask, cour, sib, nxt, own_strip, halo_strip, strip_coef, from_w, from_e = here
    parts = COLS // BLK

    def copy_in(f, c):
        source = air.at[f, :, :, pl.ds(c * BLK, BLK)]
        return pltpu.make_async_copy(source, into.at[f, c], in_sems.at[f, c])

    def copy_out(f, c):
        target = out.at[f, :, :, pl.ds(c * BLK, BLK)]
        return pltpu.make_async_copy(done.at[f, c], target, out_sems.at[f, c])

    small = start_all(zip(given, here), sems)
    for f in range(FIELDS):
        for c in range(parts):
            copy_in(f, c).start()
    wait_all(small)
    ocean_copy = pltpu.make_async_copy(levels, ocean_out, sems.at[12])
    ocean_levels(flux, ocean, mixing, mask, levels)
    ocean_copy.start()
    north, south = north_south(sib[...], nxt[...])
    halo[0] = south[:96]
    halo[1] = north[:96]
    three = [
        jnp.concatenate([cour[k], courant_rows(north[96:], south[96:], k)], 0) for k in range(3)
    ]
    for k, c in enumerate(coefficients(*three)):
        coef[k] = c
    edges = []
    for side, got in enumerate((from_w, from_e)):
        here, _, _ = received(side, got[...])
        numbers = coefficients(*(strip_coef[side, k] for k in range(3)))
        first = 0 if side == 0 else 6
        for f in range(FIELDS):
            mine = jnp.concatenate([own_strip[side, f], halo_strip[side, f]], 0)
            q = jnp.where(here, roll(got[...], first - 3 * f, 1), mine)
            for _ in range(STEPS):
                q = step(q, numbers)
            edges.append(q[:ROWS])

    def starter(f):
        flat = [into.at[f, c].reshape(LEVELS * ROWS, BLK) for c in range(parts)]

        def start(r):
            if r < 0:
                return halo[0, f * 24 + (r + 3) * 8 : f * 24 + (r + 4) * 8, :]
            if r >= ROWS:
                return halo[1, f * 24 + (r - ROWS) * 8 : f * 24 + (r - ROWS + 1) * 8, :]
            return jnp.concatenate([x[pl.ds(r, LEVELS, stride=ROWS), :] for x in flat], 1)

        return start

    def emitter(f):
        flat = [done.at[f, c].reshape(LEVELS * ROWS, BLK) for c in range(parts)]

        def emit(r, q):
            for c in range(parts):
                flat[c][pl.ds(r, LEVELS, stride=ROWS), :] = q[:, c * BLK : (c + 1) * BLK]

        return emit

    column = iota((ROWS, 128), 1)
    for fields in ((0, 1), (2, 3)):
        for f in fields:
            for c in range(parts):
                copy_in(f, c).wait()
        sweep(
            coef,
            [starter(f) for f in fields],
            [[{}, {}, {}, {}] for f in fields],
            [emitter(f) for f in fields],
        )
        for f in fields:
            for c in range(1, parts - 1):
                copy_out(f, c).start()
            for l in range(LEVELS):
                west, east = roll(edges[f], -l * 16 - 3, 1), roll(edges[FIELDS + f], 122 - l * 16, 1)
                done[f, 0, l] = jnp.where(column < 3, west, done[f, 0, l])
                done[f, parts - 1, l] = jnp.where(column >= 125, east, done[f, parts - 1, l])
            copy_out(f, 0).start()
            copy_out(f, parts - 1).start()
    for f in range(FIELDS):
        for c in range(parts):
            copy_out(f, c).wait()
    ocean_copy.wait()


def ocean_levels(flux, ocean, mixing, mask, out):
    wet = mask[...].astype(f32)
    mix = wet * mixing[...]
    for f in range(FIELDS):
        q = [ocean[f, l] for l in range(8)]
        q[0] = q[0] + wet * flux[f]
        for l in range(8):
            out[f, l] = q[l] + mix * (q[max(l - 1, 0)] + q[min(l + 1, 7)] - 2.0 * q[l])


def air_steps(air, *given):
    parts = COLS // BLK
    return pl.pallas_call(
        air_kernel,
        out_shape=(pltpu.HBM(air.shape, f32), pltpu.HBM(given[1].shape, f32)),
        in_specs=[in_hbm] * 13,
        out_specs=(in_hbm, in_hbm),
        scratch_shapes=[pltpu.VMEM(x.shape, x.dtype) for x in given]
        + [
            pltpu.VMEM((FIELDS, parts, LEVELS, ROWS, BLK), f32),
            pltpu.VMEM((FIELDS, parts, LEVELS, ROWS, BLK), f32),
            pltpu.VMEM((2, 96, COLS), f32),
            pltpu.VMEM((4, 32, COLS), f32),
            pltpu.VMEM(given[1].shape, f32),
            pltpu.SemaphoreType.DMA((FIELDS, parts)),
            pltpu.SemaphoreType.DMA((FIELDS, parts)),
            pltpu.SemaphoreType.DMA((13,)),
        ],
        compiler_params=params(),
        cost_estimate=pl.CostEstimate(flops=30000000, bytes_accessed=6000000, transcendentals=0),
        name="air_steps",
    )(*hbm(air, *given))


def fix_edges(own_sums, halo_sums, own_coef, halo_coef, from_w, from_e, coef_out, flux):
    lane = iota((32, 128), 1)
    column = iota((ROWS, 128), 1)
    for side, got in enumerate((from_w, from_e)):
        here, numbers, sums = received(side, got[...])
        three = []
        for k in range(3):
            mine = jnp.concatenate([own_coef[side, k], halo_coef[side, k]], 0)
            three.append(jnp.where(here, numbers[k], mine))
            coef_out[side, k] = three[k]
        coefs = coefficients(*three)
        mine = jnp.concatenate([own_sums[side], halo_sums[side]], 0)
        q = jnp.where(here & (lane < 64), sums, mine)
        for _ in range(STEPS):
            q = step(q, coefs)
        q = q[:ROWS].astype(bf16).astype(f32)
        for f in range(FIELDS):
            at = pl.ds(8 + f + (0 if side == 0 else 20), ROWS, stride=24)
            if side == 0:
                flux[at, :] = jnp.where(column < 3, roll(q, -f * 16 - 3, 1), flux[at, :])
            else:
                flux[at, :] = jnp.where(column >= 125, roll(q, 122 - f * 16, 1), flux[at, :])


def block_rows(ref, at, low):
    half = iota((8, BLK), 0) < 4
    if low:
        return jnp.where(half, ref[pl.ds(at + 8, 8), :], 0.0)
    return jnp.where(half, 0.0, ref[pl.ds(at + 4, 8), :])


def four_rows(ref, at):
    left = jnp.concatenate([block_rows(ref, at[0], True), block_rows(ref, at[2], True)], 0)
    right = jnp.concatenate([block_rows(ref, at[1], False), block_rows(ref, at[3], False)], 0)
    return jnp.concatenate([left, right], 1).astype(bf16)


def four_results(r):
    return r[0:4, :BLK], r[4:8, :BLK], r[8:12, BLK:], r[12:16, BLK:]


def send_kernel(routes, flux_in, halo_strip, *refs):
    edges, (offsets, early, late, out, *kept, flux, total, coef, numbers, sems) = refs[:6], refs[6:]
    listed = pltpu.make_async_copy(routes, numbers, sems.at[4])
    listed.start()
    copies = start_all(zip((halo_strip, *edges[4:6]), kept), sems)
    flux[0:8, :] = jnp.zeros((8, BLK), f32)
    flux[8 : 8 + ROWS * 24, :] = flux_in[...]
    flux[8 + ROWS * 24 :, :] = jnp.zeros((8, BLK), f32)
    fix_edges(*edges, coef, flux)
    copies.append(pltpu.make_async_copy(coef, kept[3], sems.at[3]))
    copies[3].start()
    total[...] = jnp.zeros(total.shape, f32)
    total[pl.ds(BACK, DEVICES, stride=CHUNK), :] = offsets[...]
    listed.wait()
    for t in range(0, ENTRIES, 4):
        at = [numbers[0, t + i] for i in range(4)]
        tiles, u = (early, t) if t < HALF else (late, t - HALF)
        w = jnp.concatenate(
            [
                jnp.concatenate([tiles[u], tiles[u + 1]], 0),
                jnp.concatenate([tiles[u + 2], tiles[u + 3]], 0),
            ],
            1,
        )
        r = jnp.dot(four_rows(flux, at), w, preferred_element_type=f32)
        for i, piece in enumerate(four_results(r)):
            total[pl.ds(numbers[1, t + i], 4), :] = piece
    out[...] = total[...].astype(bf16)
    wait_all(copies)


def send_blocks(routes, flux, halo_strip, edges, offsets, early, late):
    return pl.pallas_call(
        send_kernel,
        out_shape=(
            jax.ShapeDtypeStruct((DEVICES * CHUNK, BLK), bf16),
            pltpu.HBM(halo_strip.shape, f32),
            pltpu.HBM((32, 128), f32),
            pltpu.HBM((32, 128), f32),
            pltpu.HBM((2, 3, 32, 128), f32),
        ),
        in_specs=[in_vmem] * 12,
        out_specs=(in_vmem,) + (in_hbm,) * 4,
        scratch_shapes=[
            pltpu.VMEM((ROWS * 24 + 16, BLK), f32),
            pltpu.VMEM((DEVICES * CHUNK, BLK), f32),
            pltpu.VMEM((2, 3, 32, 128), f32),
            pltpu.SMEM((8, ENTRIES), jnp.int32),
            pltpu.SemaphoreType.DMA((5,)),
        ],
        compiler_params=params(),
        cost_estimate=pl.CostEstimate(flops=40000000, bytes_accessed=11000000, transcendentals=0),
        name="send_blocks",
    )(routes, flux, halo_strip, *edges, offsets, early, late)


def ocean_kernel(payload, ocean, mixing, mask, flux_out, back, got, ret, packed, kept, sems):
    got[...] = payload[...].astype(f32)
    offsets = got[pl.ds(BACK, DEVICES, stride=CHUNK), :]
    by_slot = offsets.T
    blocks = iota((OCEAN_ROWS, DEVICES), 0).astype(f32)
    flux = None
    for j in range(CAP):
        place = (by_slot[j : j + 1, :] == blocks).astype(f32).astype(bf16)
        data = jnp.concatenate(
            [got[pl.ds(j * FIELDS + f, DEVICES, stride=CHUNK), :] for f in range(FIELDS)], 1
        ).astype(bf16)
        part = jnp.dot(place, data, preferred_element_type=f32)
        flux = part if j == 0 else flux + part
    wet = mask[...].astype(f32)
    mix = wet * mixing[...]
    surface = []
    for f in range(FIELDS):
        piece = flux[:, f * BLK : (f + 1) * BLK]
        kept[f] = piece
        top, below = ocean[f, 0] + wet * piece, ocean[f, 1]
        new = top + mix * (top + below - 2.0 * top)
        surface.append((wet * new).astype(bf16))
    copies = [pltpu.make_async_copy(kept, flux_out, sems.at[0])]
    copies[0].start()
    surface = jnp.concatenate(surface, 1)
    half = DEVICES // 4
    lanes = iota((half, OCEAN_ROWS), 1).astype(f32)
    for h in range(4):
        mine = offsets[h * half : (h + 1) * half]
        for j in range(CAP):
            pick = (mine[:, j : j + 1] == lanes).astype(f32).astype(bf16)
            rows = jnp.dot(pick, surface, preferred_element_type=f32)
            for f in range(FIELDS):
                at = pl.ds(h * half * BACK + j * FIELDS + f, half, stride=BACK)
                ret[at, :] = rows[:, f * BLK : (f + 1) * BLK]
        at = pl.ds(h * half * BACK, half * BACK)
        packed[at, :] = ret[at, :].astype(bf16)
        copies.append(pltpu.make_async_copy(packed.at[at], back.at[at], sems.at[1 + h]))
        copies[1 + h].start()
    wait_all(copies)


def ocean_surface(payload, ocean, mixing, mask):
    return pl.pallas_call(
        ocean_kernel,
        out_shape=(
            pltpu.HBM((FIELDS, OCEAN_ROWS, BLK), f32),
            pltpu.HBM((DEVICES * BACK, BLK), bf16),
        ),
        in_specs=[in_vmem] * 4,
        out_specs=(in_hbm, in_hbm),
        scratch_shapes=[
            pltpu.VMEM((DEVICES * CHUNK, BLK), f32),
            pltpu.VMEM((DEVICES * BACK, BLK), f32),
            pltpu.VMEM((DEVICES * BACK, BLK), bf16),
            pltpu.VMEM((FIELDS, OCEAN_ROWS, BLK), f32),
            pltpu.SemaphoreType.DMA((5,)),
        ],
        compiler_params=params(),
        cost_estimate=pl.CostEstimate(flops=100000000, bytes_accessed=4000000, transcendentals=0),
        name="ocean_surface",
    )(payload, ocean, mixing, mask)


PARTS = (0, 16, 56, 104, 160, 224, ENTRIES)


def return_kernel(routes, payload, stored, out, got, total, numbers, tiles, done, sems):
    listed = start_all([(routes, numbers)], sems)[0]
    waits = start_tiles(stored, tiles, sems.at[pl.ds(1, 6)], PARTS)
    got[0:8, :] = jnp.zeros((8, BLK), f32)
    got[8 : 8 + DEVICES * BACK, :] = payload[...].astype(f32)
    got[8 + DEVICES * BACK :, :] = jnp.zeros((8, BLK), f32)
    total[...] = jnp.zeros(total.shape, f32)
    listed.wait()
    for t in range(0, ENTRIES, 4):
        if t in waits:
            waits[t].wait()
        at = [numbers[2, t + i] for i in range(4)]
        w = jnp.concatenate(
            [
                jnp.concatenate([tiles[t], tiles[t + 1]], 1),
                jnp.concatenate([tiles[t + 2], tiles[t + 3]], 1),
            ],
            0,
        )
        r = lax.dot_general(
            four_rows(got, at), w, (((1,), (1,)), ((), ())), preferred_element_type=f32
        )
        for i, piece in enumerate(four_results(r)):
            here = pl.ds(numbers[0, t + i], 4)
            total[here, :] = total[here, :] + piece
    copies = []
    for f in range(FIELDS):
        for c in range(COLS // BLK):
            done[f, :, c * BLK : (c + 1) * BLK] = total[pl.ds(c * FIELDS + f, ROWS, stride=24), :]
        copies.append(pltpu.make_async_copy(done.at[f], out.at[f], sems.at[7 + f]))
        copies[f].start()
    wait_all(copies)


def return_blocks(routes, payload, tiles):
    return pl.pallas_call(
        return_kernel,
        out_shape=pltpu.HBM((FIELDS, ROWS, COLS), f32),
        in_specs=[in_vmem, in_vmem, in_hbm],
        out_specs=in_hbm,
        scratch_shapes=[
            pltpu.VMEM((DEVICES * BACK + 16, BLK), f32),
            pltpu.VMEM((ROWS * 24, BLK), f32),
            pltpu.SMEM((8, ENTRIES), jnp.int32),
            pltpu.VMEM((ENTRIES, BLK, BLK), bf16),
            pltpu.VMEM((FIELDS, ROWS, COLS), f32),
            pltpu.SemaphoreType.DMA((11,)),
        ],
        compiler_params=params(24),
        cost_estimate=pl.CostEstimate(flops=40000000, bytes_accessed=11000000, transcendentals=0),
        name="return_blocks",
    )(routes, payload, *hbm(tiles))


def exchange(x, rows):
    x = x.reshape(DEVICES * CAP, rows // CAP, BLK) if rows == BACK else x.reshape(-1, 2, BLK)
    x = lax.all_to_all(x, ("face", "tile"), split_axis=0, concat_axis=0, tiled=True)
    return x.reshape(DEVICES * rows, BLK)


def shards(
    atmos_state,
    courant,
    level_weights,
    remap_tiles,
    src_block,
    owner,
    offset,
    tile_index,
    ocean_state,
    mixing,
    land_mask,
):
    faces, tile_count = lax.axis_size("face"), lax.axis_size("tile")
    nxt, sib = row_messages(atmos_state, courant)
    inner = [(i, i + 1) for i in range(1, tile_count - 1, 2)]
    nxt = lax.ppermute(nxt, "tile", inner + [(b, a) for a, b in inner])
    sib = lax.ppermute(sib, "tile", [(i, i ^ 1) for i in range(tile_count)])
    own_strip, own_coef, own_message, own_sums, level_sum, scale, numbers, *rest = own_parts(
        *(level_weights, src_block, owner.reshape(1, -1), offset, tile_index),
        *(atmos_state, courant, remap_tiles),
    )
    routes, offsets, early = rest
    halo_strip, halo_coef, halo_sums, send_w, send_e = column_messages(
        scale, nxt, sib, own_message
    )
    from_e = lax.ppermute(send_w, "face", [((i + 1) % faces, i) for i in range(faces)])
    from_w = lax.ppermute(send_e, "face", [(i, (i + 1) % faces) for i in range(faces)])
    flux, nxt, sib, late = flux_stencil(scale, level_sum, numbers, nxt, sib, remap_tiles)
    edges = (own_sums, halo_sums, own_coef, halo_coef, from_w, from_e)
    message, *edges = send_blocks(
        routes, flux, halo_strip, edges, offsets, early, late
    )
    halo_strip, from_w, from_e, strip_coef = edges
    message = exchange(message, CHUNK)
    ocean_flux, back = ocean_surface(message, ocean_state, mixing, land_mask)
    back = exchange(back, BACK)
    ocean_inputs = (ocean_flux, ocean_state, mixing, land_mask)
    edges = (own_strip, halo_strip, strip_coef, from_w, from_e)
    air_state, ocean_out = air_steps(atmos_state, *ocean_inputs, courant, sib, nxt, *edges)
    atmos_surface = return_blocks(routes, back, remap_tiles)
    return air_state, ocean_out, atmos_surface


def solution(mesh):
    return jax.shard_map(
        shards,
        mesh=mesh,
        in_specs=(
            P(None, None, "tile", "face"),
            P(None, "tile", "face"),
            P(),
            P(("face", "tile"), None, None),
            P(("face", "tile"), None),
            P(("face", "tile"), None, None),
            P(("face", "tile"), None),
            P(("face", "tile"), None),
            P(None, None, "face", "tile"),
            P("face", "tile"),
            P("face", "tile"),
        ),
        out_specs=(
            P(None, None, "tile", "face"),
            P(None, None, "face", "tile"),
            P(None, "tile", "face"),
        ),
        check_vma=False,
    )
```

```python
import jax
import jax.numpy as jnp
from jax import lax
from jax.experimental import pallas as pl
from jax.experimental.pallas import tpu as pltpu
from jax.sharding import PartitionSpec as P

STEPS = 3
FIELDS, LEVELS, ROWS, COLS, BLK = 4, 8, 24, 768, 128
MESSAGE = 112
ENTRIES, DEVICES, CAP, OCEAN_ROWS = 288, 128, 5, 64
CHUNK = 22
BACK = CAP * FIELDS
HALF = 208
f32, bf16 = jnp.float32, jnp.bfloat16


def iota(shape, dim):
    return lax.broadcasted_iota(jnp.int32, shape, dim)


def roll(x, shift, axis):
    shift = shift % x.shape[axis]
    return pltpu.roll(x, shift, axis) if shift else x


def params(mib=16):
    return pltpu.CompilerParams(vmem_limit_bytes=mib << 20)


in_vmem = pl.BlockSpec(memory_space=pltpu.VMEM)
in_hbm = pl.BlockSpec(memory_space=pltpu.HBM)


def hbm(*arrays):
    return [pltpu.with_memory_space_constraint(x, pltpu.HBM) for x in arrays]


def start_all(pairs, sems):
    copies = [pltpu.make_async_copy(a, b, sems.at[i]) for i, (a, b) in enumerate(pairs)]
    for copy in copies:
        copy.start()
    return copies


def wait_all(copies):
    for copy in copies:
        copy.wait()


def start_tiles(stored, tiles, sems, bounds):
    parts = [pl.ds(a, b - a) for a, b in zip(bounds, bounds[1:])]
    pairs = [(stored.at[part], tiles.at[part]) for part in parts]
    return dict(zip(bounds, start_all(pairs, sems)))


def row_kernel(air, cour, nxt_ref, sib_ref, top, bot, top_cour, bot_cour, sems):
    pairs = [(cour.at[:, pl.ds(0, 8), :], top_cour), (cour.at[:, pl.ds(16, 8), :], bot_cour)]
    for c in range(COLS // BLK):
        lanes = pl.ds(c * BLK, BLK)
        pairs.append((air.at[:, :, pl.ds(0, 4), lanes], top.at[c]))
        pairs.append((air.at[:, :, pl.ds(20, 4), lanes], bot.at[c]))
    copies = start_all(pairs, sems)

    def pack_numbers(out, at_top):
        first, numbers = (0, top_cour) if at_top else (5, bot_cour)
        sub = iota((8, COLS), 0)
        pair = jnp.where(sub < 4, roll(numbers[0], -first, 0), roll(numbers[1], 4 - first, 0))
        last = jnp.where(sub < 4, roll(numbers[2], -first, 0), 0.0)
        out[96:112, :] = jnp.concatenate([pair, last], 0).astype(bf16)

    def pack(out, at_top, c):
        first, rows = (0, top) if at_top else (1, bot)
        flat = rows.at[c].reshape(FIELDS * LEVELS * 4, BLK)

        def tile(i):
            return flat[pl.ds(i // 3 * 32 + first + i % 3, LEVELS, stride=4), :]

        for i in range(0, FIELDS * 3, 2):
            both = jnp.concatenate([tile(i), tile(i + 1)], 0)
            out[i * 8 : i * 8 + 16, c * BLK : (c + 1) * BLK] = both.astype(bf16)

    def send(to_top, to_bot):
        wait_all(copies[:2])
        pack_numbers(to_top, True)
        pack_numbers(to_bot, False)
        for c in range(COLS // BLK):
            wait_all(copies[2 * c + 2 : 2 * c + 4])
            pack(to_top, True, c)
            pack(to_bot, False, c)

    odd = lax.axis_index("tile") % 2

    @pl.when(odd == 1)
    def _():
        send(sib_ref, nxt_ref)

    @pl.when(odd == 0)
    def _():
        send(nxt_ref, sib_ref)


def row_messages(air, courant):
    shape = jax.ShapeDtypeStruct((MESSAGE, COLS), bf16)
    return pl.pallas_call(
        row_kernel,
        out_shape=(shape, shape),
        in_specs=[in_hbm] * 2,
        out_specs=(in_vmem,) * 2,
        scratch_shapes=[pltpu.VMEM((COLS // BLK, FIELDS, LEVELS, 4, BLK), f32)] * 2
        + [pltpu.VMEM((3, 8, COLS), f32)] * 2
        + [pltpu.SemaphoreType.DMA((14,))],
        compiler_params=params(),
        cost_estimate=pl.CostEstimate(flops=400000, bytes_accessed=2000000, transcendentals=0),
        name="row_messages",
    )(*hbm(air, courant))


def courant_rows(north, south, k):
    base = k // 2 * 8
    n, s = north[base : base + 8], south[base : base + 8]
    sub = iota(n.shape, 0)
    if k % 2:
        return jnp.where(sub < 3, roll(n, 4, 0), roll(s, 1, 0))
    return jnp.where(sub < 3, n, roll(s, 5, 0))


def halo_sum(scale, f, north, south):
    sub = iota((8, north.shape[1]), 0)
    weight = jnp.concatenate([scale[f]] * (north.shape[1] // BLK), 1)
    rows = jnp.zeros(sub.shape, f32)
    for j in range(3):
        at = slice((f * 3 + j) * 8, (f * 3 + j + 1) * 8)
        rows = jnp.where(sub == j, jnp.sum(north[at] * weight, axis=0, keepdims=True), rows)
        rows = jnp.where(sub == 5 + j, jnp.sum(south[at] * weight, axis=0, keepdims=True), rows)
    return rows


def north_south(sib, nxt):
    odd = lax.axis_index("tile") % 2 == 1
    a, b = sib.astype(f32), nxt.astype(f32)
    return jnp.where(odd, b, a), jnp.where(odd, a, b)


SHIFTS = (3, 6)


def edge_lanes(side):
    return slice(0, BLK) if side == 0 else slice(COLS - BLK, COLS)


def own_columns(side, rows):
    lane = iota((rows, 128), 1)
    return lane < 6 if side == 0 else lane >= 122


def gather_levels(level, shift):
    total = roll(level(0), shift, 1)
    for l in range(1, LEVELS):
        total = total + roll(level(l), l * 16 + shift, 1)
    return total


def spread(x):
    for s in (16, 32, 64):
        x = x + roll(x, s, 1)
    return x


def message_rows(strips, coefs, sums):
    lane = iota(strips[0].shape, 1)
    place = lane % 16
    middle = (place >= 3) & (place < 6)
    message = jnp.zeros(strips[0].shape, f32)
    for f in range(FIELDS):
        message = message + roll(jnp.where(middle, strips[f], 0.0), 3 * f - 3, 1)
    for k in range(3):
        mine = middle & (lane // 16 == k)
        message = message + roll(jnp.where(mine, coefs[k], 0.0), 9, 1)
    return message + roll(jnp.where(middle & (lane < 64), sums, 0.0), 57, 1)


def level_lanes(weights, f, rows):
    lane = iota((rows, 128), 1) // 16
    scale = jnp.zeros((rows, 128), f32)
    for l in range(LEVELS):
        scale = jnp.where(lane == l, weights[f, l], scale)
    return scale


def sum_strip(weights, strips):
    rows = strips[0].shape[0]
    group = iota((rows, 128), 1) // 16
    total = jnp.zeros((rows, 128), f32)
    for f in range(FIELDS):
        whole = spread(strips[f] * level_lanes(weights, f, rows))
        total = jnp.where(group == f, whole, total)
    return total


def route(src, owner, offset, tile_index, routes, offsets):
    row = lambda ref: ref[...].astype(f32)
    sub = iota((8, ENTRIES), 0)
    known = jnp.where(sub == 0, row(src), jnp.where(sub == 1, row(owner), row(offset))).astype(bf16)
    pick = (iota((ENTRIES, ENTRIES), 0) == tile_index[...]).astype(f32).astype(bf16)
    along = (((1,), (1,)), ((), ()))
    by_tile = lax.dot_general(known, pick, along, preferred_element_type=f32)
    down = lax.dot_general(pick, known, along, preferred_element_type=f32)
    source, dest, place = by_tile[0:1], by_tile[1:2], by_tile[2:3]
    earlier = iota((ENTRIES, ENTRIES), 0) < iota((ENTRIES, ENTRIES), 1)
    same = jnp.where(earlier & (down[:, 1:2] == dest), 1.0, 0.0)
    rank = jnp.sum(same, axis=0, keepdims=True)
    numbers = jnp.where(
        sub == 0,
        source * FIELDS,
        jnp.where(sub == 1, dest * CHUNK + rank * FIELDS, dest * BACK + rank * FIELDS),
    )
    routes[...] = numbers.astype(jnp.int32)
    device = iota((DEVICES, ENTRIES), 0).astype(f32)
    to_dest = (device == dest).astype(f32).astype(bf16)
    at_rank = jnp.where(device == rank, place + 1.0, 0.0).astype(bf16)
    offsets[...] = lax.dot_general(to_dest, at_rank, along, preferred_element_type=f32) - 1.0


def own_kernel(*refs):
    given, made, refs = refs[:8], refs[8:18], refs[18:]
    strip_out, coef, message, sums, level_sum, scale, numbers, routes, offsets, tiles = made
    here, (strip, sems) = refs[:7], refs[7:]
    half = given[7].at[pl.ds(0, HALF)]
    copies = start_all(zip((*given[:7], half), (*here, tiles)), sems)
    wait_all(copies[:5])
    route(*here[1:5], routes, offsets)
    weights, (air, cour) = here[0], here[5:7]
    for f in range(FIELDS):
        total = jnp.zeros((8, BLK), f32)
        for l in range(LEVELS):
            total = jnp.where(iota((8, BLK), 0) == l, weights[f, l], total)
        scale[f] = total
    wait_all(copies[5:7])
    for k in range(3):
        numbers[k] = cour[k]
    for side in range(2):
        lanes, own, shift = edge_lanes(side), own_columns(side, ROWS), SHIFTS[side]
        strips, coefs = [], []
        for f in range(FIELDS):
            level = lambda l: jnp.where(own, air[f, l, :, lanes], 0.0)
            strips.append(gather_levels(level, shift))
            strip[side, f] = strips[f]
        for k in range(3):
            coefs.append(spread(roll(jnp.where(own, cour[k, :, lanes], 0.0), shift, 1)))
            coef[side, k] = coefs[k]
        sums[side] = sum_strip(weights, strips)
        message[side] = message_rows(strips, coefs, sums[side])
    copy = pltpu.make_async_copy(strip, strip_out, sems.at[8])
    copy.start()
    for f in range(FIELDS):
        total = weights[f, 0] * air[f, 0]
        for l in range(1, LEVELS):
            total = total + weights[f, l] * air[f, l]
        level_sum[f] = total
    copy.wait()
    copies[7].wait()


def own_parts(*given):
    return pl.pallas_call(
        own_kernel,
        out_shape=(
            pltpu.HBM((2, FIELDS, ROWS, 128), f32),
            jax.ShapeDtypeStruct((2, 3, ROWS, 128), f32),
            jax.ShapeDtypeStruct((2, ROWS, 128), f32),
            jax.ShapeDtypeStruct((2, ROWS, 128), f32),
            jax.ShapeDtypeStruct((FIELDS, ROWS, COLS), f32),
            jax.ShapeDtypeStruct((FIELDS, 8, BLK), f32),
            jax.ShapeDtypeStruct((3, ROWS, COLS), f32),
            jax.ShapeDtypeStruct((8, ENTRIES), jnp.int32),
            jax.ShapeDtypeStruct((DEVICES, 128), f32),
            pltpu.VMEM((HALF, BLK, BLK), bf16),
        ),
        in_specs=[in_hbm] * 8,
        out_specs=(in_hbm,) + (in_vmem,) * 9,
        scratch_shapes=[pltpu.SMEM(given[0].shape, f32)]
        + [pltpu.VMEM(x.shape, x.dtype) for x in given[1:7]]
        + [pltpu.VMEM((2, FIELDS, ROWS, 128), f32), pltpu.SemaphoreType.DMA((9,))],
        compiler_params=params(),
        cost_estimate=pl.CostEstimate(flops=1600000, bytes_accessed=1200000, transcendentals=0),
        name="own_parts",
    )(*hbm(*given))


def halo_kernel(scale, nxt, sib, own_message, strip, coef, sums, send_w, send_e, halo):
    for side, send in enumerate((send_w, send_e)):
        lanes, own, shift = edge_lanes(side), own_columns(side, 8), SHIFTS[side]
        north, south = north_south(sib[:, lanes], nxt[:, lanes])
        for f in range(FIELDS):
            for j in range(3):
                at = f * 64 + j * 8
                halo[side, at : at + 8, :] = north[(f * 3 + j) * 8 : (f * 3 + j + 1) * 8]
                halo[side, at + 40 : at + 48, :] = south[(f * 3 + j) * 8 : (f * 3 + j + 1) * 8]
            halo[side, f * 64 + 24 : f * 64 + 40, :] = jnp.zeros((16, BLK), f32)
        strips, coefs = [], []
        for f in range(FIELDS):
            level = lambda l: jnp.where(own, halo[side, pl.ds(f * 64 + l, 8, stride=8), :], 0.0)
            strips.append(gather_levels(level, shift))
            strip[side, f] = strips[f]
        for k in range(3):
            rows = courant_rows(north[96:112], south[96:112], k)
            coefs.append(spread(roll(jnp.where(own, rows, 0.0), shift, 1)))
            coef[side, k] = coefs[k]
        total = jnp.zeros((8, BLK), f32)
        for f in range(FIELDS):
            rows = jnp.where(own, halo_sum(scale, f, north, south), 0.0)
            total = total + roll(rows, f * 16 + shift, 1)
        sums[side] = total
        send[:ROWS] = own_message[side]
        send[ROWS:] = message_rows(strips, coefs, sums[side])


def column_messages(scale, nxt, sib, own_message):
    message = jax.ShapeDtypeStruct((32, 128), f32)
    return pl.pallas_call(
        halo_kernel,
        out_shape=(
            jax.ShapeDtypeStruct((2, FIELDS, 8, 128), f32),
            jax.ShapeDtypeStruct((2, 3, 8, 128), f32),
            jax.ShapeDtypeStruct((2, 8, 128), f32),
            message,
            message,
        ),
        in_specs=[in_vmem] * 4,
        out_specs=(in_vmem,) * 5,
        scratch_shapes=[pltpu.VMEM((2, FIELDS * 64, BLK), f32)],
        compiler_params=params(),
        cost_estimate=pl.CostEstimate(flops=100000, bytes_accessed=400000, transcendentals=0),
        name="column_messages",
    )(scale, nxt, sib, own_message)


def received(side, got):
    lane = iota((32, 128), 1)
    place, group = lane % 16, lane // 16
    first = 0 if side == 0 else 6
    here = (place >= first) & (place < first + 3)
    spare = (place >= 12) & (place < 15)
    numbers = []
    for k in range(3):
        mine = jnp.where((group == k) & spare, got, 0.0)
        four = [roll(mine, (g - k) * 16 + first - 12, 1) for g in range(4)]
        four = (four[0] + four[1]) + (four[2] + four[3])
        numbers.append(four + roll(four, 64, 1))
    return here, numbers, roll(got, first - 60, 1)


def coefficients(cx, cy, kd):
    return 1.0 - cx - cy - 4.0 * kd, cx + kd, cy + kd, kd


def step(q, c):
    return (
        q * c[0]
        + roll(q, 1, 1) * c[1]
        + roll(q, 1, 0) * c[2]
        + (roll(q, -1, 1) + roll(q, -1, 0)) * c[3]
    )


def level_weight(weights, f, shape):
    scale = jnp.zeros(shape, f32)
    for l in range(LEVELS):
        scale = jnp.where(iota(shape, 0) == l, weights[f, l], scale)
    return scale


def flux_kernel(scale, level_sum, cour, nxt, sib, stored, flux, nxt_out, sib_out, tiles, sems):
    half = stored.at[pl.ds(HALF, ENTRIES - HALF)]
    copies = start_all([(half, tiles), (sib, sib_out), (nxt, nxt_out)], sems)
    north, south = north_south(sib[...], nxt[...])
    three = [
        jnp.concatenate([cour[k], courant_rows(north[96:], south[96:], k)], 0) for k in range(3)
    ]
    coefs = coefficients(*three)
    for f in range(FIELDS):
        rows = halo_sum(scale, f, north, south)
        q = jnp.concatenate([level_sum[f], rows], 0)
        for _ in range(STEPS):
            q = step(q, coefs)
        q = q[:ROWS].astype(bf16).astype(f32)
        for c in range(COLS // BLK):
            flux[pl.ds(c * FIELDS + f, ROWS, stride=24), :] = q[:, c * BLK : (c + 1) * BLK]
    wait_all(copies)


def flux_stencil(scale, level_sum, courant, nxt, sib, tiles):
    return pl.pallas_call(
        flux_kernel,
        out_shape=(
            jax.ShapeDtypeStruct((ROWS * 24, BLK), f32),
            pltpu.HBM(nxt.shape, bf16),
            pltpu.HBM(sib.shape, bf16),
            pltpu.VMEM((ENTRIES - HALF, BLK, BLK), bf16),
        ),
        in_specs=[in_vmem] * 5 + [in_hbm],
        out_specs=(in_vmem, in_hbm, in_hbm, in_vmem),
        scratch_shapes=[pltpu.SemaphoreType.DMA((3,))],
        compiler_params=params(),
        cost_estimate=pl.CostEstimate(flops=3000000, bytes_accessed=1000000, transcendentals=0),
        name="flux_stencil",
    )(scale, level_sum, courant, nxt, sib, *hbm(tiles))


def advance(c, q, below, above):
    return q * c[0] + roll(q, 1, 1) * c[1] + below * c[2] + (roll(q, -1, 1) + above) * c[3]


def sweep(coef, starts, done, emits):
    for r in range(-3, ROWS + 3):
        for start, d in zip(starts, done):
            d[0][r] = start(r)
        for s in range(3):
            at = r - 1 - s
            if s - 2 <= at < ROWS + 2 - s:
                c = [coef[k, at % 32 : at % 32 + 1, :] for k in range(4)]
                for d in done:
                    d[s + 1][at] = advance(c, d[s][at], d[s][at - 1], d[s][at + 1])
                if s == 2:
                    for emit, d in zip(emits, done):
                        emit(at, d[3][at])


def air_kernel(air, *refs):
    given, (out, ocean_out, *here), refs = refs[:12], refs[12:26], refs[26:]
    into, done, halo, coef, levels, in_sems, out_sems, sems = refs
    flux, ocean, mixing, mask, cour, sib, nxt, own_strip, halo_strip, strip_coef, from_w, from_e = here
    parts = COLS // BLK

    def copy_in(f, c):
        source = air.at[f, :, :, pl.ds(c * BLK, BLK)]
        return pltpu.make_async_copy(source, into.at[f, c], in_sems.at[f, c])

    def copy_out(f, c):
        target = out.at[f, :, :, pl.ds(c * BLK, BLK)]
        return pltpu.make_async_copy(done.at[f, c], target, out_sems.at[f, c])

    small = start_all(zip(given, here), sems)
    for f in range(FIELDS):
        for c in range(parts):
            copy_in(f, c).start()
    wait_all(small)
    ocean_copy = pltpu.make_async_copy(levels, ocean_out, sems.at[12])
    ocean_levels(flux, ocean, mixing, mask, levels)
    ocean_copy.start()
    north, south = north_south(sib[...], nxt[...])
    halo[0] = south[:96]
    halo[1] = north[:96]
    three = [
        jnp.concatenate([cour[k], courant_rows(north[96:], south[96:], k)], 0) for k in range(3)
    ]
    for k, c in enumerate(coefficients(*three)):
        coef[k] = c
    edges = []
    for side, got in enumerate((from_w, from_e)):
        here, _, _ = received(side, got[...])
        numbers = coefficients(*(strip_coef[side, k] for k in range(3)))
        first = 0 if side == 0 else 6
        for f in range(FIELDS):
            mine = jnp.concatenate([own_strip[side, f], halo_strip[side, f]], 0)
            q = jnp.where(here, roll(got[...], first - 3 * f, 1), mine)
            for _ in range(STEPS):
                q = step(q, numbers)
            edges.append(q[:ROWS])

    def starter(f):
        flat = [into.at[f, c].reshape(LEVELS * ROWS, BLK) for c in range(parts)]

        def start(r):
            if r < 0:
                return halo[0, f * 24 + (r + 3) * 8 : f * 24 + (r + 4) * 8, :]
            if r >= ROWS:
                return halo[1, f * 24 + (r - ROWS) * 8 : f * 24 + (r - ROWS + 1) * 8, :]
            return jnp.concatenate([x[pl.ds(r, LEVELS, stride=ROWS), :] for x in flat], 1)

        return start

    def emitter(f):
        flat = [done.at[f, c].reshape(LEVELS * ROWS, BLK) for c in range(parts)]

        def emit(r, q):
            for c in range(parts):
                flat[c][pl.ds(r, LEVELS, stride=ROWS), :] = q[:, c * BLK : (c + 1) * BLK]

        return emit

    column = iota((ROWS, 128), 1)
    for fields in ((0, 1), (2, 3)):
        for f in fields:
            for c in range(parts):
                copy_in(f, c).wait()
        sweep(
            coef,
            [starter(f) for f in fields],
            [[{}, {}, {}, {}] for f in fields],
            [emitter(f) for f in fields],
        )
        for f in fields:
            for c in range(1, parts - 1):
                copy_out(f, c).start()
            for l in range(LEVELS):
                west, east = roll(edges[f], -l * 16 - 3, 1), roll(edges[FIELDS + f], 122 - l * 16, 1)
                done[f, 0, l] = jnp.where(column < 3, west, done[f, 0, l])
                done[f, parts - 1, l] = jnp.where(column >= 125, east, done[f, parts - 1, l])
            copy_out(f, 0).start()
            copy_out(f, parts - 1).start()
    for f in range(FIELDS):
        for c in range(parts):
            copy_out(f, c).wait()
    ocean_copy.wait()


def ocean_levels(flux, ocean, mixing, mask, out):
    wet = mask[...].astype(f32)
    mix = wet * mixing[...]
    for f in range(FIELDS):
        q = [ocean[f, l] for l in range(8)]
        q[0] = q[0] + wet * flux[f]
        for l in range(8):
            out[f, l] = q[l] + mix * (q[max(l - 1, 0)] + q[min(l + 1, 7)] - 2.0 * q[l])


def air_steps(air, *given):
    parts = COLS // BLK
    return pl.pallas_call(
        air_kernel,
        out_shape=(pltpu.HBM(air.shape, f32), pltpu.HBM(given[1].shape, f32)),
        in_specs=[in_hbm] * 13,
        out_specs=(in_hbm, in_hbm),
        scratch_shapes=[pltpu.VMEM(x.shape, x.dtype) for x in given]
        + [
            pltpu.VMEM((FIELDS, parts, LEVELS, ROWS, BLK), f32),
            pltpu.VMEM((FIELDS, parts, LEVELS, ROWS, BLK), f32),
            pltpu.VMEM((2, 96, COLS), f32),
            pltpu.VMEM((4, 32, COLS), f32),
            pltpu.VMEM(given[1].shape, f32),
            pltpu.SemaphoreType.DMA((FIELDS, parts)),
            pltpu.SemaphoreType.DMA((FIELDS, parts)),
            pltpu.SemaphoreType.DMA((13,)),
        ],
        compiler_params=params(),
        cost_estimate=pl.CostEstimate(flops=30000000, bytes_accessed=6000000, transcendentals=0),
        name="air_steps",
    )(*hbm(air, *given))


def fix_edges(own_sums, halo_sums, own_coef, halo_coef, from_w, from_e, coef_out, flux):
    lane = iota((32, 128), 1)
    column = iota((ROWS, 128), 1)
    for side, got in enumerate((from_w, from_e)):
        here, numbers, sums = received(side, got[...])
        three = []
        for k in range(3):
            mine = jnp.concatenate([own_coef[side, k], halo_coef[side, k]], 0)
            three.append(jnp.where(here, numbers[k], mine))
            coef_out[side, k] = three[k]
        coefs = coefficients(*three)
        mine = jnp.concatenate([own_sums[side], halo_sums[side]], 0)
        q = jnp.where(here & (lane < 64), sums, mine)
        for _ in range(STEPS):
            q = step(q, coefs)
        q = q[:ROWS].astype(bf16).astype(f32)
        for f in range(FIELDS):
            at = pl.ds(8 + f + (0 if side == 0 else 20), ROWS, stride=24)
            if side == 0:
                flux[at, :] = jnp.where(column < 3, roll(q, -f * 16 - 3, 1), flux[at, :])
            else:
                flux[at, :] = jnp.where(column >= 125, roll(q, 122 - f * 16, 1), flux[at, :])


def block_rows(ref, at, low):
    half = iota((8, BLK), 0) < 4
    if low:
        return jnp.where(half, ref[pl.ds(at + 8, 8), :], 0.0)
    return jnp.where(half, 0.0, ref[pl.ds(at + 4, 8), :])


def four_rows(ref, at):
    left = jnp.concatenate([block_rows(ref, at[0], True), block_rows(ref, at[2], True)], 0)
    right = jnp.concatenate([block_rows(ref, at[1], False), block_rows(ref, at[3], False)], 0)
    return jnp.concatenate([left, right], 1).astype(bf16)


def four_results(r):
    return r[0:4, :BLK], r[4:8, :BLK], r[8:12, BLK:], r[12:16, BLK:]


def send_kernel(routes, flux_in, halo_strip, *refs):
    edges, (offsets, early, late, out, *kept, flux, total, coef, numbers, sems) = refs[:6], refs[6:]
    listed = pltpu.make_async_copy(routes, numbers, sems.at[4])
    listed.start()
    copies = start_all(zip((halo_strip, *edges[4:6]), kept), sems)
    flux[0:8, :] = jnp.zeros((8, BLK), f32)
    flux[8 : 8 + ROWS * 24, :] = flux_in[...]
    flux[8 + ROWS * 24 :, :] = jnp.zeros((8, BLK), f32)
    fix_edges(*edges, coef, flux)
    copies.append(pltpu.make_async_copy(coef, kept[3], sems.at[3]))
    copies[3].start()
    total[...] = jnp.zeros(total.shape, f32)
    total[pl.ds(BACK, DEVICES, stride=CHUNK), :] = offsets[...]
    listed.wait()
    for t in range(0, ENTRIES, 4):
        at = [numbers[0, t + i] for i in range(4)]
        tiles, u = (early, t) if t < HALF else (late, t - HALF)
        w = jnp.concatenate(
            [
                jnp.concatenate([tiles[u], tiles[u + 1]], 0),
                jnp.concatenate([tiles[u + 2], tiles[u + 3]], 0),
            ],
            1,
        )
        r = jnp.dot(four_rows(flux, at), w, preferred_element_type=f32)
        for i, piece in enumerate(four_results(r)):
            total[pl.ds(numbers[1, t + i], 4), :] = piece
    out[...] = total[...].astype(bf16)
    wait_all(copies)


def send_blocks(routes, flux, halo_strip, edges, offsets, early, late):
    return pl.pallas_call(
        send_kernel,
        out_shape=(
            jax.ShapeDtypeStruct((DEVICES * CHUNK, BLK), bf16),
            pltpu.HBM(halo_strip.shape, f32),
            pltpu.HBM((32, 128), f32),
            pltpu.HBM((32, 128), f32),
            pltpu.HBM((2, 3, 32, 128), f32),
        ),
        in_specs=[in_vmem] * 12,
        out_specs=(in_vmem,) + (in_hbm,) * 4,
        scratch_shapes=[
            pltpu.VMEM((ROWS * 24 + 16, BLK), f32),
            pltpu.VMEM((DEVICES * CHUNK, BLK), f32),
            pltpu.VMEM((2, 3, 32, 128), f32),
            pltpu.SMEM((8, ENTRIES), jnp.int32),
            pltpu.SemaphoreType.DMA((5,)),
        ],
        compiler_params=params(),
        cost_estimate=pl.CostEstimate(flops=40000000, bytes_accessed=11000000, transcendentals=0),
        name="send_blocks",
    )(routes, flux, halo_strip, *edges, offsets, early, late)


def ocean_kernel(payload, ocean, mixing, mask, flux_out, back, got, ret, packed, kept, sems):
    got[...] = payload[...].astype(f32)
    offsets = got[pl.ds(BACK, DEVICES, stride=CHUNK), :]
    by_slot = offsets.T
    blocks = iota((OCEAN_ROWS, DEVICES), 0).astype(f32)
    flux = None
    for j in range(CAP):
        place = (by_slot[j : j + 1, :] == blocks).astype(f32).astype(bf16)
        data = jnp.concatenate(
            [got[pl.ds(j * FIELDS + f, DEVICES, stride=CHUNK), :] for f in range(FIELDS)], 1
        ).astype(bf16)
        part = jnp.dot(place, data, preferred_element_type=f32)
        flux = part if j == 0 else flux + part
    wet = mask[...].astype(f32)
    mix = wet * mixing[...]
    surface = []
    for f in range(FIELDS):
        piece = flux[:, f * BLK : (f + 1) * BLK]
        kept[f] = piece
        top, below = ocean[f, 0] + wet * piece, ocean[f, 1]
        new = top + mix * (top + below - 2.0 * top)
        surface.append((wet * new).astype(bf16))
    copies = [pltpu.make_async_copy(kept, flux_out, sems.at[0])]
    copies[0].start()
    surface = jnp.concatenate(surface, 1)
    half = DEVICES // 4
    lanes = iota((half, OCEAN_ROWS), 1).astype(f32)
    for h in range(4):
        mine = offsets[h * half : (h + 1) * half]
        for j in range(CAP):
            pick = (mine[:, j : j + 1] == lanes).astype(f32).astype(bf16)
            rows = jnp.dot(pick, surface, preferred_element_type=f32)
            for f in range(FIELDS):
                at = pl.ds(h * half * BACK + j * FIELDS + f, half, stride=BACK)
                ret[at, :] = rows[:, f * BLK : (f + 1) * BLK]
        at = pl.ds(h * half * BACK, half * BACK)
        packed[at, :] = ret[at, :].astype(bf16)
        copies.append(pltpu.make_async_copy(packed.at[at], back.at[at], sems.at[1 + h]))
        copies[1 + h].start()
    wait_all(copies)


def ocean_surface(payload, ocean, mixing, mask):
    return pl.pallas_call(
        ocean_kernel,
        out_shape=(
            pltpu.HBM((FIELDS, OCEAN_ROWS, BLK), f32),
            pltpu.HBM((DEVICES * BACK, BLK), bf16),
        ),
        in_specs=[in_vmem] * 4,
        out_specs=(in_hbm, in_hbm),
        scratch_shapes=[
            pltpu.VMEM((DEVICES * CHUNK, BLK), f32),
            pltpu.VMEM((DEVICES * BACK, BLK), f32),
            pltpu.VMEM((DEVICES * BACK, BLK), bf16),
            pltpu.VMEM((FIELDS, OCEAN_ROWS, BLK), f32),
            pltpu.SemaphoreType.DMA((5,)),
        ],
        compiler_params=params(),
        cost_estimate=pl.CostEstimate(flops=100000000, bytes_accessed=4000000, transcendentals=0),
        name="ocean_surface",
    )(payload, ocean, mixing, mask)


PARTS = (0, 16, 56, 104, 160, 224, ENTRIES)


def return_kernel(routes, payload, stored, out, got, total, numbers, tiles, done, sems):
    listed = start_all([(routes, numbers)], sems)[0]
    waits = start_tiles(stored, tiles, sems.at[pl.ds(1, 6)], PARTS)
    got[0:8, :] = jnp.zeros((8, BLK), f32)
    got[8 : 8 + DEVICES * BACK, :] = payload[...].astype(f32)
    got[8 + DEVICES * BACK :, :] = jnp.zeros((8, BLK), f32)
    total[...] = jnp.zeros(total.shape, f32)
    listed.wait()
    for t in range(0, ENTRIES, 4):
        if t in waits:
            waits[t].wait()
        at = [numbers[2, t + i] for i in range(4)]
        w = jnp.concatenate(
            [
                jnp.concatenate([tiles[t], tiles[t + 1]], 1),
                jnp.concatenate([tiles[t + 2], tiles[t + 3]], 1),
            ],
            0,
        )
        r = lax.dot_general(
            four_rows(got, at), w, (((1,), (1,)), ((), ())), preferred_element_type=f32
        )
        for i, piece in enumerate(four_results(r)):
            here = pl.ds(numbers[0, t + i], 4)
            total[here, :] = total[here, :] + piece
    copies = []
    for f in range(FIELDS):
        for c in range(COLS // BLK):
            done[f, :, c * BLK : (c + 1) * BLK] = total[pl.ds(c * FIELDS + f, ROWS, stride=24), :]
        copies.append(pltpu.make_async_copy(done.at[f], out.at[f], sems.at[7 + f]))
        copies[f].start()
    wait_all(copies)


def return_blocks(routes, payload, tiles):
    return pl.pallas_call(
        return_kernel,
        out_shape=pltpu.HBM((FIELDS, ROWS, COLS), f32),
        in_specs=[in_vmem, in_vmem, in_hbm],
        out_specs=in_hbm,
        scratch_shapes=[
            pltpu.VMEM((DEVICES * BACK + 16, BLK), f32),
            pltpu.VMEM((ROWS * 24, BLK), f32),
            pltpu.SMEM((8, ENTRIES), jnp.int32),
            pltpu.VMEM((ENTRIES, BLK, BLK), bf16),
            pltpu.VMEM((FIELDS, ROWS, COLS), f32),
            pltpu.SemaphoreType.DMA((11,)),
        ],
        compiler_params=params(24),
        cost_estimate=pl.CostEstimate(flops=40000000, bytes_accessed=11000000, transcendentals=0),
        name="return_blocks",
    )(routes, payload, *hbm(tiles))


def exchange(x, rows):
    x = x.reshape(DEVICES * CAP, rows // CAP, BLK) if rows == BACK else x.reshape(-1, 2, BLK)
    x = lax.all_to_all(x, ("face", "tile"), split_axis=0, concat_axis=0, tiled=True)
    return x.reshape(DEVICES * rows, BLK)


def shards(
    atmos_state,
    courant,
    level_weights,
    remap_tiles,
    src_block,
    owner,
    offset,
    tile_index,
    ocean_state,
    mixing,
    land_mask,
):
    faces, tile_count = lax.axis_size("face"), lax.axis_size("tile")
    nxt, sib = row_messages(atmos_state, courant)
    inner = [(i, i + 1) for i in range(1, tile_count - 1, 2)]
    nxt = lax.ppermute(nxt, "tile", inner + [(b, a) for a, b in inner])
    sib = lax.ppermute(sib, "tile", [(i, i ^ 1) for i in range(tile_count)])
    own_strip, own_coef, own_message, own_sums, level_sum, scale, numbers, *rest = own_parts(
        *(level_weights, src_block, owner.reshape(1, -1), offset, tile_index),
        *(atmos_state, courant, remap_tiles),
    )
    routes, offsets, early = rest
    halo_strip, halo_coef, halo_sums, send_w, send_e = column_messages(
        scale, nxt, sib, own_message
    )
    from_e = lax.ppermute(send_w, "face", [((i + 1) % faces, i) for i in range(faces)])
    from_w = lax.ppermute(send_e, "face", [(i, (i + 1) % faces) for i in range(faces)])
    flux, nxt, sib, late = flux_stencil(scale, level_sum, numbers, nxt, sib, remap_tiles)
    edges = (own_sums, halo_sums, own_coef, halo_coef, from_w, from_e)
    message, *edges = send_blocks(
        routes, flux, halo_strip, edges, offsets, early, late
    )
    halo_strip, from_w, from_e, strip_coef = edges
    message = exchange(message, CHUNK)
    ocean_flux, back = ocean_surface(message, ocean_state, mixing, land_mask)
    back = exchange(back, BACK)
    ocean_inputs = (ocean_flux, ocean_state, mixing, land_mask)
    edges = (own_strip, halo_strip, strip_coef, from_w, from_e)
    air_state, ocean_out = air_steps(atmos_state, *ocean_inputs, courant, sib, nxt, *edges)
    atmos_surface = return_blocks(routes, back, remap_tiles)
    return air_state, ocean_out, atmos_surface


def solution(mesh):
    return jax.shard_map(
        shards,
        mesh=mesh,
        in_specs=(
            P(None, None, "tile", "face"),
            P(None, "tile", "face"),
            P(),
            P(("face", "tile"), None, None),
            P(("face", "tile"), None),
            P(("face", "tile"), None, None),
            P(("face", "tile"), None),
            P(("face", "tile"), None),
            P(None, None, "face", "tile"),
            P("face", "tile"),
            P("face", "tile"),
        ),
        out_specs=(
            P(None, None, "tile", "face"),
            P(None, None, "face", "tile"),
            P(None, "tile", "face"),
        ),
        check_vma=False,
    )
```

```python
import jax
import jax.numpy as jnp
from jax import lax
from jax.experimental import pallas as pl
from jax.experimental.pallas import tpu as pltpu
from jax.sharding import PartitionSpec as P

STEPS = 3
FIELDS, LEVELS, ROWS, COLS, BLK = 4, 8, 24, 768, 128
MESSAGE = 112
ENTRIES, DEVICES, CAP, OCEAN_ROWS = 288, 128, 5, 64
CHUNK = 22
BACK = CAP * FIELDS
HALF = 176
f32, bf16 = jnp.float32, jnp.bfloat16


def iota(shape, dim):
    return lax.broadcasted_iota(jnp.int32, shape, dim)


def roll(x, shift, axis):
    shift = shift % x.shape[axis]
    return pltpu.roll(x, shift, axis) if shift else x


def params(mib=16):
    return pltpu.CompilerParams(vmem_limit_bytes=mib << 20)


in_vmem = pl.BlockSpec(memory_space=pltpu.VMEM)
in_hbm = pl.BlockSpec(memory_space=pltpu.HBM)


def hbm(*arrays):
    return [pltpu.with_memory_space_constraint(x, pltpu.HBM) for x in arrays]


def start_all(pairs, sems):
    copies = [pltpu.make_async_copy(a, b, sems.at[i]) for i, (a, b) in enumerate(pairs)]
    for copy in copies:
        copy.start()
    return copies


def wait_all(copies):
    for copy in copies:
        copy.wait()


def start_tiles(stored, tiles, sems, bounds):
    parts = [pl.ds(a, b - a) for a, b in zip(bounds, bounds[1:])]
    pairs = [(stored.at[part], tiles.at[part]) for part in parts]
    return dict(zip(bounds, start_all(pairs, sems)))


def row_kernel(air, cour, nxt_ref, sib_ref, top, bot, top_cour, bot_cour, sems):
    pairs = [(cour.at[:, pl.ds(0, 8), :], top_cour), (cour.at[:, pl.ds(16, 8), :], bot_cour)]
    for c in range(COLS // BLK):
        lanes = pl.ds(c * BLK, BLK)
        pairs.append((air.at[:, :, pl.ds(0, 4), lanes], top.at[c]))
        pairs.append((air.at[:, :, pl.ds(20, 4), lanes], bot.at[c]))
    copies = start_all(pairs, sems)

    def pack_numbers(out, at_top):
        first, numbers = (0, top_cour) if at_top else (5, bot_cour)
        sub = iota((8, COLS), 0)
        pair = jnp.where(sub < 4, roll(numbers[0], -first, 0), roll(numbers[1], 4 - first, 0))
        last = jnp.where(sub < 4, roll(numbers[2], -first, 0), 0.0)
        out[96:112, :] = jnp.concatenate([pair, last], 0).astype(bf16)

    def pack(out, at_top, c):
        first, rows = (0, top) if at_top else (1, bot)
        flat = rows.at[c].reshape(FIELDS * LEVELS * 4, BLK)

        def tile(i):
            return flat[pl.ds(i // 3 * 32 + first + i % 3, LEVELS, stride=4), :]

        for i in range(0, FIELDS * 3, 2):
            both = jnp.concatenate([tile(i), tile(i + 1)], 0)
            out[i * 8 : i * 8 + 16, c * BLK : (c + 1) * BLK] = both.astype(bf16)

    def send(to_top, to_bot):
        wait_all(copies[:2])
        pack_numbers(to_top, True)
        pack_numbers(to_bot, False)
        for c in range(COLS // BLK):
            wait_all(copies[2 * c + 2 : 2 * c + 4])
            pack(to_top, True, c)
            pack(to_bot, False, c)

    odd = lax.axis_index("tile") % 2

    @pl.when(odd == 1)
    def _():
        send(sib_ref, nxt_ref)

    @pl.when(odd == 0)
    def _():
        send(nxt_ref, sib_ref)


def row_messages(air, courant):
    shape = jax.ShapeDtypeStruct((MESSAGE, COLS), bf16)
    return pl.pallas_call(
        row_kernel,
        out_shape=(shape, shape),
        in_specs=[in_hbm] * 2,
        out_specs=(in_vmem,) * 2,
        scratch_shapes=[pltpu.VMEM((COLS // BLK, FIELDS, LEVELS, 4, BLK), f32)] * 2
        + [pltpu.VMEM((3, 8, COLS), f32)] * 2
        + [pltpu.SemaphoreType.DMA((14,))],
        compiler_params=params(),
        cost_estimate=pl.CostEstimate(flops=400000, bytes_accessed=2000000, transcendentals=0),
        name="row_messages",
    )(*hbm(air, courant))


def courant_rows(north, south, k):
    base = k // 2 * 8
    n, s = north[base : base + 8], south[base : base + 8]
    sub = iota(n.shape, 0)
    if k % 2:
        return jnp.where(sub < 3, roll(n, 4, 0), roll(s, 1, 0))
    return jnp.where(sub < 3, n, roll(s, 5, 0))


def halo_sum(scale, f, north, south):
    sub = iota((8, north.shape[1]), 0)
    weight = jnp.concatenate([scale[f]] * (north.shape[1] // BLK), 1)
    rows = jnp.zeros(sub.shape, f32)
    for j in range(3):
        at = slice((f * 3 + j) * 8, (f * 3 + j + 1) * 8)
        rows = jnp.where(sub == j, jnp.sum(north[at] * weight, axis=0, keepdims=True), rows)
        rows = jnp.where(sub == 5 + j, jnp.sum(south[at] * weight, axis=0, keepdims=True), rows)
    return rows


def north_south(sib, nxt):
    odd = lax.axis_index("tile") % 2 == 1
    a, b = sib.astype(f32), nxt.astype(f32)
    return jnp.where(odd, b, a), jnp.where(odd, a, b)


SHIFTS = (3, 6)


def edge_lanes(side):
    return slice(0, BLK) if side == 0 else slice(COLS - BLK, COLS)


def own_columns(side, rows):
    lane = iota((rows, 128), 1)
    return lane < 6 if side == 0 else lane >= 122


def gather_levels(level, shift):
    total = roll(level(0), shift, 1)
    for l in range(1, LEVELS):
        total = total + roll(level(l), l * 16 + shift, 1)
    return total


def spread(x):
    for s in (16, 32, 64):
        x = x + roll(x, s, 1)
    return x


def message_rows(strips, coefs, sums):
    lane = iota(strips[0].shape, 1)
    place = lane % 16
    middle = (place >= 3) & (place < 6)
    message = jnp.zeros(strips[0].shape, f32)
    for f in range(FIELDS):
        message = message + roll(jnp.where(middle, strips[f], 0.0), 3 * f - 3, 1)
    for k in range(3):
        mine = middle & (lane // 16 == k)
        message = message + roll(jnp.where(mine, coefs[k], 0.0), 9, 1)
    return message + roll(jnp.where(middle & (lane < 64), sums, 0.0), 57, 1)


def level_lanes(weights, f, rows):
    lane = iota((rows, 128), 1) // 16
    scale = jnp.zeros((rows, 128), f32)
    for l in range(LEVELS):
        scale = jnp.where(lane == l, weights[f, l], scale)
    return scale


def sum_strip(weights, strips):
    rows = strips[0].shape[0]
    group = iota((rows, 128), 1) // 16
    total = jnp.zeros((rows, 128), f32)
    for f in range(FIELDS):
        whole = spread(strips[f] * level_lanes(weights, f, rows))
        total = jnp.where(group == f, whole, total)
    return total


def route(src, owner, offset, tile_index, routes, offsets):
    row = lambda ref: ref[...].astype(f32)
    sub = iota((8, ENTRIES), 0)
    known = jnp.where(sub == 0, row(src), jnp.where(sub == 1, row(owner), row(offset))).astype(bf16)
    pick = (iota((ENTRIES, ENTRIES), 0) == tile_index[...]).astype(f32).astype(bf16)
    along = (((1,), (1,)), ((), ()))
    by_tile = lax.dot_general(known, pick, along, preferred_element_type=f32)
    down = lax.dot_general(pick, known, along, preferred_element_type=f32)
    source, dest, place = by_tile[0:1], by_tile[1:2], by_tile[2:3]
    earlier = iota((ENTRIES, ENTRIES), 0) < iota((ENTRIES, ENTRIES), 1)
    same = jnp.where(earlier & (down[:, 1:2] == dest), 1.0, 0.0)
    rank = jnp.sum(same, axis=0, keepdims=True)
    numbers = jnp.where(
        sub == 0,
        source * FIELDS,
        jnp.where(sub == 1, dest * CHUNK + rank * FIELDS, dest * BACK + rank * FIELDS),
    )
    routes[...] = numbers.astype(jnp.int32)
    device = iota((DEVICES, ENTRIES), 0).astype(f32)
    to_dest = (device == dest).astype(f32).astype(bf16)
    at_rank = jnp.where(device == rank, place + 1.0, 0.0).astype(bf16)
    offsets[...] = lax.dot_general(to_dest, at_rank, along, preferred_element_type=f32) - 1.0


def own_kernel(*refs):
    given, made, refs = refs[:8], refs[8:18], refs[18:]
    strip_out, coef, message, sums, level_sum, scale, numbers, routes, offsets, tiles = made
    here, (strip, sems) = refs[:7], refs[7:]
    half = given[7].at[pl.ds(0, HALF)]
    copies = start_all(zip((*given[:7], half), (*here, tiles)), sems)
    wait_all(copies[:5])
    route(*here[1:5], routes, offsets)
    weights, (air, cour) = here[0], here[5:7]
    for f in range(FIELDS):
        total = jnp.zeros((8, BLK), f32)
        for l in range(LEVELS):
            total = jnp.where(iota((8, BLK), 0) == l, weights[f, l], total)
        scale[f] = total
    wait_all(copies[5:7])
    for k in range(3):
        numbers[k] = cour[k]
    for side in range(2):
        lanes, own, shift = edge_lanes(side), own_columns(side, ROWS), SHIFTS[side]
        strips, coefs = [], []
        for f in range(FIELDS):
            level = lambda l: jnp.where(own, air[f, l, :, lanes], 0.0)
            strips.append(gather_levels(level, shift))
            strip[side, f] = strips[f]
        for k in range(3):
            coefs.append(spread(roll(jnp.where(own, cour[k, :, lanes], 0.0), shift, 1)))
            coef[side, k] = coefs[k]
        sums[side] = sum_strip(weights, strips)
        message[side] = message_rows(strips, coefs, sums[side])
    copy = pltpu.make_async_copy(strip, strip_out, sems.at[8])
    copy.start()
    for f in range(FIELDS):
        total = weights[f, 0] * air[f, 0]
        for l in range(1, LEVELS):
            total = total + weights[f, l] * air[f, l]
        level_sum[f] = total
    copy.wait()
    copies[7].wait()


def own_parts(*given):
    return pl.pallas_call(
        own_kernel,
        out_shape=(
            pltpu.HBM((2, FIELDS, ROWS, 128), f32),
            jax.ShapeDtypeStruct((2, 3, ROWS, 128), f32),
            jax.ShapeDtypeStruct((2, ROWS, 128), f32),
            jax.ShapeDtypeStruct((2, ROWS, 128), f32),
            jax.ShapeDtypeStruct((FIELDS, ROWS, COLS), f32),
            jax.ShapeDtypeStruct((FIELDS, 8, BLK), f32),
            jax.ShapeDtypeStruct((3, ROWS, COLS), f32),
            jax.ShapeDtypeStruct((8, ENTRIES), jnp.int32),
            jax.ShapeDtypeStruct((DEVICES, 128), f32),
            pltpu.VMEM((HALF, BLK, BLK), bf16),
        ),
        in_specs=[in_hbm] * 8,
        out_specs=(in_hbm,) + (in_vmem,) * 9,
        scratch_shapes=[pltpu.SMEM(given[0].shape, f32)]
        + [pltpu.VMEM(x.shape, x.dtype) for x in given[1:7]]
        + [pltpu.VMEM((2, FIELDS, ROWS, 128), f32), pltpu.SemaphoreType.DMA((9,))],
        compiler_params=params(),
        cost_estimate=pl.CostEstimate(flops=1600000, bytes_accessed=1200000, transcendentals=0),
        name="own_parts",
    )(*hbm(*given))


def halo_kernel(scale, nxt, sib, own_message, strip, coef, sums, send_w, send_e, halo):
    for side, send in enumerate((send_w, send_e)):
        lanes, own, shift = edge_lanes(side), own_columns(side, 8), SHIFTS[side]
        north, south = north_south(sib[:, lanes], nxt[:, lanes])
        for f in range(FIELDS):
            for j in range(3):
                at = f * 64 + j * 8
                halo[side, at : at + 8, :] = north[(f * 3 + j) * 8 : (f * 3 + j + 1) * 8]
                halo[side, at + 40 : at + 48, :] = south[(f * 3 + j) * 8 : (f * 3 + j + 1) * 8]
            halo[side, f * 64 + 24 : f * 64 + 40, :] = jnp.zeros((16, BLK), f32)
        strips, coefs = [], []
        for f in range(FIELDS):
            level = lambda l: jnp.where(own, halo[side, pl.ds(f * 64 + l, 8, stride=8), :], 0.0)
            strips.append(gather_levels(level, shift))
            strip[side, f] = strips[f]
        for k in range(3):
            rows = courant_rows(north[96:112], south[96:112], k)
            coefs.append(spread(roll(jnp.where(own, rows, 0.0), shift, 1)))
            coef[side, k] = coefs[k]
        total = jnp.zeros((8, BLK), f32)
        for f in range(FIELDS):
            rows = jnp.where(own, halo_sum(scale, f, north, south), 0.0)
            total = total + roll(rows, f * 16 + shift, 1)
        sums[side] = total
        send[:ROWS] = own_message[side]
        send[ROWS:] = message_rows(strips, coefs, sums[side])


def column_messages(scale, nxt, sib, own_message):
    message = jax.ShapeDtypeStruct((32, 128), f32)
    return pl.pallas_call(
        halo_kernel,
        out_shape=(
            jax.ShapeDtypeStruct((2, FIELDS, 8, 128), f32),
            jax.ShapeDtypeStruct((2, 3, 8, 128), f32),
            jax.ShapeDtypeStruct((2, 8, 128), f32),
            message,
            message,
        ),
        in_specs=[in_vmem] * 4,
        out_specs=(in_vmem,) * 5,
        scratch_shapes=[pltpu.VMEM((2, FIELDS * 64, BLK), f32)],
        compiler_params=params(),
        cost_estimate=pl.CostEstimate(flops=100000, bytes_accessed=400000, transcendentals=0),
        name="column_messages",
    )(scale, nxt, sib, own_message)


def received(side, got):
    lane = iota((32, 128), 1)
    place, group = lane % 16, lane // 16
    first = 0 if side == 0 else 6
    here = (place >= first) & (place < first + 3)
    spare = (place >= 12) & (place < 15)
    numbers = []
    for k in range(3):
        mine = jnp.where((group == k) & spare, got, 0.0)
        four = [roll(mine, (g - k) * 16 + first - 12, 1) for g in range(4)]
        four = (four[0] + four[1]) + (four[2] + four[3])
        numbers.append(four + roll(four, 64, 1))
    return here, numbers, roll(got, first - 60, 1)


def coefficients(cx, cy, kd):
    return 1.0 - cx - cy - 4.0 * kd, cx + kd, cy + kd, kd


def step(q, c):
    return (
        q * c[0]
        + roll(q, 1, 1) * c[1]
        + roll(q, 1, 0) * c[2]
        + (roll(q, -1, 1) + roll(q, -1, 0)) * c[3]
    )


def level_weight(weights, f, shape):
    scale = jnp.zeros(shape, f32)
    for l in range(LEVELS):
        scale = jnp.where(iota(shape, 0) == l, weights[f, l], scale)
    return scale


def flux_kernel(scale, level_sum, cour, nxt, sib, stored, flux, nxt_out, sib_out, tiles, sems):
    half = stored.at[pl.ds(HALF, ENTRIES - HALF)]
    copies = start_all([(half, tiles), (sib, sib_out), (nxt, nxt_out)], sems)
    north, south = north_south(sib[...], nxt[...])
    three = [
        jnp.concatenate([cour[k], courant_rows(north[96:], south[96:], k)], 0) for k in range(3)
    ]
    coefs = coefficients(*three)
    for f in range(FIELDS):
        rows = halo_sum(scale, f, north, south)
        q = jnp.concatenate([level_sum[f], rows], 0)
        for _ in range(STEPS):
            q = step(q, coefs)
        q = q[:ROWS].astype(bf16).astype(f32)
        for c in range(COLS // BLK):
            flux[pl.ds(c * FIELDS + f, ROWS, stride=24), :] = q[:, c * BLK : (c + 1) * BLK]
    wait_all(copies)


def flux_stencil(scale, level_sum, courant, nxt, sib, tiles):
    return pl.pallas_call(
        flux_kernel,
        out_shape=(
            jax.ShapeDtypeStruct((ROWS * 24, BLK), f32),
            pltpu.HBM(nxt.shape, bf16),
            pltpu.HBM(sib.shape, bf16),
            pltpu.VMEM((ENTRIES - HALF, BLK, BLK), bf16),
        ),
        in_specs=[in_vmem] * 5 + [in_hbm],
        out_specs=(in_vmem, in_hbm, in_hbm, in_vmem),
        scratch_shapes=[pltpu.SemaphoreType.DMA((3,))],
        compiler_params=params(),
        cost_estimate=pl.CostEstimate(flops=3000000, bytes_accessed=1000000, transcendentals=0),
        name="flux_stencil",
    )(scale, level_sum, courant, nxt, sib, *hbm(tiles))


def advance(c, q, below, above):
    return q * c[0] + roll(q, 1, 1) * c[1] + below * c[2] + (roll(q, -1, 1) + above) * c[3]


def sweep(coef, starts, done, emits):
    for r in range(-3, ROWS + 3):
        for start, d in zip(starts, done):
            d[0][r] = start(r)
        for s in range(3):
            at = r - 1 - s
            if s - 2 <= at < ROWS + 2 - s:
                c = [coef[k, at % 32 : at % 32 + 1, :] for k in range(4)]
                for d in done:
                    d[s + 1][at] = advance(c, d[s][at], d[s][at - 1], d[s][at + 1])
                if s == 2:
                    for emit, d in zip(emits, done):
                        emit(at, d[3][at])


def air_kernel(air, *refs):
    given, (out, ocean_out, *here), refs = refs[:12], refs[12:26], refs[26:]
    into, done, halo, coef, levels, in_sems, out_sems, sems = refs
    flux, ocean, mixing, mask, cour, sib, nxt, own_strip, halo_strip, strip_coef, from_w, from_e = here
    parts = COLS // BLK

    def copy_in(f, c):
        source = air.at[f, :, :, pl.ds(c * BLK, BLK)]
        return pltpu.make_async_copy(source, into.at[f, c], in_sems.at[f, c])

    def copy_out(f, c):
        target = out.at[f, :, :, pl.ds(c * BLK, BLK)]
        return pltpu.make_async_copy(done.at[f, c], target, out_sems.at[f, c])

    small = start_all(zip(given, here), sems)
    for f in range(FIELDS):
        for c in range(parts):
            copy_in(f, c).start()
    wait_all(small)
    ocean_copy = pltpu.make_async_copy(levels, ocean_out, sems.at[12])
    ocean_levels(flux, ocean, mixing, mask, levels)
    ocean_copy.start()
    north, south = north_south(sib[...], nxt[...])
    halo[0] = south[:96]
    halo[1] = north[:96]
    three = [
        jnp.concatenate([cour[k], courant_rows(north[96:], south[96:], k)], 0) for k in range(3)
    ]
    for k, c in enumerate(coefficients(*three)):
        coef[k] = c
    edges = []
    for side, got in enumerate((from_w, from_e)):
        here, _, _ = received(side, got[...])
        numbers = coefficients(*(strip_coef[side, k] for k in range(3)))
        first = 0 if side == 0 else 6
        for f in range(FIELDS):
            mine = jnp.concatenate([own_strip[side, f], halo_strip[side, f]], 0)
            q = jnp.where(here, roll(got[...], first - 3 * f, 1), mine)
            for _ in range(STEPS):
                q = step(q, numbers)
            edges.append(q[:ROWS])

    def starter(f):
        flat = [into.at[f, c].reshape(LEVELS * ROWS, BLK) for c in range(parts)]

        def start(r):
            if r < 0:
                return halo[0, f * 24 + (r + 3) * 8 : f * 24 + (r + 4) * 8, :]
            if r >= ROWS:
                return halo[1, f * 24 + (r - ROWS) * 8 : f * 24 + (r - ROWS + 1) * 8, :]
            return jnp.concatenate([x[pl.ds(r, LEVELS, stride=ROWS), :] for x in flat], 1)

        return start

    def emitter(f):
        flat = [done.at[f, c].reshape(LEVELS * ROWS, BLK) for c in range(parts)]

        def emit(r, q):
            for c in range(parts):
                flat[c][pl.ds(r, LEVELS, stride=ROWS), :] = q[:, c * BLK : (c + 1) * BLK]

        return emit

    column = iota((ROWS, 128), 1)
    for fields in ((0, 1), (2, 3)):
        for f in fields:
            for c in range(parts):
                copy_in(f, c).wait()
        sweep(
            coef,
            [starter(f) for f in fields],
            [[{}, {}, {}, {}] for f in fields],
            [emitter(f) for f in fields],
        )
        for f in fields:
            for c in range(1, parts - 1):
                copy_out(f, c).start()
            for l in range(LEVELS):
                west, east = roll(edges[f], -l * 16 - 3, 1), roll(edges[FIELDS + f], 122 - l * 16, 1)
                done[f, 0, l] = jnp.where(column < 3, west, done[f, 0, l])
                done[f, parts - 1, l] = jnp.where(column >= 125, east, done[f, parts - 1, l])
            copy_out(f, 0).start()
            copy_out(f, parts - 1).start()
    for f in range(FIELDS):
        for c in range(parts):
            copy_out(f, c).wait()
    ocean_copy.wait()


def ocean_levels(flux, ocean, mixing, mask, out):
    wet = mask[...].astype(f32)
    mix = wet * mixing[...]
    for f in range(FIELDS):
        q = [ocean[f, l] for l in range(8)]
        q[0] = q[0] + wet * flux[f]
        for l in range(8):
            out[f, l] = q[l] + mix * (q[max(l - 1, 0)] + q[min(l + 1, 7)] - 2.0 * q[l])


def air_steps(air, *given):
    parts = COLS // BLK
    return pl.pallas_call(
        air_kernel,
        out_shape=(pltpu.HBM(air.shape, f32), pltpu.HBM(given[1].shape, f32)),
        in_specs=[in_hbm] * 13,
        out_specs=(in_hbm, in_hbm),
        scratch_shapes=[pltpu.VMEM(x.shape, x.dtype) for x in given]
        + [
            pltpu.VMEM((FIELDS, parts, LEVELS, ROWS, BLK), f32),
            pltpu.VMEM((FIELDS, parts, LEVELS, ROWS, BLK), f32),
            pltpu.VMEM((2, 96, COLS), f32),
            pltpu.VMEM((4, 32, COLS), f32),
            pltpu.VMEM(given[1].shape, f32),
            pltpu.SemaphoreType.DMA((FIELDS, parts)),
            pltpu.SemaphoreType.DMA((FIELDS, parts)),
            pltpu.SemaphoreType.DMA((13,)),
        ],
        compiler_params=params(),
        cost_estimate=pl.CostEstimate(flops=30000000, bytes_accessed=6000000, transcendentals=0),
        name="air_steps",
    )(*hbm(air, *given))


def fix_edges(own_sums, halo_sums, own_coef, halo_coef, from_w, from_e, coef_out, flux):
    lane = iota((32, 128), 1)
    column = iota((ROWS, 128), 1)
    for side, got in enumerate((from_w, from_e)):
        here, numbers, sums = received(side, got[...])
        three = []
        for k in range(3):
            mine = jnp.concatenate([own_coef[side, k], halo_coef[side, k]], 0)
            three.append(jnp.where(here, numbers[k], mine))
            coef_out[side, k] = three[k]
        coefs = coefficients(*three)
        mine = jnp.concatenate([own_sums[side], halo_sums[side]], 0)
        q = jnp.where(here & (lane < 64), sums, mine)
        for _ in range(STEPS):
            q = step(q, coefs)
        q = q[:ROWS].astype(bf16).astype(f32)
        for f in range(FIELDS):
            at = pl.ds(8 + f + (0 if side == 0 else 20), ROWS, stride=24)
            if side == 0:
                flux[at, :] = jnp.where(column < 3, roll(q, -f * 16 - 3, 1), flux[at, :])
            else:
                flux[at, :] = jnp.where(column >= 125, roll(q, 122 - f * 16, 1), flux[at, :])


def block_rows(ref, at, low):
    half = iota((8, BLK), 0) < 4
    if low:
        return jnp.where(half, ref[pl.ds(at + 8, 8), :], 0.0)
    return jnp.where(half, 0.0, ref[pl.ds(at + 4, 8), :])


def four_rows(ref, at):
    left = jnp.concatenate([block_rows(ref, at[0], True), block_rows(ref, at[2], True)], 0)
    right = jnp.concatenate([block_rows(ref, at[1], False), block_rows(ref, at[3], False)], 0)
    return jnp.concatenate([left, right], 1).astype(bf16)


def four_results(r):
    return r[0:4, :BLK], r[4:8, :BLK], r[8:12, BLK:], r[12:16, BLK:]


def send_kernel(routes, flux_in, halo_strip, *refs):
    edges, (offsets, early, late, out, *kept, flux, total, coef, numbers, sems) = refs[:6], refs[6:]
    listed = pltpu.make_async_copy(routes, numbers, sems.at[4])
    listed.start()
    copies = start_all(zip((halo_strip, *edges[4:6]), kept), sems)
    flux[0:8, :] = jnp.zeros((8, BLK), f32)
    flux[8 : 8 + ROWS * 24, :] = flux_in[...]
    flux[8 + ROWS * 24 :, :] = jnp.zeros((8, BLK), f32)
    fix_edges(*edges, coef, flux)
    copies.append(pltpu.make_async_copy(coef, kept[3], sems.at[3]))
    copies[3].start()
    total[...] = jnp.zeros(total.shape, f32)
    total[pl.ds(BACK, DEVICES, stride=CHUNK), :] = offsets[...]
    listed.wait()
    for t in range(0, ENTRIES, 4):
        at = [numbers[0, t + i] for i in range(4)]
        tiles, u = (early, t) if t < HALF else (late, t - HALF)
        w = jnp.concatenate(
            [
                jnp.concatenate([tiles[u], tiles[u + 1]], 0),
                jnp.concatenate([tiles[u + 2], tiles[u + 3]], 0),
            ],
            1,
        )
        r = jnp.dot(four_rows(flux, at), w, preferred_element_type=f32)
        for i, piece in enumerate(four_results(r)):
            total[pl.ds(numbers[1, t + i], 4), :] = piece
    out[...] = total[...].astype(bf16)
    wait_all(copies)


def send_blocks(routes, flux, halo_strip, edges, offsets, early, late):
    return pl.pallas_call(
        send_kernel,
        out_shape=(
            jax.ShapeDtypeStruct((DEVICES * CHUNK, BLK), bf16),
            pltpu.HBM(halo_strip.shape, f32),
            pltpu.HBM((32, 128), f32),
            pltpu.HBM((32, 128), f32),
            pltpu.HBM((2, 3, 32, 128), f32),
        ),
        in_specs=[in_vmem] * 12,
        out_specs=(in_vmem,) + (in_hbm,) * 4,
        scratch_shapes=[
            pltpu.VMEM((ROWS * 24 + 16, BLK), f32),
            pltpu.VMEM((DEVICES * CHUNK, BLK), f32),
            pltpu.VMEM((2, 3, 32, 128), f32),
            pltpu.SMEM((8, ENTRIES), jnp.int32),
            pltpu.SemaphoreType.DMA((5,)),
        ],
        compiler_params=params(),
        cost_estimate=pl.CostEstimate(flops=40000000, bytes_accessed=11000000, transcendentals=0),
        name="send_blocks",
    )(routes, flux, halo_strip, *edges, offsets, early, late)


def ocean_kernel(payload, ocean, mixing, mask, flux_out, back, got, ret, packed, kept, sems):
    got[...] = payload[...].astype(f32)
    offsets = got[pl.ds(BACK, DEVICES, stride=CHUNK), :]
    by_slot = offsets.T
    blocks = iota((OCEAN_ROWS, DEVICES), 0).astype(f32)
    flux = None
    for j in range(CAP):
        place = (by_slot[j : j + 1, :] == blocks).astype(f32).astype(bf16)
        data = jnp.concatenate(
            [got[pl.ds(j * FIELDS + f, DEVICES, stride=CHUNK), :] for f in range(FIELDS)], 1
        ).astype(bf16)
        part = jnp.dot(place, data, preferred_element_type=f32)
        flux = part if j == 0 else flux + part
    wet = mask[...].astype(f32)
    mix = wet * mixing[...]
    surface = []
    for f in range(FIELDS):
        piece = flux[:, f * BLK : (f + 1) * BLK]
        kept[f] = piece
        top, below = ocean[f, 0] + wet * piece, ocean[f, 1]
        new = top + mix * (top + below - 2.0 * top)
        surface.append((wet * new).astype(bf16))
    copies = [pltpu.make_async_copy(kept, flux_out, sems.at[0])]
    copies[0].start()
    surface = jnp.concatenate(surface, 1)
    half = DEVICES // 4
    lanes = iota((half, OCEAN_ROWS), 1).astype(f32)
    for h in range(4):
        mine = offsets[h * half : (h + 1) * half]
        for j in range(CAP):
            pick = (mine[:, j : j + 1] == lanes).astype(f32).astype(bf16)
            rows = jnp.dot(pick, surface, preferred_element_type=f32)
            for f in range(FIELDS):
                at = pl.ds(h * half * BACK + j * FIELDS + f, half, stride=BACK)
                ret[at, :] = rows[:, f * BLK : (f + 1) * BLK]
        at = pl.ds(h * half * BACK, half * BACK)
        packed[at, :] = ret[at, :].astype(bf16)
        copies.append(pltpu.make_async_copy(packed.at[at], back.at[at], sems.at[1 + h]))
        copies[1 + h].start()
    wait_all(copies)


def ocean_surface(payload, ocean, mixing, mask):
    return pl.pallas_call(
        ocean_kernel,
        out_shape=(
            pltpu.HBM((FIELDS, OCEAN_ROWS, BLK), f32),
            pltpu.HBM((DEVICES * BACK, BLK), bf16),
        ),
        in_specs=[in_vmem] * 4,
        out_specs=(in_hbm, in_hbm),
        scratch_shapes=[
            pltpu.VMEM((DEVICES * CHUNK, BLK), f32),
            pltpu.VMEM((DEVICES * BACK, BLK), f32),
            pltpu.VMEM((DEVICES * BACK, BLK), bf16),
            pltpu.VMEM((FIELDS, OCEAN_ROWS, BLK), f32),
            pltpu.SemaphoreType.DMA((5,)),
        ],
        compiler_params=params(),
        cost_estimate=pl.CostEstimate(flops=100000000, bytes_accessed=4000000, transcendentals=0),
        name="ocean_surface",
    )(payload, ocean, mixing, mask)


PARTS = (0, 16, 56, 104, 160, 224, ENTRIES)


def return_kernel(routes, payload, stored, out, got, total, numbers, tiles, done, sems):
    listed = start_all([(routes, numbers)], sems)[0]
    waits = start_tiles(stored, tiles, sems.at[pl.ds(1, 6)], PARTS)
    got[0:8, :] = jnp.zeros((8, BLK), f32)
    got[8 : 8 + DEVICES * BACK, :] = payload[...].astype(f32)
    got[8 + DEVICES * BACK :, :] = jnp.zeros((8, BLK), f32)
    total[...] = jnp.zeros(total.shape, f32)
    listed.wait()
    for t in range(0, ENTRIES, 4):
        if t in waits:
            waits[t].wait()
        at = [numbers[2, t + i] for i in range(4)]
        w = jnp.concatenate(
            [
                jnp.concatenate([tiles[t], tiles[t + 1]], 1),
                jnp.concatenate([tiles[t + 2], tiles[t + 3]], 1),
            ],
            0,
        )
        r = lax.dot_general(
            four_rows(got, at), w, (((1,), (1,)), ((), ())), preferred_element_type=f32
        )
        for i, piece in enumerate(four_results(r)):
            here = pl.ds(numbers[0, t + i], 4)
            total[here, :] = total[here, :] + piece
    copies = []
    for f in range(FIELDS):
        for c in range(COLS // BLK):
            done[f, :, c * BLK : (c + 1) * BLK] = total[pl.ds(c * FIELDS + f, ROWS, stride=24), :]
        copies.append(pltpu.make_async_copy(done.at[f], out.at[f], sems.at[7 + f]))
        copies[f].start()
    wait_all(copies)


def return_blocks(routes, payload, tiles):
    return pl.pallas_call(
        return_kernel,
        out_shape=pltpu.HBM((FIELDS, ROWS, COLS), f32),
        in_specs=[in_vmem, in_vmem, in_hbm],
        out_specs=in_hbm,
        scratch_shapes=[
            pltpu.VMEM((DEVICES * BACK + 16, BLK), f32),
            pltpu.VMEM((ROWS * 24, BLK), f32),
            pltpu.SMEM((8, ENTRIES), jnp.int32),
            pltpu.VMEM((ENTRIES, BLK, BLK), bf16),
            pltpu.VMEM((FIELDS, ROWS, COLS), f32),
            pltpu.SemaphoreType.DMA((11,)),
        ],
        compiler_params=params(24),
        cost_estimate=pl.CostEstimate(flops=40000000, bytes_accessed=11000000, transcendentals=0),
        name="return_blocks",
    )(routes, payload, *hbm(tiles))


def exchange(x, rows):
    x = x.reshape(DEVICES * CAP, rows // CAP, BLK) if rows == BACK else x.reshape(-1, 2, BLK)
    x = lax.all_to_all(x, ("face", "tile"), split_axis=0, concat_axis=0, tiled=True)
    return x.reshape(DEVICES * rows, BLK)


def shards(
    atmos_state,
    courant,
    level_weights,
    remap_tiles,
    src_block,
    owner,
    offset,
    tile_index,
    ocean_state,
    mixing,
    land_mask,
):
    faces, tile_count = lax.axis_size("face"), lax.axis_size("tile")
    nxt, sib = row_messages(atmos_state, courant)
    inner = [(i, i + 1) for i in range(1, tile_count - 1, 2)]
    nxt = lax.ppermute(nxt, "tile", inner + [(b, a) for a, b in inner])
    sib = lax.ppermute(sib, "tile", [(i, i ^ 1) for i in range(tile_count)])
    own_strip, own_coef, own_message, own_sums, level_sum, scale, numbers, *rest = own_parts(
        *(level_weights, src_block, owner.reshape(1, -1), offset, tile_index),
        *(atmos_state, courant, remap_tiles),
    )
    routes, offsets, early = rest
    halo_strip, halo_coef, halo_sums, send_w, send_e = column_messages(
        scale, nxt, sib, own_message
    )
    from_e = lax.ppermute(send_w, "face", [((i + 1) % faces, i) for i in range(faces)])
    from_w = lax.ppermute(send_e, "face", [(i, (i + 1) % faces) for i in range(faces)])
    flux, nxt, sib, late = flux_stencil(scale, level_sum, numbers, nxt, sib, remap_tiles)
    edges = (own_sums, halo_sums, own_coef, halo_coef, from_w, from_e)
    message, *edges = send_blocks(
        routes, flux, halo_strip, edges, offsets, early, late
    )
    halo_strip, from_w, from_e, strip_coef = edges
    message = exchange(message, CHUNK)
    ocean_flux, back = ocean_surface(message, ocean_state, mixing, land_mask)
    back = exchange(back, BACK)
    ocean_inputs = (ocean_flux, ocean_state, mixing, land_mask)
    edges = (own_strip, halo_strip, strip_coef, from_w, from_e)
    air_state, ocean_out = air_steps(atmos_state, *ocean_inputs, courant, sib, nxt, *edges)
    atmos_surface = return_blocks(routes, back, remap_tiles)
    return air_state, ocean_out, atmos_surface


def solution(mesh):
    return jax.shard_map(
        shards,
        mesh=mesh,
        in_specs=(
            P(None, None, "tile", "face"),
            P(None, "tile", "face"),
            P(),
            P(("face", "tile"), None, None),
            P(("face", "tile"), None),
            P(("face", "tile"), None, None),
            P(("face", "tile"), None),
            P(("face", "tile"), None),
            P(None, None, "face", "tile"),
            P("face", "tile"),
            P("face", "tile"),
        ),
        out_specs=(
            P(None, None, "tile", "face"),
            P(None, None, "face", "tile"),
            P(None, "tile", "face"),
        ),
        check_vma=False,
    )
```
